256 devices in a mesh: pipe: 16 (over z, x_lo), tensor: 4 (over x_hi, core), dp: 4 (over y).
Axes of the slice: x: 4 (x_hi: 2, x_lo: 2; x = x_hi * 2 + x_lo), y: 4, z: 8, core: 2. Of those that a mesh axis runs over, the one named last changes fastest.
Arguments:
- fwd_qkv: bfloat16 [3, 64, 256, 8192], P(None, ('pipe', 'dp'), None, 'tensor'), may hold values from -8 to 8, as said below
- fwd_segments: int32 [64, 256], P(('pipe', 'dp')), may hold values from 0 to 15, as said below
- parked: bfloat16 [3, 64, 256, 8192], P(None, ('pipe', 'dp'), 'tensor'), may hold values from -8 to 8, as said below
- bwd_segments: int32 [64, 256], P(('pipe', 'dp')), may hold values from 0 to 15, as said below
- grad_out: bfloat16 [64, 256, 8192], P(('pipe', 'dp'), None, 'tensor'), may hold values from -6 to 6
- loss_tokens: int32 [64], P(('pipe', 'dp')), may hold values from 1 to 256
Outputs:
- received: bfloat16 [64, 256, 8192], P(('pipe', 'dp'), None, 'tensor')
- grads: bfloat16 [3, 64, 256, 8192], P(None, ('pipe', 'dp'), None, 'tensor')
The draws below stay inside these ranges and needn't reach their ends.
Inputs may be any that keep to these rules, and one draw needn't show every extreme that they name: `fwd_qkv`: Real-valued. `parked`: Real-valued. `fwd_segments`: in each slot the numbers start at 0, never fall, and change only at positions that are multiples of 16. `bwd_segments`: in each slot the numbers start at 0, never fall, and change only at positions that are multiples of 16.
All inputs are finite; a program needn't handle non-finite values.
Results may differ from the reference program's by a relative error of at most 0.0051.
Values may be sent and summed in bfloat16 or wider, within the bound.
No kernel may reach another device: no remote copies, remote signals or barrier semaphores. Data moves between devices by JAX's collectives and lax.ppermute only.
A program may use at most 128 MiB of HBM per device.

```python
import jax
import jax.numpy as jnp
from jax import lax

HEAD_DIM = 128
SEQ = 256
FEAT = 8192
MICRO = 64
N_PIPE = 16
N_DP = 4


def stacked_draw(key):
    key_main = jax.random.fold_in(key, 0)
    values = jnp.clip(jax.random.normal(key_main, (3, MICRO, SEQ, FEAT), jnp.float32), -4.0, 4.0)
    return values.astype(jnp.bfloat16)


def segment_draw(key):
    key_rate, key_cut = jax.random.split(key, 2)
    cell_count = SEQ // 16
    rate = jax.random.randint(key_rate, (MICRO, 1), 1, 8)
    rate = jnp.where(jnp.arange(MICRO)[:, None] == 0, 8, rate)
    cuts = jax.random.randint(key_cut, (MICRO, cell_count), 0, 8) < rate
    cuts = jnp.where(jnp.arange(cell_count)[None, :] == 0, False, cuts)
    numbers = jnp.cumsum(cuts.astype(jnp.int32), axis=1)
    return jnp.repeat(numbers, 16, axis=1).astype(jnp.int32)


def draw_fwd_qkv(key, part):
    key = jax.random.fold_in(key, 11)
    return stacked_draw(key)


def draw_parked(key, part):
    key = jax.random.fold_in(key, 13)
    return stacked_draw(key)


def draw_fwd_segments(key, part):
    key = jax.random.fold_in(key, 17)
    return segment_draw(key)


def draw_bwd_segments(key, part):
    key = jax.random.fold_in(key, 19)
    return segment_draw(key)


def draw_loss_tokens(key, part):
    key = jax.random.fold_in(key, 23)
    replica = jnp.arange(MICRO) % N_DP
    spread = jax.random.randint(key, (MICRO,), 0, SEQ // (2 * N_DP))
    counts = jnp.where(replica == N_DP - 1, SEQ, (replica + 1) * (SEQ // N_DP) - spread)
    return counts.astype(jnp.int32)


def block_levels(rng, shape, shards, smallest, largest):
    level = 1.0
    for dim, parts in shards:
        steps = jax.random.uniform(jax.random.fold_in(jax.random.fold_in(rng, 6), dim), (parts,), jnp.float32, smallest / len(shards), largest / len(shards))
        level = level * jnp.repeat(jnp.exp(steps), shape[dim] // parts).reshape((-1,) + (1,) * (len(shape) - 1 - dim))
    return level


def scatter_about(own_key, shape, scale, limit, shards=(), kind=jnp.bfloat16):
    entries = jax.random.normal(own_key, shape, jnp.float32) * scale
    if len(shards) > 0:
        entries = block_levels(own_key, shape, shards, -0.22, 0.18) * entries
    return jnp.clip(entries, min=-limit, max=limit).astype(kind)


def setup_inputs(seed: int = 0) -> dict:
    seeds = jax.random.split(jax.random.key(seed), 7)
    return {
        "fwd_qkv": draw_fwd_qkv(jax.random.fold_in(seeds[6], 71), 0),
        "fwd_segments": draw_fwd_segments(jax.random.fold_in(seeds[6], 71), 0),
        "parked": draw_parked(jax.random.fold_in(seeds[6], 71), 0),
        "bwd_segments": draw_bwd_segments(jax.random.fold_in(seeds[6], 71), 0),
        "grad_out": scatter_about(seeds[4], (MICRO, SEQ, FEAT), 1.0, 6.0, ((0, 64), (2, 4))),
        "loss_tokens": draw_loss_tokens(jax.random.fold_in(seeds[6], 71), 0),
    }


def probabilities(queries, key_rows, segment):
    length = queries.shape[0]
    head_count = queries.shape[1] // HEAD_DIM
    query_heads = queries.reshape(length, head_count, HEAD_DIM).astype(jnp.float32)
    key_heads = key_rows.reshape(length, head_count, HEAD_DIM).astype(jnp.float32)
    logits = jnp.einsum("qhd,khd->hqk", query_heads, key_heads) * (HEAD_DIM ** -0.5)
    inside = segment[:, None] == segment[None, :]
    logits = jnp.where(inside[None], logits, jnp.float32(-1e30))
    highest = jnp.max(logits, axis=-1, keepdims=True)
    weights = jnp.exp(logits - highest)
    return weights / jnp.sum(weights, axis=-1, keepdims=True)


def rounded(values):
    return lax.optimization_barrier(values.astype(jnp.bfloat16)).astype(jnp.float32)


def attend(queries, key_rows, value_rows, segment):
    length = queries.shape[0]
    head_count = queries.shape[1] // HEAD_DIM
    probs_low = rounded(probabilities(queries, key_rows, segment))
    value_heads = value_rows.reshape(length, head_count, HEAD_DIM).astype(jnp.float32)
    mixed = jnp.einsum("hqk,khd->qhd", probs_low, value_heads)
    return mixed.reshape(length, head_count * HEAD_DIM).astype(jnp.bfloat16)


def attend_backward(queries, key_rows, value_rows, segment, upstream, factor):
    length = queries.shape[0]
    head_count = queries.shape[1] // HEAD_DIM
    probs = probabilities(queries, key_rows, segment)
    probs_low = rounded(probs)
    query_heads = queries.reshape(length, head_count, HEAD_DIM).astype(jnp.float32)
    key_heads = key_rows.reshape(length, head_count, HEAD_DIM).astype(jnp.float32)
    value_heads = value_rows.reshape(length, head_count, HEAD_DIM).astype(jnp.float32)
    upstream_heads = upstream.reshape(length, head_count, HEAD_DIM).astype(jnp.float32)
    grad_value = jnp.einsum("hqk,qhd->khd", probs_low, upstream_heads)
    grad_probs = jnp.einsum("qhd,khd->hqk", upstream_heads, value_heads)
    center = jnp.sum(probs * grad_probs, axis=-1, keepdims=True)
    grad_logits = rounded(probs * (grad_probs - center) * (HEAD_DIM ** -0.5))
    grad_query = jnp.einsum("hqk,khd->qhd", grad_logits, key_heads)
    grad_key = jnp.einsum("hqk,qhd->khd", grad_logits, query_heads)
    stacked = jnp.stack([grad_query, grad_key, grad_value]) * factor
    return stacked.reshape(3, length, head_count * HEAD_DIM).astype(jnp.bfloat16)


def reference(fwd_qkv, fwd_segments, parked, bwd_segments, grad_out, loss_tokens):
    forward_out = lax.map(lambda item: attend(item[0], item[1], item[2], item[3]),
                          (fwd_qkv[0], fwd_qkv[1], fwd_qkv[2], fwd_segments))
    received = jnp.roll(forward_out.reshape(N_PIPE, N_DP, SEQ, FEAT), 1, axis=0).reshape(MICRO, SEQ, FEAT)
    stash = jnp.flip(parked.reshape(3, N_PIPE, N_DP, SEQ, FEAT), axis=1).reshape(3, MICRO, SEQ, FEAT)
    upstream = jnp.roll(grad_out.reshape(N_PIPE, N_DP, SEQ, FEAT), -1, axis=0).reshape(MICRO, SEQ, FEAT)
    token_total = jnp.sum(loss_tokens.reshape(N_PIPE, N_DP).astype(jnp.float32), axis=1)
    factor = jnp.repeat(jnp.float32(N_DP * SEQ) / token_total, N_DP)
    grads = lax.map(lambda item: attend_backward(item[0], item[1], item[2], item[3], item[4], item[5]),
                    (stash[0], stash[1], stash[2], bwd_segments, upstream, factor))
    return received, jnp.transpose(grads, (1, 0, 2, 3))
```

```python
import functools
import math

import jax
import jax.numpy as jnp
from jax import lax
from jax.experimental import pallas as pl
from jax.experimental.pallas import tpu as pltpu
from jax.sharding import PartitionSpec as P

HEAD_DIM = 128
CHUNKS = 4
SCALE = HEAD_DIM ** (-0.5)
EXPONENT = SCALE * math.log2(math.e)
NT = (((1,), (1,)), ((), ()))
NN = (((1,), (0,)), ((), ()))
TN = (((0,), (0,)), ((), ()))


def product(left, right, dims):
    return lax.dot_general(left, right, dims, preferred_element_type=jnp.float32)


def probabilities(queries, keys, outside):
    logits = product(queries, keys, NT) + outside
    highest = jnp.max(logits, axis=1, keepdims=True)
    weights = jnp.exp2((logits - highest) * EXPONENT)
    return weights / jnp.sum(weights, axis=1, keepdims=True)


def outside_of(row_ref, column_ref):
    return jnp.where(column_ref[...] == row_ref[...], 0.0, -1e31).astype(jnp.float32)


def forward_kernel(qkv_ref, row_ref, column_ref, out_ref):
    outside = outside_of(row_ref, column_ref)
    for start in range(0, out_ref.shape[2], HEAD_DIM):
        head = slice(start, start + HEAD_DIM)
        probs = probabilities(qkv_ref[0, 0, :, head], qkv_ref[1, 0, :, head], outside)
        mixed = product(probs.astype(jnp.bfloat16), qkv_ref[2, 0, :, head], NN)
        out_ref[0, :, head] = mixed.astype(jnp.bfloat16)


def forward(qkv, row, column):
    _, _, length, width = qkv.shape
    step = width // CHUNKS
    return pl.pallas_call(
        forward_kernel,
        grid=(CHUNKS,),
        in_specs=[
            pl.BlockSpec((3, 1, length, step), lambda c: (0, 0, 0, c)),
            pl.BlockSpec((1, length), lambda c: (0, 0)),
            pl.BlockSpec((length, 1), lambda c: (0, 0)),
        ],
        out_specs=pl.BlockSpec((1, length, step), lambda c: (0, 0, c)),
        out_shape=jax.ShapeDtypeStruct((1, length, width), jnp.bfloat16),
        compiler_params=pltpu.CompilerParams(vmem_limit_bytes=32 * 1024 * 1024),
        cost_estimate=pl.CostEstimate(
            flops=4 * length * length * width,
            bytes_accessed=8 * length * width,
            transcendentals=length * length * width // HEAD_DIM,
        ),
    )(qkv, row, column)


def backward_kernel(parts, *refs):
    pieces, refs = refs[:parts], refs[parts:]
    upstream_ref, row_ref, column_ref, factor_ref = refs[:4]
    out_ref, stash = refs[-2:]
    mine = lax.axis_index("tensor")
    rows = pieces[0].shape[2]
    for k in range(parts):
        start = pl.multiple_of((mine ^ k) * rows, rows)
        stash[:, pl.ds(start, rows), :] = pieces[k][:, 0]
    outside = outside_of(row_ref, column_ref)
    factor = factor_ref[0]
    for start in range(0, upstream_ref.shape[2], HEAD_DIM):
        head = slice(start, start + HEAD_DIM)
        queries, keys, values = stash[0, :, head], stash[1, :, head], stash[2, :, head]
        upstream = upstream_ref[0, :, head]
        probs = probabilities(queries, keys, outside)
        grad_value = product(probs.astype(jnp.bfloat16), upstream, TN)
        grad_probs = product(upstream, values, NT)
        center = jnp.sum(probs * grad_probs, axis=1, keepdims=True)
        grad_logits = (probs * (grad_probs - center) * SCALE).astype(jnp.bfloat16)
        out_ref[0, 0, :, head] = (product(grad_logits, keys, NN) * factor).astype(jnp.bfloat16)
        out_ref[1, 0, :, head] = (product(grad_logits, queries, TN) * factor).astype(jnp.bfloat16)
        out_ref[2, 0, :, head] = (grad_value * factor).astype(jnp.bfloat16)


def backward(chunk, pieces, upstream, row, column, factor, earlier):
    _, length, width = upstream.shape
    step = width // CHUNKS
    parts = len(pieces)
    whole = pl.BlockSpec(memory_space=pltpu.VMEM)
    operands = [*pieces, upstream, row, column, factor]
    in_specs = [whole] * parts + [
        pl.BlockSpec((1, length, step), lambda i: (0, 0, chunk)),
        pl.BlockSpec((1, length), lambda i: (0, 0)),
        pl.BlockSpec((length, 1), lambda i: (0, 0)),
        pl.BlockSpec(memory_space=pltpu.SMEM),
    ]
    aliases = {}
    if earlier is not None:
        aliases = {len(operands): 0}
        operands.append(earlier)
        in_specs.append(pl.BlockSpec(memory_space=pl.ANY))
    return pl.pallas_call(
        functools.partial(backward_kernel, parts),
        grid=(1,),
        in_specs=in_specs,
        out_specs=pl.BlockSpec((3, 1, length, step), lambda i: (0, 0, 0, chunk)),
        out_shape=jax.ShapeDtypeStruct((3, 1, length, width), jnp.bfloat16),
        scratch_shapes=[pltpu.VMEM((3, length, step), jnp.bfloat16)],
        input_output_aliases=aliases,
        compiler_params=pltpu.CompilerParams(vmem_limit_bytes=32 * 1024 * 1024),
        cost_estimate=pl.CostEstimate(
            flops=10 * length * length * step,
            bytes_accessed=14 * length * step,
            transcendentals=length * length * step // HEAD_DIM,
        ),
    )(*operands)


def shifted(array, by):
    sections = lax.axis_size("pipe")
    return lax.ppermute(array, "pipe", [(i, (i + by) % sections) for i in range(sections)])


def fetched(piece, k):
    sections, tensors = lax.axis_size("pipe"), lax.axis_size("tensor")
    pairs = [
        (p * tensors + t, (sections - 1 - p) * tensors + (t ^ k))
        for p in range(sections)
        for t in range(tensors)
    ]
    return lax.ppermute(piece, ("pipe", "tensor"), pairs)


def on_device(fwd_qkv, fwd_segments, parked, bwd_segments, grad_out, loss_tokens):
    length, width = grad_out.shape[1:]
    tensors = lax.axis_size("tensor")
    mine = lax.axis_index("tensor")
    step = width // CHUNKS
    pieces = []
    for chunk in range(CHUNKS):
        pieces.append([])
        for k in range(tensors):
            start = (mine ^ k) * width + chunk * step
            piece = lax.dynamic_slice_in_dim(parked, start, step, axis=3)
            pieces[-1].append(fetched(piece, k))
    upstream = shifted(grad_out, -1)
    token_total = lax.psum(loss_tokens.astype(jnp.float32), "dp")
    factor = jnp.float32(lax.axis_size("dp") * length) / token_total
    forward_out = forward(fwd_qkv, fwd_segments, fwd_segments.reshape(length, 1))
    received = shifted(forward_out, 1)
    column = bwd_segments.reshape(length, 1)
    grads = None
    for chunk in range(CHUNKS):
        grads = backward(chunk, pieces[chunk], upstream, bwd_segments, column, factor, grads)
    return (received, grads)


def solution(mesh):
    placed = (
        P(None, ("pipe", "dp"), None, "tensor"),
        P(("pipe", "dp"), None),
        P(None, ("pipe", "dp"), "tensor", None),
        P(("pipe", "dp"), None),
        P(("pipe", "dp"), None, "tensor"),
        P(("pipe", "dp")),
    )
    return jax.shard_map(
        on_device,
        mesh=mesh,
        in_specs=placed,
        out_specs=(P(("pipe", "dp"), None, "tensor"), P(None, ("pipe", "dp"), None, "tensor")),
        check_vma=False,
    )
```

```python
import functools
import math

import jax
import jax.numpy as jnp
from jax import lax
from jax.experimental import pallas as pl
from jax.experimental.pallas import tpu as pltpu
from jax.sharding import PartitionSpec as P

HEAD_DIM = 128
CHUNKS = 4
SCALE = HEAD_DIM ** (-0.5)
EXPONENT = SCALE * math.log2(math.e)
NT = (((1,), (1,)), ((), ()))
NN = (((1,), (0,)), ((), ()))
TN = (((0,), (0,)), ((), ()))


def product(left, right, dims):
    return lax.dot_general(left, right, dims, preferred_element_type=jnp.float32)


def probabilities(queries, keys, outside):
    logits = product(queries, keys, NT) + outside
    highest = jnp.max(logits, axis=1, keepdims=True)
    weights = jnp.exp2((logits - highest) * EXPONENT)
    return weights / jnp.sum(weights, axis=1, keepdims=True)


def outside_of(row_ref, column_ref):
    return jnp.where(column_ref[...] == row_ref[...], 0.0, -1e31).astype(jnp.float32)


def forward_kernel(qkv_ref, row_ref, column_ref, out_ref):
    outside = outside_of(row_ref, column_ref)
    for start in range(0, out_ref.shape[2], HEAD_DIM):
        head = slice(start, start + HEAD_DIM)
        probs = probabilities(qkv_ref[0, 0, :, head], qkv_ref[1, 0, :, head], outside)
        mixed = product(probs.astype(jnp.bfloat16), qkv_ref[2, 0, :, head], NN)
        out_ref[0, :, head] = mixed.astype(jnp.bfloat16)


def forward(qkv, row, column):
    _, _, length, width = qkv.shape
    step = width // CHUNKS
    return pl.pallas_call(
        forward_kernel,
        grid=(CHUNKS,),
        in_specs=[
            pl.BlockSpec((3, 1, length, step), lambda c: (0, 0, 0, c)),
            pl.BlockSpec((1, length), lambda c: (0, 0)),
            pl.BlockSpec((length, 1), lambda c: (0, 0)),
        ],
        out_specs=pl.BlockSpec((1, length, step), lambda c: (0, 0, c)),
        out_shape=jax.ShapeDtypeStruct((1, length, width), jnp.bfloat16),
        compiler_params=pltpu.CompilerParams(vmem_limit_bytes=32 * 1024 * 1024),
        cost_estimate=pl.CostEstimate(
            flops=4 * length * length * width,
            bytes_accessed=8 * length * width,
            transcendentals=length * length * width // HEAD_DIM,
        ),
    )(qkv, row, column)


def backward_kernel(parts, *refs):
    pieces, refs = refs[:parts], refs[parts:]
    upstream_ref, row_ref, column_ref, factor_ref = refs[:4]
    out_ref, stash = refs[-2:]
    mine = lax.axis_index("tensor")
    rows = pieces[0].shape[2]
    for k in range(parts):
        start = pl.multiple_of((mine ^ k) * rows, rows)
        stash[:, pl.ds(start, rows), :] = pieces[k][:, 0]
    outside = outside_of(row_ref, column_ref)
    factor = factor_ref[0]
    for start in range(0, upstream_ref.shape[2], HEAD_DIM):
        head = slice(start, start + HEAD_DIM)
        queries, keys, values = stash[0, :, head], stash[1, :, head], stash[2, :, head]
        upstream = upstream_ref[0, :, head]
        probs = probabilities(queries, keys, outside)
        grad_value = product(probs.astype(jnp.bfloat16), upstream, TN)
        grad_probs = product(upstream, values, NT)
        center = jnp.sum(probs * grad_probs, axis=1, keepdims=True)
        grad_logits = (probs * (grad_probs - center) * SCALE).astype(jnp.bfloat16)
        out_ref[0, 0, :, head] = (product(grad_logits, keys, NN) * factor).astype(jnp.bfloat16)
        out_ref[1, 0, :, head] = (product(grad_logits, queries, TN) * factor).astype(jnp.bfloat16)
        out_ref[2, 0, :, head] = (grad_value * factor).astype(jnp.bfloat16)


def backward(chunk, pieces, upstream, row, column, factor, earlier):
    _, length, width = upstream.shape
    step = width // CHUNKS
    parts = len(pieces)
    whole = pl.BlockSpec(memory_space=pltpu.VMEM)
    operands = [*pieces, upstream, row, column, factor]
    in_specs = [whole] * parts + [
        pl.BlockSpec((1, length, step), lambda i: (0, 0, chunk)),
        pl.BlockSpec((1, length), lambda i: (0, 0)),
        pl.BlockSpec((length, 1), lambda i: (0, 0)),
        pl.BlockSpec(memory_space=pltpu.SMEM),
    ]
    aliases = {}
    if earlier is not None:
        aliases = {len(operands): 0}
        operands.append(earlier)
        in_specs.append(pl.BlockSpec(memory_space=pl.ANY))
    return pl.pallas_call(
        functools.partial(backward_kernel, parts),
        grid=(1,),
        in_specs=in_specs,
        out_specs=pl.BlockSpec((3, 1, length, step), lambda i: (0, 0, 0, chunk)),
        out_shape=jax.ShapeDtypeStruct((3, 1, length, width), jnp.bfloat16),
        scratch_shapes=[pltpu.VMEM((3, length, step), jnp.bfloat16)],
        input_output_aliases=aliases,
        compiler_params=pltpu.CompilerParams(vmem_limit_bytes=32 * 1024 * 1024),
        cost_estimate=pl.CostEstimate(
            flops=10 * length * length * step,
            bytes_accessed=14 * length * step,
            transcendentals=length * length * step // HEAD_DIM,
        ),
    )(*operands)


def moved(array, target):
    sections, tensors = lax.axis_size("pipe"), lax.axis_size("tensor")
    pairs = []
    for p in range(sections):
        for t in range(tensors):
            section, tensor = target(p, t)
            pairs.append((p * tensors + t, section % sections * tensors + tensor))
    return lax.ppermute(array, ("pipe", "tensor"), pairs)


def fetched(piece, k):
    last = lax.axis_size("pipe") - 1
    return moved(piece, lambda p, t: (last - p, t ^ k))


def swapped(array):
    return moved(array, lambda p, t: (p ^ (t & 1), t))


def stepped(array, by):
    kept = 1 if by > 0 else 0

    def target(p, t):
        if t & 1 == 0:
            return p + by, t
        return (p if p & 1 == kept else p + 2 * by), t

    return moved(array, target)


def on_device(fwd_qkv, fwd_segments, parked, bwd_segments, grad_out, loss_tokens):
    length, width = grad_out.shape[1:]
    tensors = lax.axis_size("tensor")
    mine = lax.axis_index("tensor")
    step = width // CHUNKS
    def fetched_chunk(whole, chunk):
        starts = [(mine ^ k) * width + chunk * step for k in range(tensors)]
        cut = [lax.dynamic_slice_in_dim(whole, start, step, axis=3) for start in starts]
        fetches = []
        for k, piece in enumerate(cut):
            with jax.named_scope(f"stash_{chunk}_{k}"):
                fetches.append(fetched(piece, k))
        return fetches

    pieces = [fetched_chunk(parked, chunk) for chunk in range(3)]
    with jax.named_scope("swap_grad"):
        swapped_grad = swapped(grad_out)
    token_total = lax.psum(loss_tokens.astype(jnp.float32), "dp")
    with jax.named_scope("forward_heads"):
        forward_out = forward(fwd_qkv, fwd_segments, fwd_segments.reshape(length, 1))
    pieces[0], swapped_grad, token_total, forward_out = lax.optimization_barrier(
        (pieces[0], swapped_grad, token_total, forward_out)
    )
    with jax.named_scope("step_grad"):
        upstream = stepped(swapped_grad, -1)
    factor = jnp.float32(lax.axis_size("dp") * length) / token_total
    with jax.named_scope("swap_out"):
        swapped_out = swapped(forward_out)
    pieces[1], swapped_out = lax.optimization_barrier((pieces[1], swapped_out))
    column = bwd_segments.reshape(length, 1)
    grads = None
    for chunk in range(CHUNKS):
        with jax.named_scope(f"backward_{chunk}"):
            grads = backward(
                chunk, pieces[chunk], upstream, bwd_segments, column, factor, grads
            )
        if len(pieces) < CHUNKS:
            parked, grads = lax.optimization_barrier((parked, grads))
            pieces.append(fetched_chunk(parked, len(pieces)))
    with jax.named_scope("step_out"):
        received = stepped(swapped_out, 1)
    return (received, grads)


def solution(mesh):
    placed = (
        P(None, ("pipe", "dp"), None, "tensor"),
        P(("pipe", "dp"), None),
        P(None, ("pipe", "dp"), "tensor", None),
        P(("pipe", "dp"), None),
        P(("pipe", "dp"), None, "tensor"),
        P(("pipe", "dp")),
    )
    return jax.shard_map(
        on_device,
        mesh=mesh,
        in_specs=placed,
        out_specs=(P(("pipe", "dp"), None, "tensor"), P(None, ("pipe", "dp"), None, "tensor")),
        check_vma=False,
    )
```

```python
import functools
import math

import jax
import jax.numpy as jnp
from jax import lax
from jax.experimental import pallas as pl
from jax.experimental.pallas import tpu as pltpu
from jax.sharding import PartitionSpec as P

HEAD_DIM = 128
CHUNKS = 4
SCALE = HEAD_DIM ** (-0.5)
EXPONENT = SCALE * math.log2(math.e)
NT = (((1,), (1,)), ((), ()))
NN = (((1,), (0,)), ((), ()))
TN = (((0,), (0,)), ((), ()))


def product(left, right, dims):
    return lax.dot_general(left, right, dims, preferred_element_type=jnp.float32)


def probabilities(queries, keys, outside):
    logits = product(queries, keys, NT) + outside
    highest = jnp.max(logits, axis=1, keepdims=True)
    weights = jnp.exp2((logits - highest) * EXPONENT)
    return weights / jnp.sum(weights, axis=1, keepdims=True)


def outside_of(row_ref, column_ref):
    return jnp.where(column_ref[...] == row_ref[...], 0.0, -1e31).astype(jnp.float32)


def forward_kernel(qkv_ref, row_ref, column_ref, out_ref):
    outside = outside_of(row_ref, column_ref)
    for start in range(0, out_ref.shape[2], HEAD_DIM):
        head = slice(start, start + HEAD_DIM)
        probs = probabilities(qkv_ref[0, 0, :, head], qkv_ref[1, 0, :, head], outside)
        mixed = product(probs.astype(jnp.bfloat16), qkv_ref[2, 0, :, head], NN)
        out_ref[0, :, head] = mixed.astype(jnp.bfloat16)


def forward(qkv, row, column):
    _, _, length, width = qkv.shape
    step = width // CHUNKS
    return pl.pallas_call(
        forward_kernel,
        grid=(CHUNKS,),
        in_specs=[
            pl.BlockSpec((3, 1, length, step), lambda c: (0, 0, 0, c)),
            pl.BlockSpec((1, length), lambda c: (0, 0)),
            pl.BlockSpec((length, 1), lambda c: (0, 0)),
        ],
        out_specs=pl.BlockSpec((1, length, step), lambda c: (0, 0, c)),
        out_shape=jax.ShapeDtypeStruct((1, length, width), jnp.bfloat16),
        compiler_params=pltpu.CompilerParams(vmem_limit_bytes=32 * 1024 * 1024),
        cost_estimate=pl.CostEstimate(
            flops=4 * length * length * width,
            bytes_accessed=8 * length * width,
            transcendentals=length * length * width // HEAD_DIM,
        ),
    )(qkv, row, column)


def backward_kernel(parts, *refs):
    pieces, refs = refs[:parts], refs[parts:]
    direct_ref, around_ref, row_ref, column_ref, factor_ref = refs[:5]
    out_ref, stash = refs[-2:]
    mine = lax.axis_index("tensor")
    rows = pieces[0].shape[2]
    for k in range(parts):
        start = pl.multiple_of((mine ^ k) * rows, rows)
        stash[:, pl.ds(start, rows), :] = pieces[k][:, 0]
    outside = outside_of(row_ref, column_ref)
    factor = factor_ref[0]
    around = took_both(-1)
    for start in range(0, direct_ref.shape[2], HEAD_DIM):
        head = slice(start, start + HEAD_DIM)
        queries, keys, values = stash[0, :, head], stash[1, :, head], stash[2, :, head]
        upstream = jnp.where(around, around_ref[0, :, head], direct_ref[0, :, head])
        probs = probabilities(queries, keys, outside)
        grad_value = product(probs.astype(jnp.bfloat16), upstream, TN)
        grad_probs = product(upstream, values, NT)
        center = jnp.sum(probs * grad_probs, axis=1, keepdims=True)
        grad_logits = (probs * (grad_probs - center) * SCALE).astype(jnp.bfloat16)
        out_ref[0, 0, :, head] = (product(grad_logits, keys, NN) * factor).astype(jnp.bfloat16)
        out_ref[1, 0, :, head] = (product(grad_logits, queries, TN) * factor).astype(jnp.bfloat16)
        out_ref[2, 0, :, head] = (grad_value * factor).astype(jnp.bfloat16)


def backward(chunk, pieces, upstream, row, column, factor, earlier):
    _, length, width = upstream[0].shape
    step = width // CHUNKS
    parts = len(pieces)
    piece_specs = [
        pl.BlockSpec((3, 1, p.shape[2], step), lambda i, c=chunk if p.shape[3] > step else 0: (0, 0, 0, c))
        for p in pieces
    ]
    operands = [*pieces, *upstream, row, column, factor]
    in_specs = piece_specs + [
        pl.BlockSpec((1, length, step), lambda i: (0, 0, chunk)),
        pl.BlockSpec((1, length, step), lambda i: (0, 0, chunk)),
        pl.BlockSpec((1, length), lambda i: (0, 0)),
        pl.BlockSpec((length, 1), lambda i: (0, 0)),
        pl.BlockSpec(memory_space=pltpu.SMEM),
    ]
    aliases = {}
    if earlier is not None:
        aliases = {len(operands): 0}
        operands.append(earlier)
        in_specs.append(pl.BlockSpec(memory_space=pl.ANY))
    return pl.pallas_call(
        functools.partial(backward_kernel, parts),
        grid=(1,),
        in_specs=in_specs,
        out_specs=pl.BlockSpec((3, 1, length, step), lambda i: (0, 0, 0, chunk)),
        out_shape=jax.ShapeDtypeStruct((3, 1, length, width), jnp.bfloat16),
        scratch_shapes=[pltpu.VMEM((3, length, step), jnp.bfloat16)],
        input_output_aliases=aliases,
        compiler_params=pltpu.CompilerParams(vmem_limit_bytes=32 * 1024 * 1024),
        cost_estimate=pl.CostEstimate(
            flops=10 * length * length * step,
            bytes_accessed=14 * length * step,
            transcendentals=length * length * step // HEAD_DIM,
        ),
    )(*operands)


def moved(array, target):
    sections, tensors = lax.axis_size("pipe"), lax.axis_size("tensor")
    pairs = []
    for p in range(sections):
        for t in range(tensors):
            section, tensor = target(p, t)
            pairs.append((p * tensors + t, section % sections * tensors + tensor))
    return lax.ppermute(array, ("pipe", "tensor"), pairs)


def fetched(piece, k):
    last = lax.axis_size("pipe") - 1
    return moved(piece, lambda p, t: (last - p, t ^ k))


def first_hop(array, by):
    return moved(array, lambda p, t: (p ^ 1 if t & 1 else p + by, t))


def second_hop(array, by):
    sections, tensors = lax.axis_size("pipe"), lax.axis_size("tensor")
    pairs = []
    for p in range(0 if by > 0 else 1, sections, 2):
        for t in range(1, tensors, 2):
            pairs.append((p * tensors + t, (p + 2 * by) % sections * tensors + t))
    return lax.ppermute(array, ("pipe", "tensor"), pairs)


def took_both(by):
    kept = 0 if by > 0 else 1
    return jnp.logical_and(lax.axis_index("pipe") & 1 == kept, lax.axis_index("tensor") & 1 == 1)


def odd_pairs(kind):
    sections, tensors = lax.axis_size("pipe"), lax.axis_size("tensor")
    pairs = []
    for p in range(sections):
        for t in range(tensors):
            if t & 1 and kind == "swap":
                pairs.append((p * tensors + t, (p ^ 1) * tensors + t))
            if kind == "step" and (t & 1 == 0 or p & 1 == 0):
                pairs.append((p * tensors + t, (p + 1 + (t & 1)) % sections * tensors + t))
    return pairs


def on_device(fwd_qkv, fwd_segments, parked, bwd_segments, grad_out, loss_tokens):
    length, width = grad_out.shape[1:]
    tensors = lax.axis_size("tensor")
    mine = lax.axis_index("tensor")
    step = width // CHUNKS

    def fetched_part(whole, k, first, count):
        start = (mine ^ k) * width + first * step
        piece = lax.dynamic_slice_in_dim(whole, start, count * step, axis=3)
        with jax.named_scope(f"stash_{k}_{first}"):
            return fetched(piece, k)

    with jax.named_scope("step_grad_1"):
        upstream_direct = first_hop(grad_out, -1)
    early = [fetched_part(parked, k, 0, CHUNKS) for k in range(2)]
    with jax.named_scope("step_grad_2"):
        upstream_around = second_hop(upstream_direct, -1)
    early[0], fwd_qkv, loss_tokens, parked = lax.optimization_barrier(
        (early[0], fwd_qkv, loss_tokens, parked)
    )
    token_total = lax.psum(loss_tokens.astype(jnp.float32), "dp")
    with jax.named_scope("forward_heads"):
        forward_out = forward(fwd_qkv, fwd_segments, fwd_segments.reshape(length, 1))
    token_total, forward_out = lax.optimization_barrier((token_total, forward_out))
    factor = jnp.float32(lax.axis_size("dp") * length) / token_total
    with jax.named_scope("swap_out"):
        swapped_out = lax.ppermute(forward_out, ("pipe", "tensor"), odd_pairs("swap"))
    early[1], upstream_around, parked = lax.optimization_barrier(
        (early[1], upstream_around, parked)
    )
    late = [[fetched_part(parked, k, c, 1) for k in range(2, tensors)] for c in range(4)]
    upstream = (upstream_direct, upstream_around)
    odd = lax.axis_index("tensor") & 1 == 1
    stepping = jnp.where(odd, swapped_out, forward_out)
    late[:3], stepping = lax.optimization_barrier((late[:3], stepping))
    column = bwd_segments.reshape(length, 1)
    grads = None
    for chunk in range(CHUNKS):
        with jax.named_scope(f"backward_{chunk}"):
            grads = backward(
                chunk, early + late[chunk], upstream, bwd_segments, column, factor, grads
            )
    with jax.named_scope("step_out"):
        stepped_out = lax.ppermute(stepping, ("pipe", "tensor"), odd_pairs("step"))
    last = lax.axis_index("pipe") & 1 == 1
    received = jnp.where(jnp.logical_and(odd, last), swapped_out, stepped_out)
    return (received, grads)


def solution(mesh):
    placed = (
        P(None, ("pipe", "dp"), None, "tensor"),
        P(("pipe", "dp"), None),
        P(None, ("pipe", "dp"), "tensor", None),
        P(("pipe", "dp"), None),
        P(("pipe", "dp"), None, "tensor"),
        P(("pipe", "dp")),
    )
    return jax.shard_map(
        on_device,
        mesh=mesh,
        in_specs=placed,
        out_specs=(P(("pipe", "dp"), None, "tensor"), P(None, ("pipe", "dp"), None, "tensor")),
        check_vma=False,
    )
```

```python
import functools
import math

import jax
import jax.numpy as jnp
from jax import lax
from jax.experimental import pallas as pl
from jax.experimental.pallas import tpu as pltpu
from jax.sharding import PartitionSpec as P

HEAD_DIM = 128
CHUNKS = 4
SCALE = HEAD_DIM ** (-0.5)
EXPONENT = SCALE * math.log2(math.e)
NT = (((1,), (1,)), ((), ()))
NN = (((1,), (0,)), ((), ()))
TN = (((0,), (0,)), ((), ()))


def product(left, right, dims):
    return lax.dot_general(left, right, dims, preferred_element_type=jnp.float32)


def probabilities(queries, keys, outside):
    logits = product(queries, keys, NT) + outside
    highest = jnp.max(logits, axis=1, keepdims=True)
    weights = jnp.exp2((logits - highest) * EXPONENT)
    return weights / jnp.sum(weights, axis=1, keepdims=True)


def outside_of(row_ref, column_ref):
    return jnp.where(column_ref[...] == row_ref[...], 0.0, -1e31).astype(jnp.float32)


def forward_kernel(qkv_ref, row_ref, column_ref, out_ref):
    outside = outside_of(row_ref, column_ref)
    for start in range(0, out_ref.shape[2], HEAD_DIM):
        head = slice(start, start + HEAD_DIM)
        probs = probabilities(qkv_ref[0, 0, :, head], qkv_ref[1, 0, :, head], outside)
        mixed = product(probs.astype(jnp.bfloat16), qkv_ref[2, 0, :, head], NN)
        out_ref[0, :, head] = mixed.astype(jnp.bfloat16)


def forward(qkv, row, column):
    _, _, length, width = qkv.shape
    step = width // CHUNKS
    return pl.pallas_call(
        forward_kernel,
        grid=(CHUNKS,),
        in_specs=[
            pl.BlockSpec((3, 1, length, step), lambda c: (0, 0, 0, c)),
            pl.BlockSpec((1, length), lambda c: (0, 0)),
            pl.BlockSpec((length, 1), lambda c: (0, 0)),
        ],
        out_specs=pl.BlockSpec((1, length, step), lambda c: (0, 0, c)),
        out_shape=jax.ShapeDtypeStruct((1, length, width), jnp.bfloat16),
        compiler_params=pltpu.CompilerParams(vmem_limit_bytes=32 * 1024 * 1024),
        cost_estimate=pl.CostEstimate(
            flops=4 * length * length * width,
            bytes_accessed=8 * length * width,
            transcendentals=length * length * width // HEAD_DIM,
        ),
    )(qkv, row, column)


def backward_kernel(parts, *refs):
    pieces, refs = refs[:parts], refs[parts:]
    direct_ref, around_ref, row_ref, column_ref, factor_ref = refs[:5]
    out_ref, stash = refs[-2:]
    mine = lax.axis_index("tensor")
    rows = pieces[0].shape[2]
    for k in range(parts):
        start = pl.multiple_of((mine ^ k) * rows, rows)
        stash[:, pl.ds(start, rows), :] = pieces[k][:, 0]
    outside = outside_of(row_ref, column_ref)
    factor = factor_ref[0]
    around = came_around(-1)
    for start in range(0, direct_ref.shape[2], HEAD_DIM):
        head = slice(start, start + HEAD_DIM)
        queries, keys, values = stash[0, :, head], stash[1, :, head], stash[2, :, head]
        upstream = jnp.where(around, around_ref[0, :, head], direct_ref[0, :, head])
        probs = probabilities(queries, keys, outside)
        grad_value = product(probs.astype(jnp.bfloat16), upstream, TN)
        grad_probs = product(upstream, values, NT)
        center = jnp.sum(probs * grad_probs, axis=1, keepdims=True)
        grad_logits = (probs * (grad_probs - center) * SCALE).astype(jnp.bfloat16)
        out_ref[0, 0, :, head] = (product(grad_logits, keys, NN) * factor).astype(jnp.bfloat16)
        out_ref[1, 0, :, head] = (product(grad_logits, queries, TN) * factor).astype(jnp.bfloat16)
        out_ref[2, 0, :, head] = (grad_value * factor).astype(jnp.bfloat16)


def backward(chunk, pieces, upstream, row, column, factor, earlier):
    _, length, width = upstream[0].shape
    step = width // CHUNKS
    parts = len(pieces)
    piece_specs = [
        pl.BlockSpec((3, 1, p.shape[2], step), lambda i, c=chunk % (p.shape[3] // step): (0, 0, 0, c))
        for p in pieces
    ]
    operands = [*pieces, *upstream, row, column, factor]
    in_specs = piece_specs + [
        pl.BlockSpec((1, length, step), lambda i: (0, 0, chunk)),
        pl.BlockSpec((1, length, step), lambda i: (0, 0, chunk)),
        pl.BlockSpec((1, length), lambda i: (0, 0)),
        pl.BlockSpec((length, 1), lambda i: (0, 0)),
        pl.BlockSpec(memory_space=pltpu.SMEM),
    ]
    aliases = {}
    if earlier is not None:
        aliases = {len(operands): 0}
        operands.append(earlier)
        in_specs.append(pl.BlockSpec(memory_space=pl.ANY))
    return pl.pallas_call(
        functools.partial(backward_kernel, parts),
        grid=(1,),
        in_specs=in_specs,
        out_specs=pl.BlockSpec((3, 1, length, step), lambda i: (0, 0, 0, chunk)),
        out_shape=jax.ShapeDtypeStruct((3, 1, length, width), jnp.bfloat16),
        scratch_shapes=[pltpu.VMEM((3, length, step), jnp.bfloat16)],
        input_output_aliases=aliases,
        compiler_params=pltpu.CompilerParams(vmem_limit_bytes=32 * 1024 * 1024),
        cost_estimate=pl.CostEstimate(
            flops=10 * length * length * step,
            bytes_accessed=14 * length * step,
            transcendentals=length * length * step // HEAD_DIM,
        ),
    )(*operands)


def moved(array, target):
    sections, tensors = lax.axis_size("pipe"), lax.axis_size("tensor")
    pairs = []
    for p in range(sections):
        for t in range(tensors):
            section, tensor = target(p, t)
            pairs.append((p * tensors + t, section % sections * tensors + tensor))
    return lax.ppermute(array, ("pipe", "tensor"), pairs)


def fetched(piece, k):
    last = lax.axis_size("pipe") - 1
    return moved(piece, lambda p, t: (last - p, t ^ k))


def detoured(p, t, by):
    half = lax.axis_size("pipe") // 2
    return (t & 1) * (p % half == (half - 1 if by > 0 else 0))


def shift_pairs(by, leg):
    sections, tensors = lax.axis_size("pipe"), lax.axis_size("tensor")
    pairs = []
    for p in range(sections):
        for t in range(tensors):
            aside = detoured(p, t, by)
            start, end = p, p + by
            if leg == "aside":
                end = p - by
            if leg == "onward":
                start = p - by
            if aside == (leg != "direct"):
                pairs.append((start % sections * tensors + t, end % sections * tensors + t))
    return pairs


def shifted(array, by, leg):
    with jax.named_scope(f"{leg}_{'out' if by > 0 else 'grad'}"):
        return lax.ppermute(array, ("pipe", "tensor"), shift_pairs(by, leg))


def came_around(by):
    sections = lax.axis_size("pipe")
    source = (lax.axis_index("pipe") + sections - by) % sections
    return detoured(source, lax.axis_index("tensor"), by) == 1


def on_device(fwd_qkv, fwd_segments, parked, bwd_segments, grad_out, loss_tokens):
    length, width = grad_out.shape[1:]
    tensors = lax.axis_size("tensor")
    mine = lax.axis_index("tensor")
    step = width // CHUNKS

    def fetched_part(whole, k, first, count):
        start = (mine ^ k) * width + first * step
        piece = lax.dynamic_slice_in_dim(whole, start, count * step, axis=3)
        with jax.named_scope(f"stash_{k}_{first}"):
            return fetched(piece, k)

    upstream_direct = shifted(grad_out, -1, "direct")
    upstream_aside = shifted(grad_out, -1, "aside")
    early = [fetched_part(parked, k, 0, CHUNKS) for k in range(3)]
    upstream_around = shifted(upstream_aside, -1, "onward")
    early[0], parked, loss_tokens = lax.optimization_barrier((early[0], parked, loss_tokens))
    token_total = lax.psum(loss_tokens.astype(jnp.float32), "dp")
    late = [fetched_part(parked, 3, 0, 2)]
    early[1], parked, token_total = lax.optimization_barrier((early[1], parked, token_total))
    factor = jnp.float32(lax.axis_size("dp") * length) / token_total
    early, upstream_direct, upstream_around, fwd_qkv, token_total = lax.optimization_barrier(
        (early, upstream_direct, upstream_around, fwd_qkv, token_total)
    )
    upstream = (upstream_direct, upstream_around)
    with jax.named_scope("forward_heads"):
        forward_out = forward(fwd_qkv, fwd_segments, fwd_segments.reshape(length, 1))
    late[0], forward_out = lax.optimization_barrier((late[0], forward_out))
    late += [late[0], fetched_part(parked, 3, 2, 1), fetched_part(parked, 3, 3, 1)]
    received = shifted(forward_out, 1, "direct")
    received_aside = shifted(forward_out, 1, "aside")
    received_around = shifted(received_aside, 1, "onward")
    column = bwd_segments.reshape(length, 1)
    grads = None
    for chunk in range(CHUNKS):
        with jax.named_scope(f"backward_{chunk}"):
            grads = backward(
                chunk, early + [late[chunk]], upstream, bwd_segments, column, factor, grads
            )
    received = jnp.where(came_around(1), received_around, received)
    return (received, grads)


def solution(mesh):
    placed = (
        P(None, ("pipe", "dp"), None, "tensor"),
        P(("pipe", "dp"), None),
        P(None, ("pipe", "dp"), "tensor", None),
        P(("pipe", "dp"), None),
        P(("pipe", "dp"), None, "tensor"),
        P(("pipe", "dp")),
    )
    return jax.shard_map(
        on_device,
        mesh=mesh,
        in_specs=placed,
        out_specs=(P(("pipe", "dp"), None, "tensor"), P(None, ("pipe", "dp"), None, "tensor")),
        check_vma=False,
    )
```

```python
import functools
import math

import jax
import jax.numpy as jnp
from jax import lax
from jax.experimental import pallas as pl
from jax.experimental.pallas import tpu as pltpu
from jax.sharding import PartitionSpec as P

HEAD_DIM = 128
FORWARD_STEPS = 4
CHUNKS = ((0, 8), (8, 4), (12, 4))
SCALE = HEAD_DIM ** (-0.5)
EXPONENT = SCALE * math.log2(math.e)
NT = (((1,), (1,)), ((), ()))
NN = (((1,), (0,)), ((), ()))
TN = (((0,), (0,)), ((), ()))
AXES = ("pipe", "tensor")


def product(left, right, dims):
    return lax.dot_general(left, right, dims, preferred_element_type=jnp.float32)


def probabilities(queries, keys, outside):
    logits = product(queries, keys, NT) + outside
    highest = jnp.max(logits, axis=1, keepdims=True)
    weights = jnp.exp2((logits - highest) * EXPONENT)
    return weights * (1.0 / jnp.sum(weights, axis=1, keepdims=True))


def outside_of(segment_ref):
    length = segment_ref.shape[1]
    across = jnp.broadcast_to(segment_ref[...].astype(jnp.float32), (length, length))
    return jnp.where(across == across.T, 0.0, -1e31).astype(jnp.float32)


def forward_kernel(qkv_ref, grad_ref, segment_ref, out_ref, aside_ref, outside):
    sends_out = detoured(lax.axis_index("pipe"), 1, 1) == 1

    @pl.when(pl.program_id(0) == 0)
    def _():
        outside[...] = outside_of(segment_ref)

    for start in range(0, out_ref.shape[2], HEAD_DIM):
        head = slice(start, start + HEAD_DIM)
        probs = probabilities(qkv_ref[0, 0, :, head], qkv_ref[1, 0, :, head], outside[...])
        mixed = product(probs.astype(jnp.bfloat16), qkv_ref[2, 0, :, head], NN)
        mixed = mixed.astype(jnp.bfloat16)
        out_ref[0, :, head] = mixed
        aside_ref[0, :, head] = jnp.where(sends_out, mixed, grad_ref[0, :, head])


def forward(qkv, grad_out, segment):
    _, _, length, width = qkv.shape
    step = width // FORWARD_STEPS
    columns = pl.BlockSpec((1, length, step), lambda c: (0, 0, c))
    out = jax.ShapeDtypeStruct((1, length, width), jnp.bfloat16)
    return pl.pallas_call(
        forward_kernel,
        grid=(FORWARD_STEPS,),
        in_specs=[
            pl.BlockSpec((3, 1, length, step), lambda c: (0, 0, 0, c)),
            columns,
            pl.BlockSpec((1, length), lambda c: (0, 0)),
        ],
        out_specs=[columns, columns],
        out_shape=[out, out],
        scratch_shapes=[pltpu.VMEM((length, length), jnp.float32)],
        compiler_params=pltpu.CompilerParams(vmem_limit_bytes=56 * 1024 * 1024),
        cost_estimate=pl.CostEstimate(
            flops=4 * length * length * width,
            bytes_accessed=12 * length * width,
            transcendentals=length * length * width // HEAD_DIM,
        ),
    )(qkv, grad_out, segment)


def backward_kernel(parts, *refs):
    pieces, refs = refs[:parts], refs[parts:]
    direct_ref, around_ref, segment_ref, factor_ref = refs[:4]
    out_ref, stash = refs[-2:] if len(refs) < 8 else (refs[-3], refs[-1])
    around = came_around(-1)
    mine = lax.axis_index("tensor")
    rows = pieces[0].shape[2]
    for k in range(parts):
        start = pl.multiple_of((mine ^ k) * rows, rows)
        stash[:, pl.ds(start, rows), :] = pieces[k][:, 0]
    outside = outside_of(segment_ref)
    factor = factor_ref[0]
    for start in range(0, direct_ref.shape[2], HEAD_DIM):
        head = slice(start, start + HEAD_DIM)
        queries, keys, values = stash[0, :, head], stash[1, :, head], stash[2, :, head]
        upstream = jnp.where(around, around_ref[0, :, head], direct_ref[0, :, head])
        probs = probabilities(queries, keys, outside)
        grad_value = product(probs.astype(jnp.bfloat16), upstream, TN)
        grad_probs = product(upstream, values, NT)
        center = jnp.sum(probs * grad_probs, axis=1, keepdims=True)
        grad_logits = (probs * (grad_probs - center) * SCALE).astype(jnp.bfloat16)
        out_ref[0, 0, :, head] = (product(grad_logits, keys, NN) * factor).astype(jnp.bfloat16)
        out_ref[1, 0, :, head] = (product(grad_logits, queries, TN) * factor).astype(jnp.bfloat16)
        out_ref[2, 0, :, head] = (grad_value * factor).astype(jnp.bfloat16)


def backward(chunk, pieces, upstream, segment, factor, earlier, carried=None):
    _, length, width = upstream[0].shape
    first, heads = CHUNKS[chunk]
    step = heads * HEAD_DIM
    place = first // heads
    parts = len(pieces)
    operands = [*pieces, *upstream, segment, factor]
    in_specs = [pl.BlockSpec(memory_space=pltpu.VMEM)] * parts + [
        pl.BlockSpec((1, length, step), lambda i: (0, 0, place)),
        pl.BlockSpec((1, length, step), lambda i: (0, 0, place)),
        pl.BlockSpec((1, length), lambda i: (0, 0)),
        pl.BlockSpec(memory_space=pltpu.SMEM),
    ]
    out_specs = [pl.BlockSpec((3, 1, length, step), lambda i: (0, 0, 0, place))]
    out_shape = [jax.ShapeDtypeStruct((3, 1, length, width), jnp.bfloat16)]
    aliases = {}
    for array in (earlier, carried):
        if array is not None:
            aliases[len(operands)] = len(aliases)
            operands.append(array)
            in_specs.append(pl.BlockSpec(memory_space=pl.ANY))
    if carried is not None:
        out_specs.append(pl.BlockSpec(memory_space=pl.ANY))
        out_shape.append(jax.ShapeDtypeStruct(carried.shape, carried.dtype))
    return pl.pallas_call(
        functools.partial(backward_kernel, parts),
        grid=(1,),
        in_specs=in_specs,
        out_specs=out_specs,
        out_shape=out_shape,
        scratch_shapes=[pltpu.VMEM((3, length, step), jnp.bfloat16)],
        input_output_aliases=aliases,
        compiler_params=pltpu.CompilerParams(vmem_limit_bytes=32 * 1024 * 1024),
        cost_estimate=pl.CostEstimate(
            flops=10 * length * length * step,
            bytes_accessed=14 * length * step,
            transcendentals=length * length * step // HEAD_DIM,
        ),
    )(*operands)


def fetched(piece, k):
    sections, tensors = lax.axis_size("pipe"), lax.axis_size("tensor")
    pairs = [
        (p * tensors + t, (sections - 1 - p) * tensors + (t ^ k))
        for p in range(sections)
        for t in range(tensors)
    ]
    return lax.ppermute(piece, AXES, pairs)


def detoured(p, t, by):
    half = lax.axis_size("pipe") // 2
    return (t & 1) * (p % half == (half - 1 if by > 0 else 0))


def shifted(array, by):
    sections, tensors = lax.axis_size("pipe"), lax.axis_size("tensor")
    pairs = [
        (p * tensors + t, (p + by) % sections * tensors + t)
        for p in range(sections)
        for t in range(tensors)
        if not detoured(p, t, by)
    ]
    with jax.named_scope("direct_out" if by > 0 else "direct_grad"):
        return lax.ppermute(array, AXES, pairs)


def detour(array, leg):
    sections, tensors = lax.axis_size("pipe"), lax.axis_size("tensor")
    pairs = []
    for by in (-1, 1):
        for p in range(sections):
            for t in range(tensors):
                if detoured(p, t, by):
                    start, end = (p, p - by) if leg == "aside" else (p - by, p + by)
                    pairs.append((start % sections * tensors + t, end % sections * tensors + t))
    with jax.named_scope(f"{leg}_both"):
        return lax.ppermute(array, AXES, pairs)


def came_around(by):
    sections = lax.axis_size("pipe")
    source = (lax.axis_index("pipe") + sections - by) % sections
    return detoured(source, lax.axis_index("tensor"), by) == 1


def on_device(fwd_qkv, fwd_segments, parked, bwd_segments, grad_out, loss_tokens):
    length, width = grad_out.shape[1:]
    tensors = lax.axis_size("tensor")
    mine = lax.axis_index("tensor")

    def fetched_chunk(whole, chunk):
        first, heads = CHUNKS[chunk]
        pieces = []
        for k in range(tensors):
            start = (mine ^ k) * width + first * HEAD_DIM
            piece = lax.dynamic_slice_in_dim(whole, start, heads * HEAD_DIM, axis=3)
            with jax.named_scope(f"stash_{k}_{chunk}"):
                pieces.append(fetched(piece, k))
        return pieces

    upstream_direct = shifted(grad_out, -1)
    with jax.named_scope("forward_heads"):
        forward_out, aside = forward(fwd_qkv, grad_out, fwd_segments)
    received_direct = shifted(forward_out, 1)
    around = detour(detour(aside, "aside"), "onward")
    upstream = (upstream_direct, around)
    pieces = [fetched_chunk(parked, 0)]
    tokens = loss_tokens.astype(jnp.float32)
    pieces[0][0], tokens = lax.optimization_barrier((pieces[0][0], tokens))
    token_total = lax.psum(tokens, "dp")
    factor = jnp.float32(lax.axis_size("dp") * length) / token_total
    parked, token_total = lax.optimization_barrier((parked, token_total))
    pieces.append(fetched_chunk(parked, 1))
    received = jnp.where(came_around(1), around, received_direct)
    (grads,) = backward(0, pieces[0], upstream, bwd_segments, factor, None)
    parked, grads = lax.optimization_barrier((parked, grads))
    pieces.append(fetched_chunk(parked, 2))
    (grads,) = backward(1, pieces[1], upstream, bwd_segments, factor, grads)
    grads, received = backward(2, pieces[2], upstream, bwd_segments, factor, grads, received)
    return (received, grads)


def solution(mesh):
    placed = (
        P(None, ("pipe", "dp"), None, "tensor"),
        P(("pipe", "dp"), None),
        P(None, ("pipe", "dp"), "tensor", None),
        P(("pipe", "dp"), None),
        P(("pipe", "dp"), None, "tensor"),
        P(("pipe", "dp")),
    )
    return jax.shard_map(
        on_device,
        mesh=mesh,
        in_specs=placed,
        out_specs=(P(("pipe", "dp"), None, "tensor"), P(None, ("pipe", "dp"), None, "tensor")),
        check_vma=False,
    )
```

```python
import functools
import math

import jax
import jax.numpy as jnp
from jax import lax
from jax.experimental import pallas as pl
from jax.experimental.pallas import tpu as pltpu
from jax.sharding import PartitionSpec as P

HEAD_DIM = 128
FORWARD_STEPS = 4
CHUNKS = ((0, 8), (8, 4), (12, 4))
SCALE = HEAD_DIM ** (-0.5)
EXPONENT = SCALE * math.log2(math.e)
NT = (((1,), (1,)), ((), ()))
NN = (((1,), (0,)), ((), ()))
TN = (((0,), (0,)), ((), ()))
AXES = ("pipe", "tensor")


def product(left, right, dims):
    return lax.dot_general(left, right, dims, preferred_element_type=jnp.float32)


def probabilities(queries, keys, outside):
    logits = product(queries, keys, NT) + outside
    highest = jnp.max(logits, axis=1, keepdims=True)
    weights = jnp.exp2((logits - highest) * EXPONENT)
    return weights * (1.0 / jnp.sum(weights, axis=1, keepdims=True))


def outside_of(segment_ref):
    length = segment_ref.shape[1]
    across = jnp.broadcast_to(segment_ref[...].astype(jnp.float32), (length, length))
    return jnp.where(across == across.T, 0.0, -1e31).astype(jnp.float32)


def forward_kernel(qkv_ref, segment_ref, out_ref, outside):
    @pl.when(pl.program_id(0) == 0)
    def _():
        outside[...] = outside_of(segment_ref)

    for start in range(0, out_ref.shape[2], HEAD_DIM):
        head = slice(start, start + HEAD_DIM)
        probs = probabilities(qkv_ref[0, 0, :, head], qkv_ref[1, 0, :, head], outside[...])
        mixed = product(probs.astype(jnp.bfloat16), qkv_ref[2, 0, :, head], NN)
        out_ref[0, :, head] = mixed.astype(jnp.bfloat16)


def forward(qkv, segment):
    _, _, length, width = qkv.shape
    step = width // FORWARD_STEPS
    return pl.pallas_call(
        forward_kernel,
        grid=(FORWARD_STEPS,),
        in_specs=[
            pl.BlockSpec((3, 1, length, step), lambda c: (0, 0, 0, c)),
            pl.BlockSpec((1, length), lambda c: (0, 0)),
        ],
        out_specs=pl.BlockSpec((1, length, step), lambda c: (0, 0, c)),
        out_shape=jax.ShapeDtypeStruct((1, length, width), jnp.bfloat16),
        scratch_shapes=[pltpu.VMEM((length, length), jnp.float32)],
        compiler_params=pltpu.CompilerParams(vmem_limit_bytes=56 * 1024 * 1024),
        cost_estimate=pl.CostEstimate(
            flops=4 * length * length * width,
            bytes_accessed=8 * length * width,
            transcendentals=length * length * width // HEAD_DIM,
        ),
    )(qkv, segment)


def backward_kernel(parts, *refs):
    pieces, refs = refs[:parts], refs[parts:]
    upstream_ref, segment_ref, factor_ref = refs[:3]
    out_ref, stash = refs[-2:] if len(refs) < 7 else (refs[-3], refs[-1])
    mine = lax.axis_index("tensor")
    rows = pieces[0].shape[2]
    for k in range(parts):
        start = pl.multiple_of((mine ^ k) * rows, rows)
        stash[:, pl.ds(start, rows), :] = pieces[k][:, 0]
    outside = outside_of(segment_ref)
    factor = factor_ref[0]
    for start in range(0, upstream_ref.shape[2], HEAD_DIM):
        head = slice(start, start + HEAD_DIM)
        queries, keys, values = stash[0, :, head], stash[1, :, head], stash[2, :, head]
        upstream = upstream_ref[0, :, head]
        probs = probabilities(queries, keys, outside)
        grad_value = product(probs.astype(jnp.bfloat16), upstream, TN)
        grad_probs = product(upstream, values, NT)
        center = jnp.sum(probs * grad_probs, axis=1, keepdims=True)
        grad_logits = (probs * (grad_probs - center) * SCALE).astype(jnp.bfloat16)
        out_ref[0, 0, :, head] = (product(grad_logits, keys, NN) * factor).astype(jnp.bfloat16)
        out_ref[1, 0, :, head] = (product(grad_logits, queries, TN) * factor).astype(jnp.bfloat16)
        out_ref[2, 0, :, head] = (grad_value * factor).astype(jnp.bfloat16)


def backward(chunk, pieces, upstream, segment, factor, earlier, carried=None):
    _, length, width = upstream.shape
    first, heads = CHUNKS[chunk]
    step = heads * HEAD_DIM
    place = first // heads
    parts = len(pieces)
    operands = [*pieces, upstream, segment, factor]
    in_specs = [pl.BlockSpec(memory_space=pltpu.VMEM)] * parts + [
        pl.BlockSpec((1, length, step), lambda i: (0, 0, place)),
        pl.BlockSpec((1, length), lambda i: (0, 0)),
        pl.BlockSpec(memory_space=pltpu.SMEM),
    ]
    out_specs = [pl.BlockSpec((3, 1, length, step), lambda i: (0, 0, 0, place))]
    out_shape = [jax.ShapeDtypeStruct((3, 1, length, width), jnp.bfloat16)]
    aliases = {}
    for array in (earlier, carried):
        if array is not None:
            aliases[len(operands)] = len(aliases)
            operands.append(array)
            in_specs.append(pl.BlockSpec(memory_space=pl.ANY))
    if carried is not None:
        out_specs.append(pl.BlockSpec(memory_space=pl.ANY))
        out_shape.append(jax.ShapeDtypeStruct(carried.shape, carried.dtype))
    return pl.pallas_call(
        functools.partial(backward_kernel, parts),
        grid=(1,),
        in_specs=in_specs,
        out_specs=out_specs,
        out_shape=out_shape,
        scratch_shapes=[pltpu.VMEM((3, length, step), jnp.bfloat16)],
        input_output_aliases=aliases,
        compiler_params=pltpu.CompilerParams(vmem_limit_bytes=32 * 1024 * 1024),
        cost_estimate=pl.CostEstimate(
            flops=10 * length * length * step,
            bytes_accessed=14 * length * step,
            transcendentals=length * length * step // HEAD_DIM,
        ),
    )(*operands)


def fetched(piece, k):
    sections, tensors = lax.axis_size("pipe"), lax.axis_size("tensor")
    pairs = [
        (p * tensors + t, (sections - 1 - p) * tensors + (t ^ k))
        for p in range(sections)
        for t in range(tensors)
    ]
    return lax.ppermute(piece, AXES, pairs)


def detoured(p, t, by):
    half = lax.axis_size("pipe") // 2
    return (t & 1) * (p % half == (half - 1 if by > 0 else 0))


def shift_pairs(by, leg):
    sections, tensors = lax.axis_size("pipe"), lax.axis_size("tensor")
    pairs = []
    for p in range(sections):
        for t in range(tensors):
            aside = detoured(p, t, by)
            start, end = p, p + by
            if leg == "aside":
                end = p - by
            if leg == "onward":
                start = p - by
            if leg == "whole" or aside == (leg != "direct"):
                pairs.append((start % sections * tensors + t, end % sections * tensors + t))
    return pairs


def shifted(array, by, leg):
    with jax.named_scope(f"{leg}_{'out' if by > 0 else 'grad'}"):
        return lax.ppermute(array, AXES, shift_pairs(by, leg))


def came_around(by):
    sections = lax.axis_size("pipe")
    source = (lax.axis_index("pipe") + sections - by) % sections
    return detoured(source, lax.axis_index("tensor"), by) == 1


def on_device(fwd_qkv, fwd_segments, parked, bwd_segments, grad_out, loss_tokens):
    length, width = grad_out.shape[1:]
    tensors = lax.axis_size("tensor")
    mine = lax.axis_index("tensor")

    def fetched_chunk(whole, chunk):
        first, heads = CHUNKS[chunk]
        pieces = []
        for k in range(tensors):
            start = (mine ^ k) * width + first * HEAD_DIM
            piece = lax.dynamic_slice_in_dim(whole, start, heads * HEAD_DIM, axis=3)
            with jax.named_scope(f"stash_{k}_{chunk}"):
                pieces.append(fetched(piece, k))
        return pieces

    upstream = shifted(grad_out, -1, "whole")
    with jax.named_scope("forward_heads"):
        forward_out = forward(fwd_qkv, fwd_segments)
    received_direct = shifted(forward_out, 1, "whole")
    received_aside = shifted(forward_out, 1, "aside")
    received_around = shifted(received_aside, 1, "onward")
    pieces = [fetched_chunk(parked, 0)]
    tokens = loss_tokens.astype(jnp.float32)
    pieces[0][0], tokens = lax.optimization_barrier((pieces[0][0], tokens))
    token_total = lax.psum(tokens, "dp")
    factor = jnp.float32(lax.axis_size("dp") * length) / token_total
    parked, token_total = lax.optimization_barrier((parked, token_total))
    pieces.append(fetched_chunk(parked, 1))
    received = received_direct
    (grads,) = backward(0, pieces[0], upstream, bwd_segments, factor, None)
    parked, grads = lax.optimization_barrier((parked, grads))
    pieces.append(fetched_chunk(parked, 2))
    (grads,) = backward(1, pieces[1], upstream, bwd_segments, factor, grads)
    grads, received = backward(2, pieces[2], upstream, bwd_segments, factor, grads, received)
    return (received, grads)


def solution(mesh):
    placed = (
        P(None, ("pipe", "dp"), None, "tensor"),
        P(("pipe", "dp"), None),
        P(None, ("pipe", "dp"), "tensor", None),
        P(("pipe", "dp"), None),
        P(("pipe", "dp"), None, "tensor"),
        P(("pipe", "dp")),
    )
    return jax.shard_map(
        on_device,
        mesh=mesh,
        in_specs=placed,
        out_specs=(P(("pipe", "dp"), None, "tensor"), P(None, ("pipe", "dp"), None, "tensor")),
        check_vma=False,
    )
```

```python
import functools
import math

import jax
import jax.numpy as jnp
from jax import lax
from jax.experimental import pallas as pl
from jax.experimental.pallas import tpu as pltpu
from jax.sharding import PartitionSpec as P

HEAD_DIM = 128
FORWARD_STEPS = 4
CHUNKS = ((0, 8), (8, 4), (12, 4))
SCALE = HEAD_DIM ** (-0.5)
EXPONENT = SCALE * math.log2(math.e)
NT = (((1,), (1,)), ((), ()))
NN = (((1,), (0,)), ((), ()))
TN = (((0,), (0,)), ((), ()))
AXES = ("pipe", "tensor")


def product(left, right, dims):
    return lax.dot_general(left, right, dims, preferred_element_type=jnp.float32)


def probabilities(queries, keys, outside):
    logits = product(queries, keys, NT) + outside
    highest = jnp.max(logits, axis=1, keepdims=True)
    weights = jnp.exp2((logits - highest) * EXPONENT)
    return weights * (1.0 / jnp.sum(weights, axis=1, keepdims=True))


def outside_of(segment_ref):
    length = segment_ref.shape[1]
    across = jnp.broadcast_to(segment_ref[...].astype(jnp.float32), (length, length))
    return jnp.where(across == across.T, 0.0, -1e31).astype(jnp.float32)


def forward_kernel(qkv_ref, segment_ref, out_ref, outside):
    @pl.when(pl.program_id(0) == 0)
    def _():
        outside[...] = outside_of(segment_ref)

    for start in range(0, out_ref.shape[2], HEAD_DIM):
        head = slice(start, start + HEAD_DIM)
        probs = probabilities(qkv_ref[0, 0, :, head], qkv_ref[1, 0, :, head], outside[...])
        mixed = product(probs.astype(jnp.bfloat16), qkv_ref[2, 0, :, head], NN)
        out_ref[0, :, head] = mixed.astype(jnp.bfloat16)


def forward(qkv, segment):
    _, _, length, width = qkv.shape
    step = width // FORWARD_STEPS
    return pl.pallas_call(
        forward_kernel,
        grid=(FORWARD_STEPS,),
        in_specs=[
            pl.BlockSpec((3, 1, length, step), lambda c: (0, 0, 0, c)),
            pl.BlockSpec((1, length), lambda c: (0, 0)),
        ],
        out_specs=pl.BlockSpec((1, length, step), lambda c: (0, 0, c)),
        out_shape=jax.ShapeDtypeStruct((1, length, width), jnp.bfloat16),
        scratch_shapes=[pltpu.VMEM((length, length), jnp.float32)],
        compiler_params=pltpu.CompilerParams(vmem_limit_bytes=56 * 1024 * 1024),
        cost_estimate=pl.CostEstimate(
            flops=4 * length * length * width,
            bytes_accessed=8 * length * width,
            transcendentals=length * length * width // HEAD_DIM,
        ),
    )(qkv, segment)


def backward_kernel(parts, carries, *refs):
    pieces, refs = refs[:parts], refs[parts:]
    upstream_ref, segment_ref, factor_ref = refs[:3]
    out_ref, stash = refs[-2:]
    if carries:
        out_ref = refs[-3]
        refs[-2][...] = refs[3][...]
    mine = lax.axis_index("tensor")
    rows = pieces[0].shape[2]
    found = [piece[:, 0] for piece in pieces]
    if parts > 4:
        around = found.pop(1)
        found[0] = jnp.where(detoured(lax.axis_index("pipe")), around, found[0])
    for k, piece in enumerate(found):
        start = pl.multiple_of((mine ^ k) * rows, rows)
        stash[:, pl.ds(start, rows), :] = piece
    outside = outside_of(segment_ref)
    factor = factor_ref[0]
    for start in range(0, upstream_ref.shape[2], HEAD_DIM):
        head = slice(start, start + HEAD_DIM)
        queries, keys, values = stash[0, :, head], stash[1, :, head], stash[2, :, head]
        upstream = upstream_ref[0, :, head]
        probs = probabilities(queries, keys, outside)
        grad_value = product(probs.astype(jnp.bfloat16), upstream, TN)
        grad_probs = product(upstream, values, NT)
        center = jnp.sum(probs * grad_probs, axis=1, keepdims=True)
        grad_logits = (probs * (grad_probs - center) * SCALE).astype(jnp.bfloat16)
        out_ref[0, 0, :, head] = (product(grad_logits, keys, NN) * factor).astype(jnp.bfloat16)
        out_ref[1, 0, :, head] = (product(grad_logits, queries, TN) * factor).astype(jnp.bfloat16)
        out_ref[2, 0, :, head] = (grad_value * factor).astype(jnp.bfloat16)


def backward(chunk, pieces, upstream, segment, factor, earlier, carried=None):
    _, length, width = upstream.shape
    first, heads = CHUNKS[chunk]
    step = heads * HEAD_DIM
    place = first // heads
    parts = len(pieces)
    operands = [*pieces, upstream, segment, factor]
    in_specs = [pl.BlockSpec(memory_space=pltpu.VMEM)] * parts + [
        pl.BlockSpec((1, length, step), lambda i: (0, 0, place)),
        pl.BlockSpec((1, length), lambda i: (0, 0)),
        pl.BlockSpec(memory_space=pltpu.SMEM),
    ]
    out_specs = [pl.BlockSpec((3, 1, length, step), lambda i: (0, 0, 0, place))]
    out_shape = [jax.ShapeDtypeStruct((3, 1, length, width), jnp.bfloat16)]
    if carried is not None:
        whole = pl.BlockSpec(carried.shape, lambda i: (0, 0, 0))
        operands.append(carried)
        in_specs.append(whole)
        out_specs.append(whole)
        out_shape.append(jax.ShapeDtypeStruct(carried.shape, carried.dtype))
    aliases = {}
    if earlier is not None:
        aliases = {len(operands): 0}
        operands.append(earlier)
        in_specs.append(pl.BlockSpec(memory_space=pl.ANY))
    return pl.pallas_call(
        functools.partial(backward_kernel, parts, carried is not None),
        grid=(1,),
        in_specs=in_specs,
        out_specs=out_specs,
        out_shape=out_shape,
        scratch_shapes=[pltpu.VMEM((3, length, step), jnp.bfloat16)],
        input_output_aliases=aliases,
        compiler_params=pltpu.CompilerParams(vmem_limit_bytes=32 * 1024 * 1024),
        cost_estimate=pl.CostEstimate(
            flops=10 * length * length * step,
            bytes_accessed=14 * length * step,
            transcendentals=length * length * step // HEAD_DIM,
        ),
    )(*operands)


def fetched(piece, k, leg="direct"):
    sections, tensors = lax.axis_size("pipe"), lax.axis_size("tensor")
    pairs = []
    for p in range(sections):
        for t in range(tensors):
            start, end = p, sections - 1 - p
            if leg == "aside":
                end = p ^ 1
            if leg == "onward":
                start = p ^ 1
            if leg == "all" or (leg == "direct") != detoured(p):
                pairs.append((start * tensors + t, end * tensors + (t ^ k)))
    return lax.ppermute(piece, AXES, pairs)


def detoured(section):
    half = lax.axis_size("pipe") // 2
    place = section % half
    return (place == 2) | (place == half - 3)


def shifted(array, by):
    sections = lax.axis_size("pipe")
    with jax.named_scope("direct_out" if by > 0 else "direct_grad"):
        return lax.ppermute(array, "pipe", [(p, (p + by) % sections) for p in range(sections)])


def on_device(fwd_qkv, fwd_segments, parked, bwd_segments, grad_out, loss_tokens):
    length, width = grad_out.shape[1:]
    tensors = lax.axis_size("tensor")
    mine = lax.axis_index("tensor")

    def fetched_chunk(whole, chunk):
        first, heads = CHUNKS[chunk]
        pieces = []
        for k in range(tensors):
            start = (mine ^ k) * width + first * HEAD_DIM
            piece = lax.dynamic_slice_in_dim(whole, start, heads * HEAD_DIM, axis=3)
            around = chunk == 0 and k == 0
            with jax.named_scope(f"stash_{k}_{chunk}"):
                pieces.append(fetched(piece, k, "direct" if around else "all"))
            if around:
                with jax.named_scope("aside_0"):
                    piece = fetched(piece, k, "aside")
                with jax.named_scope("onward_0"):
                    pieces.append(fetched(piece, k, "onward"))
        return pieces

    upstream = shifted(grad_out, -1)
    pieces = [fetched_chunk(parked, 0)]
    with jax.named_scope("forward_heads"):
        forward_out = forward(fwd_qkv, fwd_segments)
    received = shifted(forward_out, 1)
    tokens = loss_tokens.astype(jnp.float32)
    pieces[0][0], tokens = lax.optimization_barrier((pieces[0][0], tokens))
    token_total = lax.psum(tokens, "dp")
    factor = jnp.float32(lax.axis_size("dp") * length) / token_total
    parked, token_total = lax.optimization_barrier((parked, token_total))
    pieces.append(fetched_chunk(parked, 1))
    (grads,) = backward(0, pieces[0], upstream, bwd_segments, factor, None)
    parked, grads = lax.optimization_barrier((parked, grads))
    pieces.append(fetched_chunk(parked, 2))
    grads, received = backward(1, pieces[1], upstream, bwd_segments, factor, grads, received)
    (grads,) = backward(2, pieces[2], upstream, bwd_segments, factor, grads)
    return (received, grads)


def solution(mesh):
    placed = (
        P(None, ("pipe", "dp"), None, "tensor"),
        P(("pipe", "dp"), None),
        P(None, ("pipe", "dp"), "tensor", None),
        P(("pipe", "dp"), None),
        P(("pipe", "dp"), None, "tensor"),
        P(("pipe", "dp")),
    )
    return jax.shard_map(
        on_device,
        mesh=mesh,
        in_specs=placed,
        out_specs=(P(("pipe", "dp"), None, "tensor"), P(None, ("pipe", "dp"), None, "tensor")),
        check_vma=False,
    )
```

```python
import functools
import math

import jax
import jax.numpy as jnp
from jax import lax
from jax.experimental import pallas as pl
from jax.experimental.pallas import tpu as pltpu
from jax.sharding import PartitionSpec as P

HEAD_DIM = 128
FORWARD_STEPS = 2
CHUNKS = ((8, 8), (0, 6), (6, 2))
SCALE = HEAD_DIM ** (-0.5)
EXPONENT = SCALE * math.log2(math.e)
NT = (((1,), (1,)), ((), ()))
NN = (((1,), (0,)), ((), ()))
TN = (((0,), (0,)), ((), ()))
AXES = ("pipe", "tensor")


def product(left, right, dims):
    return lax.dot_general(left, right, dims, preferred_element_type=jnp.float32)


def probabilities(queries, keys, outside):
    logits = product(keys, queries, NT) + outside
    highest = jnp.max(logits, axis=0, keepdims=True)
    weights = jnp.exp2((logits - highest) * EXPONENT)
    return weights * (1.0 / jnp.sum(weights, axis=0, keepdims=True))


def outside_of(segment_ref):
    length = segment_ref.shape[1]
    across = jnp.broadcast_to(segment_ref[...].astype(jnp.float32), (length, length))
    return jnp.where(across == across.T, 0.0, -1e31).astype(jnp.float32)


def forward_kernel(qkv_ref, segment_ref, out_ref, outside):
    @pl.when(pl.program_id(0) == 0)
    def _():
        outside[...] = outside_of(segment_ref)

    for start in range(0, out_ref.shape[2], HEAD_DIM):
        head = slice(start, start + HEAD_DIM)
        probs = probabilities(qkv_ref[0, 0, :, head], qkv_ref[1, 0, :, head], outside[...])
        mixed = product(probs.astype(jnp.bfloat16), qkv_ref[2, 0, :, head], TN)
        out_ref[0, :, head] = mixed.astype(jnp.bfloat16)


def forward(qkv, segment):
    _, _, length, width = qkv.shape
    step = width // FORWARD_STEPS
    return pl.pallas_call(
        forward_kernel,
        grid=(FORWARD_STEPS,),
        in_specs=[
            pl.BlockSpec((3, 1, length, step), lambda c: (0, 0, 0, c)),
            pl.BlockSpec((1, length), lambda c: (0, 0)),
        ],
        out_specs=pl.BlockSpec((1, length, step), lambda c: (0, 0, c)),
        out_shape=jax.ShapeDtypeStruct((1, length, width), jnp.bfloat16),
        scratch_shapes=[pltpu.VMEM((length, length), jnp.float32)],
        compiler_params=pltpu.CompilerParams(vmem_limit_bytes=56 * 1024 * 1024),
        cost_estimate=pl.CostEstimate(
            flops=4 * length * length * width,
            bytes_accessed=8 * length * width,
            transcendentals=length * length * width // HEAD_DIM,
        ),
    )(qkv, segment)


def backward_kernel(parts, carries, *refs):
    pieces, refs = refs[:parts], refs[parts:]
    upstream_ref, segment_ref, factor_ref = refs[:3]
    out_ref, stash = refs[-2:]
    if carries:
        out_ref = refs[-3]
        refs[-2][...] = refs[3][...]
    mine = lax.axis_index("tensor")
    rows = pieces[0].shape[2]
    found = [piece[:, 0] for piece in pieces]
    if parts > 4:
        around = found.pop(1)
        found[0] = jnp.where(detoured(lax.axis_index("pipe")), around, found[0])
    for k, piece in enumerate(found):
        start = pl.multiple_of((mine ^ k) * rows, rows)
        stash[:, pl.ds(start, rows), :] = piece
    outside = outside_of(segment_ref)
    factor = factor_ref[0]
    for start in range(0, upstream_ref.shape[2], HEAD_DIM):
        head = slice(start, start + HEAD_DIM)
        queries, keys, values = stash[0, :, head], stash[1, :, head], stash[2, :, head]
        upstream = upstream_ref[0, :, head]
        probs = probabilities(queries, keys, outside)
        grad_value = product(probs.astype(jnp.bfloat16), upstream, NN)
        grad_probs = product(values, upstream, NT)
        center = jnp.sum(probs * grad_probs, axis=0, keepdims=True)
        grad_logits = (probs * ((grad_probs - center) * SCALE)).astype(jnp.bfloat16)
        out_ref[0, 0, :, head] = (product(grad_logits, keys, TN) * factor).astype(jnp.bfloat16)
        out_ref[1, 0, :, head] = (product(grad_logits, queries, NN) * factor).astype(jnp.bfloat16)
        out_ref[2, 0, :, head] = (grad_value * factor).astype(jnp.bfloat16)


def backward(chunk, pieces, upstream, segment, factor, earlier, carried=None):
    _, length, width = upstream.shape
    first, heads = CHUNKS[chunk]
    step = heads * HEAD_DIM
    place = first // heads
    parts = len(pieces)
    operands = [*pieces, upstream, segment, factor]
    in_specs = [pl.BlockSpec(memory_space=pltpu.VMEM)] * parts + [
        pl.BlockSpec((1, length, step), lambda i: (0, 0, place)),
        pl.BlockSpec((1, length), lambda i: (0, 0)),
        pl.BlockSpec(memory_space=pltpu.SMEM),
    ]
    out_specs = [pl.BlockSpec((3, 1, length, step), lambda i: (0, 0, 0, place))]
    out_shape = [jax.ShapeDtypeStruct((3, 1, length, width), jnp.bfloat16)]
    if carried is not None:
        whole = pl.BlockSpec(carried.shape, lambda i: (0, 0, 0))
        operands.append(carried)
        in_specs.append(whole)
        out_specs.append(whole)
        out_shape.append(jax.ShapeDtypeStruct(carried.shape, carried.dtype))
    aliases = {}
    if earlier is not None:
        aliases = {len(operands): 0}
        operands.append(earlier)
        in_specs.append(pl.BlockSpec(memory_space=pl.ANY))
    return pl.pallas_call(
        functools.partial(backward_kernel, parts, carried is not None),
        grid=(1,),
        in_specs=in_specs,
        out_specs=out_specs,
        out_shape=out_shape,
        scratch_shapes=[pltpu.VMEM((3, length, step), jnp.bfloat16)],
        input_output_aliases=aliases,
        compiler_params=pltpu.CompilerParams(vmem_limit_bytes=32 * 1024 * 1024),
        cost_estimate=pl.CostEstimate(
            flops=10 * length * length * step,
            bytes_accessed=14 * length * step,
            transcendentals=length * length * step // HEAD_DIM,
        ),
    )(*operands)


def fetched(piece, k, leg="direct"):
    sections, tensors = lax.axis_size("pipe"), lax.axis_size("tensor")
    pairs = []
    for p in range(sections):
        for t in range(tensors):
            start, end = p, sections - 1 - p
            if leg == "aside":
                end = p ^ 1
            if leg == "onward":
                start = p ^ 1
            if leg == "all" or (leg == "direct") != detoured(p):
                pairs.append((start * tensors + t, end * tensors + (t ^ k)))
    return lax.ppermute(piece, AXES, pairs)


def detoured(section):
    half = lax.axis_size("pipe") // 2
    place = section % half
    return (place == 2) | (place == half - 3)


def shifted(array, by):
    sections = lax.axis_size("pipe")
    with jax.named_scope("direct_out" if by > 0 else "direct_grad"):
        return lax.ppermute(array, "pipe", [(p, (p + by) % sections) for p in range(sections)])


def on_device(fwd_qkv, fwd_segments, parked, bwd_segments, grad_out, loss_tokens):
    length, width = grad_out.shape[1:]
    tensors = lax.axis_size("tensor")
    mine = lax.axis_index("tensor")

    def fetched_chunk(whole, chunk):
        first, heads = CHUNKS[chunk]
        pieces = []
        for k in range(tensors):
            start = (mine ^ k) * width + first * HEAD_DIM
            piece = lax.dynamic_slice_in_dim(whole, start, heads * HEAD_DIM, axis=3)
            around = chunk == 0 and k == 0
            with jax.named_scope(f"stash_{k}_{chunk}"):
                pieces.append(fetched(piece, k, "direct" if around else "all"))
            if around:
                with jax.named_scope("aside_0"):
                    piece = fetched(piece, k, "aside")
                with jax.named_scope("onward_0"):
                    pieces.append(fetched(piece, k, "onward"))
        return pieces

    upstream = shifted(grad_out, -1)
    pieces = [fetched_chunk(parked, 0)]
    with jax.named_scope("forward_heads"):
        forward_out = forward(fwd_qkv, fwd_segments)
    received = shifted(forward_out, 1)
    tokens = loss_tokens.astype(jnp.float32)
    pieces[0][0], tokens = lax.optimization_barrier((pieces[0][0], tokens))
    token_total = lax.psum(tokens, "dp")
    factor = jnp.float32(lax.axis_size("dp") * length) / token_total
    parked, token_total = lax.optimization_barrier((parked, token_total))
    pieces.append(fetched_chunk(parked, 1))
    (grads,) = backward(0, pieces[0], upstream, bwd_segments, factor, None)
    parked, grads = lax.optimization_barrier((parked, grads))
    pieces.append(fetched_chunk(parked, 2))
    grads, received = backward(1, pieces[1], upstream, bwd_segments, factor, grads, received)
    (grads,) = backward(2, pieces[2], upstream, bwd_segments, factor, grads)
    return (received, grads)


def solution(mesh):
    placed = (
        P(None, ("pipe", "dp"), None, "tensor"),
        P(("pipe", "dp"), None),
        P(None, ("pipe", "dp"), "tensor", None),
        P(("pipe", "dp"), None),
        P(("pipe", "dp"), None, "tensor"),
        P(("pipe", "dp")),
    )
    return jax.shard_map(
        on_device,
        mesh=mesh,
        in_specs=placed,
        out_specs=(P(("pipe", "dp"), None, "tensor"), P(None, ("pipe", "dp"), None, "tensor")),
        check_vma=False,
    )
```

```python
import functools
import math

import jax
import jax.numpy as jnp
from jax import lax
from jax.experimental import pallas as pl
from jax.experimental.pallas import tpu as pltpu
from jax.sharding import PartitionSpec as P

HEAD_DIM = 128
FORWARD_STEPS = 2
CHUNKS = ((0, 10), (12, 4), (10, 2))
DETOUR = (0, 10)
SCALE = HEAD_DIM ** (-0.5)
EXPONENT = SCALE * math.log2(math.e)
NT = (((1,), (1,)), ((), ()))
NN = (((1,), (0,)), ((), ()))
TN = (((0,), (0,)), ((), ()))
AXES = ("pipe", "tensor")


def product(left, right, dims):
    return lax.dot_general(left, right, dims, preferred_element_type=jnp.float32)


def probabilities(queries, keys, outside):
    logits = product(keys, queries, NT) + outside
    highest = jnp.max(logits, axis=0, keepdims=True)
    weights = jnp.exp2((logits - highest) * EXPONENT)
    return weights * (1.0 / jnp.sum(weights, axis=0, keepdims=True))


def outside_of(segment_ref):
    length = segment_ref.shape[1]
    across = jnp.broadcast_to(segment_ref[...].astype(jnp.float32), (length, length))
    return jnp.where(across == across.T, 0.0, -1e31).astype(jnp.float32)


def forward_kernel(qkv_ref, segment_ref, out_ref, outside):
    @pl.when(pl.program_id(0) == 0)
    def _():
        outside[...] = outside_of(segment_ref)

    for start in range(0, out_ref.shape[2], HEAD_DIM):
        head = slice(start, start + HEAD_DIM)
        probs = probabilities(qkv_ref[0, 0, :, head], qkv_ref[1, 0, :, head], outside[...])
        mixed = product(probs.astype(jnp.bfloat16), qkv_ref[2, 0, :, head], TN)
        out_ref[0, :, head] = mixed.astype(jnp.bfloat16)


def forward(qkv, segment):
    _, _, length, width = qkv.shape
    step = width // FORWARD_STEPS
    return pl.pallas_call(
        forward_kernel,
        grid=(FORWARD_STEPS,),
        in_specs=[
            pl.BlockSpec((3, 1, length, step), lambda c: (0, 0, 0, c)),
            pl.BlockSpec((1, length), lambda c: (0, 0)),
        ],
        out_specs=pl.BlockSpec((1, length, step), lambda c: (0, 0, c)),
        out_shape=jax.ShapeDtypeStruct((1, length, width), jnp.bfloat16),
        scratch_shapes=[pltpu.VMEM((length, length), jnp.float32)],
        compiler_params=pltpu.CompilerParams(vmem_limit_bytes=56 * 1024 * 1024),
        cost_estimate=pl.CostEstimate(
            flops=4 * length * length * width,
            bytes_accessed=8 * length * width,
            transcendentals=length * length * width // HEAD_DIM,
        ),
    )(qkv, segment)


def backward_kernel(parts, around_from, carries, *refs):
    pieces, refs = refs[:parts], refs[parts:]
    upstream_ref, segment_ref, factor_ref = refs[:3]
    out_ref, stash = refs[-2:]
    if carries:
        out_ref = refs[-3]
        refs[-2][...] = refs[3][...]
    mine = lax.axis_index("tensor")
    rows = pieces[0].shape[2]
    if around_from is not None:
        columns = slice(around_from, around_from + pieces[0].shape[3])
        around = pieces[-1][:, 0, :, columns]
        pieces = pieces[:-1]
    found = [piece[:, 0] for piece in pieces]
    if around_from is not None:
        found[0] = jnp.where(detoured(lax.axis_index("pipe")), around, found[0])
    for k, piece in enumerate(found):
        start = pl.multiple_of((mine ^ k) * rows, rows)
        stash[:, pl.ds(start, rows), :] = piece
    outside = outside_of(segment_ref)
    factor = factor_ref[0]
    for start in range(0, upstream_ref.shape[2], HEAD_DIM):
        head = slice(start, start + HEAD_DIM)
        queries, keys, values = stash[0, :, head], stash[1, :, head], stash[2, :, head]
        upstream = upstream_ref[0, :, head]
        probs = probabilities(queries, keys, outside)
        grad_value = product(probs.astype(jnp.bfloat16), upstream, NN)
        grad_probs = product(values, upstream, NT)
        center = jnp.sum(probs * grad_probs, axis=0, keepdims=True)
        grad_logits = (probs * ((grad_probs - center) * SCALE)).astype(jnp.bfloat16)
        out_ref[0, 0, :, head] = (product(grad_logits, keys, TN) * factor).astype(jnp.bfloat16)
        out_ref[1, 0, :, head] = (product(grad_logits, queries, NN) * factor).astype(jnp.bfloat16)
        out_ref[2, 0, :, head] = (grad_value * factor).astype(jnp.bfloat16)


def backward(chunk, pieces, around, upstream, segment, factor, earlier, carried=None):
    _, length, width = upstream.shape
    first, heads = CHUNKS[chunk]
    step = heads * HEAD_DIM
    place = first // heads
    around_from = None
    if DETOUR[0] <= first and first + heads <= sum(DETOUR):
        around_from = (first - DETOUR[0]) * HEAD_DIM
        pieces = [*pieces, around]
    parts = len(pieces)
    operands = [*pieces, upstream, segment, factor]
    in_specs = [pl.BlockSpec(memory_space=pltpu.VMEM)] * parts + [
        pl.BlockSpec((1, length, step), lambda i: (0, 0, place)),
        pl.BlockSpec((1, length), lambda i: (0, 0)),
        pl.BlockSpec(memory_space=pltpu.SMEM),
    ]
    out_specs = [pl.BlockSpec((3, 1, length, step), lambda i: (0, 0, 0, place))]
    out_shape = [jax.ShapeDtypeStruct((3, 1, length, width), jnp.bfloat16)]
    if carried is not None:
        whole = pl.BlockSpec(carried.shape, lambda i: (0, 0, 0))
        operands.append(carried)
        in_specs.append(whole)
        out_specs.append(whole)
        out_shape.append(jax.ShapeDtypeStruct(carried.shape, carried.dtype))
    aliases = {}
    if earlier is not None:
        aliases = {len(operands): 0}
        operands.append(earlier)
        in_specs.append(pl.BlockSpec(memory_space=pl.ANY))
    return pl.pallas_call(
        functools.partial(backward_kernel, parts, around_from, carried is not None),
        grid=(1,),
        in_specs=in_specs,
        out_specs=out_specs,
        out_shape=out_shape,
        scratch_shapes=[pltpu.VMEM((3, length, step), jnp.bfloat16)],
        input_output_aliases=aliases,
        compiler_params=pltpu.CompilerParams(vmem_limit_bytes=32 * 1024 * 1024),
        cost_estimate=pl.CostEstimate(
            flops=10 * length * length * step,
            bytes_accessed=14 * length * step,
            transcendentals=length * length * step // HEAD_DIM,
        ),
    )(*operands)


def fetched(piece, k, leg="direct"):
    sections, tensors = lax.axis_size("pipe"), lax.axis_size("tensor")
    pairs = []
    for p in range(sections):
        for t in range(tensors):
            start, end = p, sections - 1 - p
            if leg == "aside":
                end = p ^ 1
            if leg == "onward":
                start = p ^ 1
            if leg == "all" or (leg == "direct") != detoured(p):
                pairs.append((start * tensors + t, end * tensors + (t ^ k)))
    return lax.ppermute(piece, AXES, pairs)


def detoured(section):
    half = lax.axis_size("pipe") // 2
    place = section % half
    return (place == 2) | (place == half - 3)


def shifted(array, by):
    sections = lax.axis_size("pipe")
    with jax.named_scope("direct_out" if by > 0 else "direct_grad"):
        return lax.ppermute(array, "pipe", [(p, (p + by) % sections) for p in range(sections)])


def on_device(fwd_qkv, fwd_segments, parked, bwd_segments, grad_out, loss_tokens):
    length, width = grad_out.shape[1:]
    tensors = lax.axis_size("tensor")
    mine = lax.axis_index("tensor")

    def cut(whole, k, first, heads):
        start = (mine ^ k) * width + first * HEAD_DIM
        return lax.dynamic_slice_in_dim(whole, start, heads * HEAD_DIM, axis=3)

    def fetched_chunk(whole, chunk):
        first, heads = CHUNKS[chunk]
        pieces = []
        for k in range(tensors):
            goes_around = k == 0 and DETOUR[0] <= first and first + heads <= sum(DETOUR)
            with jax.named_scope(f"stash_{k}_{chunk}"):
                piece = cut(whole, k, first, heads)
                pieces.append(fetched(piece, k, "direct" if goes_around else "all"))
        return pieces

    upstream = shifted(grad_out, -1)
    with jax.named_scope("aside_0"):
        around = fetched(cut(parked, 0, *DETOUR), 0, "aside")
    with jax.named_scope("onward_0"):
        around = fetched(around, 0, "onward")
    pieces = [fetched_chunk(parked, 0)]
    with jax.named_scope("forward_heads"):
        forward_out = forward(fwd_qkv, fwd_segments)
    received = shifted(forward_out, 1)
    tokens = loss_tokens.astype(jnp.float32)
    pieces[0][0], tokens = lax.optimization_barrier((pieces[0][0], tokens))
    token_total = lax.psum(tokens, "dp")
    factor = jnp.float32(lax.axis_size("dp") * length) / token_total
    parked, token_total = lax.optimization_barrier((parked, token_total))
    pieces.append(fetched_chunk(parked, 1))
    (grads,) = backward(0, pieces[0], around, upstream, bwd_segments, factor, None)
    parked, grads = lax.optimization_barrier((parked, grads))
    pieces.append(fetched_chunk(parked, 2))
    grads, received = backward(
        1, pieces[1], around, upstream, bwd_segments, factor, grads, received
    )
    (grads,) = backward(2, pieces[2], around, upstream, bwd_segments, factor, grads)
    return (received, grads)


def solution(mesh):
    placed = (
        P(None, ("pipe", "dp"), None, "tensor"),
        P(("pipe", "dp"), None),
        P(None, ("pipe", "dp"), "tensor", None),
        P(("pipe", "dp"), None),
        P(("pipe", "dp"), None, "tensor"),
        P(("pipe", "dp")),
    )
    return jax.shard_map(
        on_device,
        mesh=mesh,
        in_specs=placed,
        out_specs=(P(("pipe", "dp"), None, "tensor"), P(None, ("pipe", "dp"), None, "tensor")),
        check_vma=False,
    )
```

```python
import functools
import math

import jax
import jax.numpy as jnp
from jax import lax
from jax.experimental import pallas as pl
from jax.experimental.pallas import tpu as pltpu
from jax.sharding import PartitionSpec as P

HEAD_DIM = 128
FORWARD_STEPS = 2
CHUNKS = ((0, 8), (8, 4), (12, 4))
DETOUR = (0, 8)
SCALE = HEAD_DIM ** (-0.5)
EXPONENT = SCALE * math.log2(math.e)
NT = (((1,), (1,)), ((), ()))
NN = (((1,), (0,)), ((), ()))
TN = (((0,), (0,)), ((), ()))
AXES = ("pipe", "tensor")


def product(left, right, dims):
    return lax.dot_general(left, right, dims, preferred_element_type=jnp.float32)


def probabilities(queries, keys, outside):
    logits = product(keys, queries, NT) + outside
    highest = jnp.max(logits, axis=0, keepdims=True)
    weights = jnp.exp2((logits - highest) * EXPONENT)
    return weights * (1.0 / jnp.sum(weights, axis=0, keepdims=True))


def outside_of(segment_ref):
    length = segment_ref.shape[1]
    across = jnp.broadcast_to(segment_ref[...].astype(jnp.float32), (length, length))
    return jnp.where(across == across.T, 0.0, -1e31).astype(jnp.float32)


def forward_kernel(qkv_ref, segment_ref, out_ref, outside):
    @pl.when(pl.program_id(0) == 0)
    def _():
        outside[...] = outside_of(segment_ref)

    for start in range(0, out_ref.shape[2], HEAD_DIM):
        head = slice(start, start + HEAD_DIM)
        probs = probabilities(qkv_ref[0, 0, :, head], qkv_ref[1, 0, :, head], outside[...])
        mixed = product(probs.astype(jnp.bfloat16), qkv_ref[2, 0, :, head], TN)
        out_ref[0, :, head] = mixed.astype(jnp.bfloat16)


def forward(qkv, segment):
    _, _, length, width = qkv.shape
    step = width // FORWARD_STEPS
    return pl.pallas_call(
        forward_kernel,
        grid=(FORWARD_STEPS,),
        in_specs=[
            pl.BlockSpec((3, 1, length, step), lambda c: (0, 0, 0, c)),
            pl.BlockSpec((1, length), lambda c: (0, 0)),
        ],
        out_specs=pl.BlockSpec((1, length, step), lambda c: (0, 0, c)),
        out_shape=jax.ShapeDtypeStruct((1, length, width), jnp.bfloat16),
        scratch_shapes=[pltpu.VMEM((length, length), jnp.float32)],
        compiler_params=pltpu.CompilerParams(vmem_limit_bytes=56 * 1024 * 1024),
        cost_estimate=pl.CostEstimate(
            flops=4 * length * length * width,
            bytes_accessed=8 * length * width,
            transcendentals=length * length * width // HEAD_DIM,
        ),
    )(qkv, segment)


def backward_kernel(parts, around_from, carries, *refs):
    pieces, refs = refs[:parts], refs[parts:]
    upstream_ref, segment_ref, factor_ref = refs[:3]
    out_ref, stash = refs[-2:]
    if carries:
        out_ref = refs[-3]
        refs[-2][...] = refs[3][...]
    mine = lax.axis_index("tensor")
    rows = pieces[0].shape[2]
    if around_from is not None:
        columns = slice(around_from, around_from + pieces[0].shape[3])
        around = pieces[-1][:, 0, :, columns]
        pieces = pieces[:-1]
    found = [piece[:, 0] for piece in pieces]
    if around_from is not None:
        found[0] = jnp.where(detoured(lax.axis_index("pipe")), around, found[0])
    for k, piece in enumerate(found):
        start = pl.multiple_of((mine ^ k) * rows, rows)
        stash[:, pl.ds(start, rows), :] = piece
    outside = outside_of(segment_ref)
    factor = factor_ref[0]
    for start in range(0, upstream_ref.shape[2], HEAD_DIM):
        head = slice(start, start + HEAD_DIM)
        queries, keys, values = stash[0, :, head], stash[1, :, head], stash[2, :, head]
        upstream = upstream_ref[0, :, head]
        probs = probabilities(queries, keys, outside)
        grad_value = product(probs.astype(jnp.bfloat16), upstream, NN)
        grad_probs = product(values, upstream, NT)
        center = jnp.sum(probs * grad_probs, axis=0, keepdims=True)
        grad_logits = (probs * ((grad_probs - center) * SCALE)).astype(jnp.bfloat16)
        out_ref[0, 0, :, head] = (product(grad_logits, keys, TN) * factor).astype(jnp.bfloat16)
        out_ref[1, 0, :, head] = (product(grad_logits, queries, NN) * factor).astype(jnp.bfloat16)
        out_ref[2, 0, :, head] = (grad_value * factor).astype(jnp.bfloat16)


def backward(chunk, pieces, around, upstream, segment, factor, earlier, carried=None):
    _, length, width = upstream.shape
    first, heads = CHUNKS[chunk]
    step = heads * HEAD_DIM
    place = first // heads
    around_from = None
    if DETOUR[0] <= first and first + heads <= sum(DETOUR):
        around_from = (first - DETOUR[0]) * HEAD_DIM
        pieces = [*pieces, around]
    parts = len(pieces)
    operands = [*pieces, upstream, segment, factor]
    in_specs = [pl.BlockSpec(memory_space=pltpu.VMEM)] * parts + [
        pl.BlockSpec((1, length, step), lambda i: (0, 0, place)),
        pl.BlockSpec((1, length), lambda i: (0, 0)),
        pl.BlockSpec(memory_space=pltpu.SMEM),
    ]
    out_specs = [pl.BlockSpec((3, 1, length, step), lambda i: (0, 0, 0, place))]
    out_shape = [jax.ShapeDtypeStruct((3, 1, length, width), jnp.bfloat16)]
    if carried is not None:
        whole = pl.BlockSpec(carried.shape, lambda i: (0, 0, 0))
        operands.append(carried)
        in_specs.append(whole)
        out_specs.append(whole)
        out_shape.append(jax.ShapeDtypeStruct(carried.shape, carried.dtype))
    aliases = {}
    if earlier is not None:
        aliases = {len(operands): 0}
        operands.append(earlier)
        in_specs.append(pl.BlockSpec(memory_space=pl.ANY))
    return pl.pallas_call(
        functools.partial(backward_kernel, parts, around_from, carried is not None),
        grid=(1,),
        in_specs=in_specs,
        out_specs=out_specs,
        out_shape=out_shape,
        scratch_shapes=[pltpu.VMEM((3, length, step), jnp.bfloat16)],
        input_output_aliases=aliases,
        compiler_params=pltpu.CompilerParams(vmem_limit_bytes=32 * 1024 * 1024),
        cost_estimate=pl.CostEstimate(
            flops=10 * length * length * step,
            bytes_accessed=14 * length * step,
            transcendentals=length * length * step // HEAD_DIM,
        ),
    )(*operands)


def fetched(piece, k, leg="direct"):
    sections, tensors = lax.axis_size("pipe"), lax.axis_size("tensor")
    pairs = []
    for p in range(sections):
        for t in range(tensors):
            start, end = p, sections - 1 - p
            if leg == "aside":
                end = p ^ 1
            if leg == "onward":
                start = p ^ 1
            if leg == "all" or (leg == "direct") != detoured(p):
                pairs.append((start * tensors + t, end * tensors + (t ^ k)))
    return lax.ppermute(piece, AXES, pairs)


def detoured(section):
    half = lax.axis_size("pipe") // 2
    place = section % half
    return (place == 2) | (place == half - 3)


def shifted(array, by):
    sections = lax.axis_size("pipe")
    with jax.named_scope("direct_out" if by > 0 else "direct_grad"):
        return lax.ppermute(array, "pipe", [(p, (p + by) % sections) for p in range(sections)])


def on_device(fwd_qkv, fwd_segments, parked, bwd_segments, grad_out, loss_tokens):
    length, width = grad_out.shape[1:]
    tensors = lax.axis_size("tensor")
    mine = lax.axis_index("tensor")

    def cut(whole, k, first, heads):
        start = (mine ^ k) * width + first * HEAD_DIM
        return lax.dynamic_slice_in_dim(whole, start, heads * HEAD_DIM, axis=3)

    def fetched_chunk(whole, chunk):
        first, heads = CHUNKS[chunk]
        pieces = []
        for k in range(tensors):
            goes_around = k == 0 and DETOUR[0] <= first and first + heads <= sum(DETOUR)
            with jax.named_scope(f"stash_{k}_{chunk}"):
                piece = cut(whole, k, first, heads)
                pieces.append(fetched(piece, k, "direct" if goes_around else "all"))
        return pieces

    upstream = shifted(grad_out, -1)
    with jax.named_scope("aside_0"):
        around = fetched(cut(parked, 0, *DETOUR), 0, "aside")
    with jax.named_scope("onward_0"):
        around = fetched(around, 0, "onward")
    pieces = [fetched_chunk(parked, 0)]
    with jax.named_scope("forward_heads"):
        forward_out = forward(fwd_qkv, fwd_segments)
    received = shifted(forward_out, 1)
    tokens = loss_tokens.astype(jnp.float32)
    pieces[0][3], tokens = lax.optimization_barrier((pieces[0][3], tokens))
    token_total = lax.psum(tokens, "dp")
    factor = jnp.float32(lax.axis_size("dp") * length) / token_total
    parked, token_total = lax.optimization_barrier((parked, token_total))
    pieces.append(fetched_chunk(parked, 1))
    (grads,) = backward(0, pieces[0], around, upstream, bwd_segments, factor, None)
    parked, grads = lax.optimization_barrier((parked, grads))
    pieces.append(fetched_chunk(parked, 2))
    grads, received = backward(
        1, pieces[1], around, upstream, bwd_segments, factor, grads, received
    )
    (grads,) = backward(2, pieces[2], around, upstream, bwd_segments, factor, grads)
    return (received, grads)


def solution(mesh):
    placed = (
        P(None, ("pipe", "dp"), None, "tensor"),
        P(("pipe", "dp"), None),
        P(None, ("pipe", "dp"), "tensor", None),
        P(("pipe", "dp"), None),
        P(("pipe", "dp"), None, "tensor"),
        P(("pipe", "dp")),
    )
    return jax.shard_map(
        on_device,
        mesh=mesh,
        in_specs=placed,
        out_specs=(P(("pipe", "dp"), None, "tensor"), P(None, ("pipe", "dp"), None, "tensor")),
        check_vma=False,
    )
```

```python
import functools
import math

import jax
import jax.numpy as jnp
from jax import lax
from jax.experimental import pallas as pl
from jax.experimental.pallas import tpu as pltpu
from jax.sharding import PartitionSpec as P

HEAD_DIM = 128
FORWARD_STEPS = 2
CHUNKS = ((0, 10), (12, 4), (10, 2))
DETOUR = (0, 10)
SCALE = HEAD_DIM ** (-0.5)
EXPONENT = SCALE * math.log2(math.e)
NT = (((1,), (1,)), ((), ()))
NN = (((1,), (0,)), ((), ()))
TN = (((0,), (0,)), ((), ()))
AXES = ("pipe", "tensor")


def product(left, right, dims):
    return lax.dot_general(left, right, dims, preferred_element_type=jnp.float32)


def probabilities(queries, keys, outside):
    logits = product(keys, queries, NT) + outside
    highest = jnp.max(logits, axis=0, keepdims=True)
    weights = jnp.exp2((logits - highest) * EXPONENT)
    return weights * (1.0 / jnp.sum(weights, axis=0, keepdims=True))


def outside_of(segment_ref):
    length = segment_ref.shape[1]
    across = jnp.broadcast_to(segment_ref[...].astype(jnp.float32), (length, length))
    return jnp.where(across == across.T, 0.0, -1e31).astype(jnp.float32)


def forward_kernel(qkv_ref, segment_ref, out_ref, outside):
    @pl.when(pl.program_id(0) == 0)
    def _():
        outside[...] = outside_of(segment_ref)

    for start in range(0, out_ref.shape[2], HEAD_DIM):
        head = slice(start, start + HEAD_DIM)
        probs = probabilities(qkv_ref[0, 0, :, head], qkv_ref[1, 0, :, head], outside[...])
        mixed = product(probs.astype(jnp.bfloat16), qkv_ref[2, 0, :, head], TN)
        out_ref[0, :, head] = mixed.astype(jnp.bfloat16)


def forward(qkv, segment):
    _, _, length, width = qkv.shape
    step = width // FORWARD_STEPS
    return pl.pallas_call(
        forward_kernel,
        grid=(FORWARD_STEPS,),
        in_specs=[
            pl.BlockSpec((3, 1, length, step), lambda c: (0, 0, 0, c)),
            pl.BlockSpec((1, length), lambda c: (0, 0)),
        ],
        out_specs=pl.BlockSpec((1, length, step), lambda c: (0, 0, c)),
        out_shape=jax.ShapeDtypeStruct((1, length, width), jnp.bfloat16),
        scratch_shapes=[pltpu.VMEM((length, length), jnp.float32)],
        compiler_params=pltpu.CompilerParams(vmem_limit_bytes=56 * 1024 * 1024),
        cost_estimate=pl.CostEstimate(
            flops=4 * length * length * width,
            bytes_accessed=8 * length * width,
            transcendentals=length * length * width // HEAD_DIM,
        ),
    )(qkv, segment)


def backward_kernel(parts, around_from, carries, *refs):
    pieces, refs = refs[:parts], refs[parts:]
    upstream_ref, segment_ref, factor_ref = refs[:3]
    out_ref, stash = refs[-2:]
    if carries:
        out_ref = refs[-3]
        refs[-2][...] = refs[3][...]
    mine = lax.axis_index("tensor")
    rows = pieces[0].shape[2]
    if around_from is not None:
        columns = slice(around_from, around_from + pieces[0].shape[3])
        around = pieces[-1][:, 0, :, columns]
        pieces = pieces[:-1]
    found = [piece[:, 0] for piece in pieces]
    if around_from is not None:
        found[0] = jnp.where(detoured(lax.axis_index("pipe")), around, found[0])
    for k, piece in enumerate(found):
        start = pl.multiple_of((mine ^ k) * rows, rows)
        stash[:, pl.ds(start, rows), :] = piece
    outside = outside_of(segment_ref)
    factor = factor_ref[0]
    for start in range(0, upstream_ref.shape[2], HEAD_DIM):
        head = slice(start, start + HEAD_DIM)
        queries, keys, values = stash[0, :, head], stash[1, :, head], stash[2, :, head]
        upstream = upstream_ref[0, :, head]
        probs = probabilities(queries, keys, outside)
        grad_value = product(probs.astype(jnp.bfloat16), upstream, NN)
        grad_probs = product(values, upstream, NT)
        center = jnp.sum(probs * grad_probs, axis=0, keepdims=True)
        grad_logits = (probs * ((grad_probs - center) * SCALE)).astype(jnp.bfloat16)
        out_ref[0, 0, :, head] = (product(grad_logits, keys, TN) * factor).astype(jnp.bfloat16)
        out_ref[1, 0, :, head] = (product(grad_logits, queries, NN) * factor).astype(jnp.bfloat16)
        out_ref[2, 0, :, head] = (grad_value * factor).astype(jnp.bfloat16)


def backward(chunk, pieces, around, upstream, segment, factor, earlier, carried=None):
    _, length, width = upstream.shape
    first, heads = CHUNKS[chunk]
    step = heads * HEAD_DIM
    place = first // heads
    around_from = None
    if DETOUR[0] <= first and first + heads <= sum(DETOUR):
        around_from = (first - DETOUR[0]) * HEAD_DIM
        pieces = [*pieces, around]
    parts = len(pieces)
    operands = [*pieces, upstream, segment, factor]
    in_specs = [pl.BlockSpec(memory_space=pltpu.VMEM)] * parts + [
        pl.BlockSpec((1, length, step), lambda i: (0, 0, place)),
        pl.BlockSpec((1, length), lambda i: (0, 0)),
        pl.BlockSpec(memory_space=pltpu.SMEM),
    ]
    out_specs = [pl.BlockSpec((3, 1, length, step), lambda i: (0, 0, 0, place))]
    out_shape = [jax.ShapeDtypeStruct((3, 1, length, width), jnp.bfloat16)]
    if carried is not None:
        whole = pl.BlockSpec(carried.shape, lambda i: (0, 0, 0))
        operands.append(carried)
        in_specs.append(whole)
        out_specs.append(whole)
        out_shape.append(jax.ShapeDtypeStruct(carried.shape, carried.dtype))
    aliases = {}
    if earlier is not None:
        aliases = {len(operands): 0}
        operands.append(earlier)
        in_specs.append(pl.BlockSpec(memory_space=pl.ANY))
    return pl.pallas_call(
        functools.partial(backward_kernel, parts, around_from, carried is not None),
        grid=(1,),
        in_specs=in_specs,
        out_specs=out_specs,
        out_shape=out_shape,
        scratch_shapes=[pltpu.VMEM((3, length, step), jnp.bfloat16)],
        input_output_aliases=aliases,
        compiler_params=pltpu.CompilerParams(vmem_limit_bytes=32 * 1024 * 1024),
        cost_estimate=pl.CostEstimate(
            flops=10 * length * length * step,
            bytes_accessed=14 * length * step,
            transcendentals=length * length * step // HEAD_DIM,
        ),
    )(*operands)


def fetched(piece, k, leg="direct"):
    sections, tensors = lax.axis_size("pipe"), lax.axis_size("tensor")
    pairs = []
    for p in range(sections):
        for t in range(tensors):
            start, end = p, sections - 1 - p
            if leg == "aside":
                end = p ^ 1
            if leg == "onward":
                start = p ^ 1
            if leg == "all" or (leg == "direct") != detoured(p):
                pairs.append((start * tensors + t, end * tensors + (t ^ k)))
    return lax.ppermute(piece, AXES, pairs)


def detoured(section):
    half = lax.axis_size("pipe") // 2
    place = section % half
    return (place == 2) | (place == half - 3)


def shifted(array, by):
    sections = lax.axis_size("pipe")
    with jax.named_scope("direct_out" if by > 0 else "direct_grad"):
        return lax.ppermute(array, "pipe", [(p, (p + by) % sections) for p in range(sections)])


def on_device(fwd_qkv, fwd_segments, parked, bwd_segments, grad_out, loss_tokens):
    length, width = grad_out.shape[1:]
    tensors = lax.axis_size("tensor")
    mine = lax.axis_index("tensor")

    def cut(whole, k, first, heads):
        start = (mine ^ k) * width + first * HEAD_DIM
        return lax.dynamic_slice_in_dim(whole, start, heads * HEAD_DIM, axis=3)

    def fetched_chunk(whole, chunk):
        first, heads = CHUNKS[chunk]
        pieces = []
        for k in range(tensors):
            goes_around = k == 0 and DETOUR[0] <= first and first + heads <= sum(DETOUR)
            with jax.named_scope(f"stash_{k}_{chunk}"):
                piece = cut(whole, k, first, heads)
                pieces.append(fetched(piece, k, "direct" if goes_around else "all"))
        return pieces

    upstream = shifted(grad_out, -1)
    with jax.named_scope("aside_0"):
        around = fetched(cut(parked, 0, *DETOUR), 0, "aside")
    with jax.named_scope("onward_0"):
        around = fetched(around, 0, "onward")
    pieces = [fetched_chunk(parked, 0)]
    with jax.named_scope("forward_heads"):
        forward_out = forward(fwd_qkv, fwd_segments)
    received = shifted(forward_out, 1)
    tokens = loss_tokens.astype(jnp.float32)
    pieces[0][3], tokens = lax.optimization_barrier((pieces[0][3], tokens))
    token_total = lax.psum(tokens, "dp")
    factor = jnp.float32(lax.axis_size("dp") * length) / token_total
    parked, token_total = lax.optimization_barrier((parked, token_total))
    pieces.append(fetched_chunk(parked, 1))
    (grads,) = backward(0, pieces[0], around, upstream, bwd_segments, factor, None)
    parked, grads = lax.optimization_barrier((parked, grads))
    pieces.append(fetched_chunk(parked, 2))
    grads, received = backward(
        1, pieces[1], around, upstream, bwd_segments, factor, grads, received
    )
    (grads,) = backward(2, pieces[2], around, upstream, bwd_segments, factor, grads)
    return (received, grads)


def solution(mesh):
    placed = (
        P(None, ("pipe", "dp"), None, "tensor"),
        P(("pipe", "dp"), None),
        P(None, ("pipe", "dp"), "tensor", None),
        P(("pipe", "dp"), None),
        P(("pipe", "dp"), None, "tensor"),
        P(("pipe", "dp")),
    )
    return jax.shard_map(
        on_device,
        mesh=mesh,
        in_specs=placed,
        out_specs=(P(("pipe", "dp"), None, "tensor"), P(None, ("pipe", "dp"), None, "tensor")),
        check_vma=False,
    )
```

```python
import functools
import math

import jax
import jax.numpy as jnp
from jax import lax
from jax.experimental import pallas as pl
from jax.experimental.pallas import tpu as pltpu
from jax.sharding import PartitionSpec as P

HEAD_DIM = 128
FORWARD_STEPS = 2
CHUNKS = ((0, 10), (12, 4), (10, 2))
DETOUR = (0, 10)
SCALE = HEAD_DIM ** (-0.5)
EXPONENT = SCALE * math.log2(math.e)
NT = (((1,), (1,)), ((), ()))
NN = (((1,), (0,)), ((), ()))
TN = (((0,), (0,)), ((), ()))
AXES = ("pipe", "tensor")


def product(left, right, dims):
    return lax.dot_general(left, right, dims, preferred_element_type=jnp.float32)


def probabilities(queries, keys, outside):
    logits = product(keys, queries, NT) + outside
    highest = jnp.max(logits, axis=0, keepdims=True)
    weights = jnp.exp2((logits - highest) * EXPONENT)
    return weights * (1.0 / jnp.sum(weights, axis=0, keepdims=True))


def outside_of(segment_ref):
    length = segment_ref.shape[1]
    across = jnp.broadcast_to(segment_ref[...].astype(jnp.float32), (length, length))
    return jnp.where(across == across.T, 0.0, -1e31).astype(jnp.float32)


def forward_kernel(qkv_ref, segment_ref, out_ref, outside):
    @pl.when(pl.program_id(0) == 0)
    def _():
        outside[...] = outside_of(segment_ref)

    for start in range(0, out_ref.shape[2], HEAD_DIM):
        head = slice(start, start + HEAD_DIM)
        probs = probabilities(qkv_ref[0, 0, :, head], qkv_ref[1, 0, :, head], outside[...])
        mixed = product(probs.astype(jnp.bfloat16), qkv_ref[2, 0, :, head], TN)
        out_ref[0, :, head] = mixed.astype(jnp.bfloat16)


def forward(qkv, segment):
    _, _, length, width = qkv.shape
    step = width // FORWARD_STEPS
    return pl.pallas_call(
        forward_kernel,
        grid=(FORWARD_STEPS,),
        in_specs=[
            pl.BlockSpec((3, 1, length, step), lambda c: (0, 0, 0, c)),
            pl.BlockSpec((1, length), lambda c: (0, 0)),
        ],
        out_specs=pl.BlockSpec((1, length, step), lambda c: (0, 0, c)),
        out_shape=jax.ShapeDtypeStruct((1, length, width), jnp.bfloat16),
        scratch_shapes=[pltpu.VMEM((length, length), jnp.float32)],
        compiler_params=pltpu.CompilerParams(vmem_limit_bytes=56 * 1024 * 1024),
        cost_estimate=pl.CostEstimate(
            flops=4 * length * length * width,
            bytes_accessed=8 * length * width,
            transcendentals=length * length * width // HEAD_DIM,
        ),
    )(qkv, segment)


def backward_kernel(parts, around_from, carries, *refs):
    pieces, refs = refs[:parts], refs[parts:]
    upstream_ref, segment_ref, factor_ref = refs[:3]
    out_ref, stash = refs[-2:]
    if carries:
        out_ref = refs[-3]
        refs[-2][...] = refs[3][...]
    mine = lax.axis_index("tensor")
    rows = pieces[0].shape[2]
    if around_from is not None:
        columns = slice(around_from, around_from + pieces[0].shape[3])
        around = pieces[-1][:, 0, :, columns]
        pieces = pieces[:-1]
    found = [piece[:, 0] for piece in pieces]
    if around_from is not None:
        found[0] = jnp.where(detoured(lax.axis_index("pipe")), around, found[0])
    for k, piece in enumerate(found):
        start = pl.multiple_of((mine ^ k) * rows, rows)
        stash[:, pl.ds(start, rows), :] = piece
    outside = outside_of(segment_ref)
    factor = factor_ref[0]
    for start in range(0, upstream_ref.shape[2], HEAD_DIM):
        head = slice(start, start + HEAD_DIM)
        queries, keys, values = stash[0, :, head], stash[1, :, head], stash[2, :, head]
        upstream = upstream_ref[0, :, head]
        probs = probabilities(queries, keys, outside)
        grad_value = product(probs.astype(jnp.bfloat16), upstream, NN)
        grad_probs = product(values, upstream, NT)
        center = jnp.sum(probs * grad_probs, axis=0, keepdims=True)
        grad_logits = (probs * ((grad_probs - center) * SCALE)).astype(jnp.bfloat16)
        out_ref[0, 0, :, head] = (product(grad_logits, keys, TN) * factor).astype(jnp.bfloat16)
        out_ref[1, 0, :, head] = (product(grad_logits, queries, NN) * factor).astype(jnp.bfloat16)
        out_ref[2, 0, :, head] = (grad_value * factor).astype(jnp.bfloat16)


def backward(chunk, pieces, around, upstream, segment, factor, earlier, carried=None):
    _, length, width = upstream.shape
    first, heads = CHUNKS[chunk]
    step = heads * HEAD_DIM
    place = first // heads
    around_from = None
    if DETOUR[0] <= first and first + heads <= sum(DETOUR):
        around_from = (first - DETOUR[0]) * HEAD_DIM
        pieces = [*pieces, around]
    parts = len(pieces)
    operands = [*pieces, upstream, segment, factor]
    in_specs = [pl.BlockSpec(memory_space=pltpu.VMEM)] * parts + [
        pl.BlockSpec((1, length, step), lambda i: (0, 0, place)),
        pl.BlockSpec((1, length), lambda i: (0, 0)),
        pl.BlockSpec(memory_space=pltpu.SMEM),
    ]
    out_specs = [pl.BlockSpec((3, 1, length, step), lambda i: (0, 0, 0, place))]
    out_shape = [jax.ShapeDtypeStruct((3, 1, length, width), jnp.bfloat16)]
    if carried is not None:
        whole = pl.BlockSpec(carried.shape, lambda i: (0, 0, 0))
        operands.append(carried)
        in_specs.append(whole)
        out_specs.append(whole)
        out_shape.append(jax.ShapeDtypeStruct(carried.shape, carried.dtype))
    aliases = {}
    if earlier is not None:
        aliases = {len(operands): 0}
        operands.append(earlier)
        in_specs.append(pl.BlockSpec(memory_space=pl.ANY))
    return pl.pallas_call(
        functools.partial(backward_kernel, parts, around_from, carried is not None),
        grid=(1,),
        in_specs=in_specs,
        out_specs=out_specs,
        out_shape=out_shape,
        scratch_shapes=[pltpu.VMEM((3, length, step), jnp.bfloat16)],
        input_output_aliases=aliases,
        compiler_params=pltpu.CompilerParams(vmem_limit_bytes=32 * 1024 * 1024),
        cost_estimate=pl.CostEstimate(
            flops=10 * length * length * step,
            bytes_accessed=14 * length * step,
            transcendentals=length * length * step // HEAD_DIM,
        ),
    )(*operands)


def fetched(piece, k, leg="direct"):
    sections, tensors = lax.axis_size("pipe"), lax.axis_size("tensor")
    pairs = []
    for p in range(sections):
        for t in range(tensors):
            start, end = p, sections - 1 - p
            if leg == "aside":
                end = p ^ 1
            if leg == "onward":
                start = p ^ 1
            if leg == "all" or (leg == "direct") != detoured(p):
                pairs.append((start * tensors + t, end * tensors + (t ^ k)))
    return lax.ppermute(piece, AXES, pairs)


def detoured(section):
    half = lax.axis_size("pipe") // 2
    place = section % half
    return (place == 2) | (place == half - 3)


def shifted(array, by):
    sections = lax.axis_size("pipe")
    with jax.named_scope("direct_out" if by > 0 else "direct_grad"):
        return lax.ppermute(array, "pipe", [(p, (p + by) % sections) for p in range(sections)])


def on_device(fwd_qkv, fwd_segments, parked, bwd_segments, grad_out, loss_tokens):
    length, width = grad_out.shape[1:]
    tensors = lax.axis_size("tensor")
    mine = lax.axis_index("tensor")

    def cut(whole, k, first, heads):
        start = (mine ^ k) * width + first * HEAD_DIM
        return lax.dynamic_slice_in_dim(whole, start, heads * HEAD_DIM, axis=3)

    def fetched_chunk(whole, chunk, partners):
        first, heads = CHUNKS[chunk]
        pieces = []
        for k in partners:
            goes_around = k == 0 and DETOUR[0] <= first and first + heads <= sum(DETOUR)
            with jax.named_scope(f"stash_{k}_{chunk}"):
                piece = cut(whole, k, first, heads)
                pieces.append(fetched(piece, k, "direct" if goes_around else "all"))
        return pieces

    upstream = shifted(grad_out, -1)
    leading = cut(parked, 3, *CHUNKS[0])
    leading, parked = lax.optimization_barrier((leading, parked))
    with jax.named_scope("stash_3_0"):
        leading = fetched(leading, 3, "all")
    with jax.named_scope("aside_0"):
        around = fetched(cut(parked, 0, *DETOUR), 0, "aside")
    with jax.named_scope("onward_0"):
        around = fetched(around, 0, "onward")
    pieces = [[*fetched_chunk(parked, 0, range(3)), leading]]
    with jax.named_scope("forward_heads"):
        forward_out = forward(fwd_qkv, fwd_segments)
    received = shifted(forward_out, 1)
    tokens = loss_tokens.astype(jnp.float32)
    pieces[0][3], tokens = lax.optimization_barrier((pieces[0][3], tokens))
    token_total = lax.psum(tokens, "dp")
    factor = jnp.float32(lax.axis_size("dp") * length) / token_total
    parked, token_total = lax.optimization_barrier((parked, token_total))
    pieces.append(fetched_chunk(parked, 1, range(tensors)))
    (grads,) = backward(0, pieces[0], around, upstream, bwd_segments, factor, None)
    parked, grads = lax.optimization_barrier((parked, grads))
    pieces.append(fetched_chunk(parked, 2, range(tensors)))
    grads, received = backward(
        1, pieces[1], around, upstream, bwd_segments, factor, grads, received
    )
    (grads,) = backward(2, pieces[2], around, upstream, bwd_segments, factor, grads)
    return (received, grads)


def solution(mesh):
    placed = (
        P(None, ("pipe", "dp"), None, "tensor"),
        P(("pipe", "dp"), None),
        P(None, ("pipe", "dp"), "tensor", None),
        P(("pipe", "dp"), None),
        P(("pipe", "dp"), None, "tensor"),
        P(("pipe", "dp")),
    )
    return jax.shard_map(
        on_device,
        mesh=mesh,
        in_specs=placed,
        out_specs=(P(("pipe", "dp"), None, "tensor"), P(None, ("pipe", "dp"), None, "tensor")),
        check_vma=False,
    )
```

```python
import functools
import math

import jax
import jax.numpy as jnp
from jax import lax
from jax.experimental import pallas as pl
from jax.experimental.pallas import tpu as pltpu
from jax.sharding import PartitionSpec as P

HEAD_DIM = 128
FORWARD_STEPS = 2
CHUNKS = ((0, 10), (12, 4), (10, 2))
SCALE = HEAD_DIM ** (-0.5)
EXPONENT = SCALE * math.log2(math.e)
NT = (((1,), (1,)), ((), ()))
NN = (((1,), (0,)), ((), ()))
TN = (((0,), (0,)), ((), ()))
AXES = ("pipe", "tensor")


def product(left, right, dims):
    return lax.dot_general(left, right, dims, preferred_element_type=jnp.float32)


def probabilities(queries, keys, outside):
    logits = product(keys, queries, NT) + outside
    highest = jnp.max(logits, axis=0, keepdims=True)
    weights = jnp.exp2((logits - highest) * EXPONENT)
    return weights * (1.0 / jnp.sum(weights, axis=0, keepdims=True))


def outside_of(segment_ref):
    length = segment_ref.shape[1]
    across = jnp.broadcast_to(segment_ref[...].astype(jnp.float32), (length, length))
    return jnp.where(across == across.T, 0.0, -1e31).astype(jnp.float32)


def forward_kernel(qkv_ref, segment_ref, out_ref, outside):
    @pl.when(pl.program_id(0) == 0)
    def _():
        outside[...] = outside_of(segment_ref)

    for start in range(0, out_ref.shape[2], HEAD_DIM):
        head = slice(start, start + HEAD_DIM)
        probs = probabilities(qkv_ref[0, 0, :, head], qkv_ref[1, 0, :, head], outside[...])
        mixed = product(probs.astype(jnp.bfloat16), qkv_ref[2, 0, :, head], TN)
        out_ref[0, :, head] = mixed.astype(jnp.bfloat16)


def forward(qkv, segment):
    _, _, length, width = qkv.shape
    step = width // FORWARD_STEPS
    return pl.pallas_call(
        forward_kernel,
        grid=(FORWARD_STEPS,),
        in_specs=[
            pl.BlockSpec((3, 1, length, step), lambda c: (0, 0, 0, c)),
            pl.BlockSpec((1, length), lambda c: (0, 0)),
        ],
        out_specs=pl.BlockSpec((1, length, step), lambda c: (0, 0, c)),
        out_shape=jax.ShapeDtypeStruct((1, length, width), jnp.bfloat16),
        scratch_shapes=[pltpu.VMEM((length, length), jnp.float32)],
        compiler_params=pltpu.CompilerParams(vmem_limit_bytes=56 * 1024 * 1024),
        cost_estimate=pl.CostEstimate(
            flops=4 * length * length * width,
            bytes_accessed=8 * length * width,
            transcendentals=length * length * width // HEAD_DIM,
        ),
    )(qkv, segment)


def backward_kernel(parts, carries, *refs):
    pieces, refs = refs[:parts], refs[parts:]
    upstream_ref, segment_ref, factor_ref = refs[:3]
    out_ref, stash = refs[-2:]
    if carries:
        out_ref = refs[-3]
        refs[-2][...] = refs[3][...]
    mine = lax.axis_index("tensor")
    rows = pieces[0].shape[2]
    found = [piece[:, 0] for piece in pieces]
    if parts > 4:
        found[0] = jnp.where(detoured(lax.axis_index("pipe")), found.pop(), found[0])
    for k, piece in enumerate(found):
        start = pl.multiple_of((mine ^ k) * rows, rows)
        stash[:, pl.ds(start, rows), :] = piece
    outside = outside_of(segment_ref)
    factor = factor_ref[0]
    for start in range(0, upstream_ref.shape[2], HEAD_DIM):
        head = slice(start, start + HEAD_DIM)
        queries, keys, values = stash[0, :, head], stash[1, :, head], stash[2, :, head]
        upstream = upstream_ref[0, :, head]
        probs = probabilities(queries, keys, outside)
        grad_value = product(probs.astype(jnp.bfloat16), upstream, NN)
        grad_probs = product(values, upstream, NT)
        center = jnp.sum(probs * grad_probs, axis=0, keepdims=True)
        grad_logits = (probs * ((grad_probs - center) * SCALE)).astype(jnp.bfloat16)
        out_ref[0, 0, :, head] = (product(grad_logits, keys, TN) * factor).astype(jnp.bfloat16)
        out_ref[1, 0, :, head] = (product(grad_logits, queries, NN) * factor).astype(jnp.bfloat16)
        out_ref[2, 0, :, head] = (grad_value * factor).astype(jnp.bfloat16)


def backward(chunk, pieces, around, upstream, segment, factor, earlier, carried=None):
    _, length, width = upstream.shape
    first, heads = CHUNKS[chunk]
    step = heads * HEAD_DIM
    place = first // heads
    if around is not None:
        pieces = [*pieces, around]
    parts = len(pieces)
    operands = [*pieces, upstream, segment, factor]
    in_specs = [pl.BlockSpec(memory_space=pltpu.VMEM)] * parts + [
        pl.BlockSpec((1, length, step), lambda i: (0, 0, place)),
        pl.BlockSpec((1, length), lambda i: (0, 0)),
        pl.BlockSpec(memory_space=pltpu.SMEM),
    ]
    out_specs = [pl.BlockSpec((3, 1, length, step), lambda i: (0, 0, 0, place))]
    out_shape = [jax.ShapeDtypeStruct((3, 1, length, width), jnp.bfloat16)]
    if carried is not None:
        whole = pl.BlockSpec(carried.shape, lambda i: (0, 0, 0))
        operands.append(carried)
        in_specs.append(whole)
        out_specs.append(whole)
        out_shape.append(jax.ShapeDtypeStruct(carried.shape, carried.dtype))
    aliases = {}
    if earlier is not None:
        aliases = {len(operands): 0}
        operands.append(earlier)
        in_specs.append(pl.BlockSpec(memory_space=pl.ANY))
    return pl.pallas_call(
        functools.partial(backward_kernel, parts, carried is not None),
        grid=(1,),
        in_specs=in_specs,
        out_specs=out_specs,
        out_shape=out_shape,
        scratch_shapes=[pltpu.VMEM((3, length, step), jnp.bfloat16)],
        input_output_aliases=aliases,
        compiler_params=pltpu.CompilerParams(vmem_limit_bytes=32 * 1024 * 1024),
        cost_estimate=pl.CostEstimate(
            flops=10 * length * length * step,
            bytes_accessed=14 * length * step,
            transcendentals=length * length * step // HEAD_DIM,
        ),
    )(*operands)


def cut_kernel(spans, whole_ref, *refs):
    outs, sems = refs[:-1], refs[-1]
    width = whole_ref.shape[3] // lax.axis_size("tensor")
    copies = []
    for i, (k, first, heads) in enumerate(spans):
        start = (lax.axis_index("tensor") ^ k) * width + first * HEAD_DIM
        columns = pl.ds(pl.multiple_of(start, HEAD_DIM), heads * HEAD_DIM)
        copies.append(pltpu.make_async_copy(whole_ref.at[:, :, :, columns], outs[i], sems.at[i]))
    for copy in copies:
        copy.start()
    for copy in copies:
        copy.wait()


def cut_by_copy(whole, spans):
    return pl.pallas_call(
        functools.partial(cut_kernel, spans),
        in_specs=[pl.BlockSpec(memory_space=pl.ANY)],
        out_specs=[pl.BlockSpec(memory_space=pl.ANY)] * len(spans),
        out_shape=[
            jax.ShapeDtypeStruct((*whole.shape[:3], heads * HEAD_DIM), whole.dtype)
            for _, _, heads in spans
        ],
        scratch_shapes=[pltpu.SemaphoreType.DMA((len(spans),))],
        compiler_params=pltpu.CompilerParams(vmem_limit_bytes=60 * 1024 * 1024),
    )(whole)


def fetched(piece, k, leg="direct"):
    sections, tensors = lax.axis_size("pipe"), lax.axis_size("tensor")
    pairs = []
    for p in range(sections):
        for t in range(tensors):
            start, end = p, sections - 1 - p
            if leg == "aside":
                end = p ^ 1
            if leg == "onward":
                start = p ^ 1
            if leg == "all" or (leg == "direct") != detoured(p):
                pairs.append((start * tensors + t, end * tensors + (t ^ k)))
    return lax.ppermute(piece, AXES, pairs)


def detoured(section):
    half = lax.axis_size("pipe") // 2
    place = section % half
    return (place == 2) | (place == half - 3)


def shifted(array, by):
    sections = lax.axis_size("pipe")
    with jax.named_scope("direct_out" if by > 0 else "direct_grad"):
        return lax.ppermute(array, "pipe", [(p, (p + by) % sections) for p in range(sections)])


def on_device(fwd_qkv, fwd_segments, parked, bwd_segments, grad_out, loss_tokens):
    length, width = grad_out.shape[1:]
    tensors = lax.axis_size("tensor")
    mine = lax.axis_index("tensor")

    def cut(whole, k, first, heads):
        start = (mine ^ k) * width + first * HEAD_DIM
        return lax.dynamic_slice_in_dim(whole, start, heads * HEAD_DIM, axis=3)

    def fetched_chunk(whole, chunk):
        first, heads = CHUNKS[chunk]
        pieces = []
        for k in range(tensors):
            with jax.named_scope(f"stash_{k}_{chunk}"):
                pieces.append(fetched(cut(whole, k, first, heads), k, "all"))
        return pieces

    upstream = shifted(grad_out, -1)
    (leading,) = cut_by_copy(parked, [(3, *CHUNKS[0])])
    leading, parked = lax.optimization_barrier((leading, parked))
    rest = cut_by_copy(parked, [(k, *CHUNKS[0]) for k in range(3)])
    with jax.named_scope("aside_0"):
        around = fetched(rest[0], 0, "aside")
    with jax.named_scope("onward_0"):
        around = fetched(around, 0, "onward")
    pieces = [[]]
    for k, piece in enumerate([*rest, leading]):
        with jax.named_scope(f"stash_{k}_0"):
            pieces[0].append(fetched(piece, k, "direct" if k == 0 else "all"))
    with jax.named_scope("forward_heads"):
        forward_out = forward(fwd_qkv, fwd_segments)
    received = shifted(forward_out, 1)
    tokens = loss_tokens.astype(jnp.float32)
    pieces[0][3], tokens = lax.optimization_barrier((pieces[0][3], tokens))
    token_total = lax.psum(tokens, "dp")
    factor = jnp.float32(lax.axis_size("dp") * length) / token_total
    parked, token_total = lax.optimization_barrier((parked, token_total))
    pieces.append(fetched_chunk(parked, 1))
    (grads,) = backward(0, pieces[0], around, upstream, bwd_segments, factor, None)
    parked, grads = lax.optimization_barrier((parked, grads))
    pieces.append(fetched_chunk(parked, 2))
    grads, received = backward(
        1, pieces[1], None, upstream, bwd_segments, factor, grads, received
    )
    (grads,) = backward(2, pieces[2], None, upstream, bwd_segments, factor, grads)
    return (received, grads)


def solution(mesh):
    placed = (
        P(None, ("pipe", "dp"), None, "tensor"),
        P(("pipe", "dp"), None),
        P(None, ("pipe", "dp"), "tensor", None),
        P(("pipe", "dp"), None),
        P(("pipe", "dp"), None, "tensor"),
        P(("pipe", "dp")),
    )
    return jax.shard_map(
        on_device,
        mesh=mesh,
        in_specs=placed,
        out_specs=(P(("pipe", "dp"), None, "tensor"), P(None, ("pipe", "dp"), None, "tensor")),
        check_vma=False,
    )
```

```python
import functools
import math

import jax
import jax.numpy as jnp
from jax import lax
from jax.experimental import pallas as pl
from jax.experimental.pallas import tpu as pltpu
from jax.sharding import PartitionSpec as P

HEAD_DIM = 128
FORWARD_STEPS = 2
CHUNKS = ((0, 10), (12, 4), (10, 2))
DETOUR = (0, 10)
SCALE = HEAD_DIM ** (-0.5)
EXPONENT = SCALE * math.log2(math.e)
NT = (((1,), (1,)), ((), ()))
NN = (((1,), (0,)), ((), ()))
TN = (((0,), (0,)), ((), ()))
AXES = ("pipe", "tensor")


def product(left, right, dims):
    return lax.dot_general(left, right, dims, preferred_element_type=jnp.float32)


def probabilities(queries, keys, outside):
    logits = product(keys, queries, NT) + outside
    highest = jnp.max(logits, axis=0, keepdims=True)
    weights = jnp.exp2((logits - highest) * EXPONENT)
    return weights * (1.0 / jnp.sum(weights, axis=0, keepdims=True))


def outside_of(segment_ref):
    length = segment_ref.shape[1]
    across = jnp.broadcast_to(segment_ref[...].astype(jnp.float32), (length, length))
    return jnp.where(across == across.T, 0.0, -1e31).astype(jnp.float32)


def forward_kernel(qkv_ref, segment_ref, out_ref, outside):
    @pl.when(pl.program_id(0) == 0)
    def _():
        outside[...] = outside_of(segment_ref)

    for start in range(0, out_ref.shape[2], HEAD_DIM):
        head = slice(start, start + HEAD_DIM)
        probs = probabilities(qkv_ref[0, 0, :, head], qkv_ref[1, 0, :, head], outside[...])
        mixed = product(probs.astype(jnp.bfloat16), qkv_ref[2, 0, :, head], TN)
        out_ref[0, :, head] = mixed.astype(jnp.bfloat16)


def forward(qkv, segment):
    _, _, length, width = qkv.shape
    step = width // FORWARD_STEPS
    return pl.pallas_call(
        forward_kernel,
        grid=(FORWARD_STEPS,),
        in_specs=[
            pl.BlockSpec((3, 1, length, step), lambda c: (0, 0, 0, c)),
            pl.BlockSpec((1, length), lambda c: (0, 0)),
        ],
        out_specs=pl.BlockSpec((1, length, step), lambda c: (0, 0, c)),
        out_shape=jax.ShapeDtypeStruct((1, length, width), jnp.bfloat16),
        scratch_shapes=[pltpu.VMEM((length, length), jnp.float32)],
        compiler_params=pltpu.CompilerParams(vmem_limit_bytes=56 * 1024 * 1024),
        cost_estimate=pl.CostEstimate(
            flops=4 * length * length * width,
            bytes_accessed=8 * length * width,
            transcendentals=length * length * width // HEAD_DIM,
        ),
    )(qkv, segment)


def backward_kernel(parts, around_from, carries, *refs):
    pieces, refs = refs[:parts], refs[parts:]
    upstream_ref, segment_ref, factor_ref = refs[:3]
    out_ref, stash = refs[-2:]
    if carries:
        out_ref = refs[-3]
        refs[-2][...] = refs[3][...]
    mine = lax.axis_index("tensor")
    rows = pieces[0].shape[2]
    if around_from is not None:
        columns = slice(around_from, around_from + pieces[0].shape[3])
        around = pieces[-1][:, 0, :, columns]
        pieces = pieces[:-1]
    found = [piece[:, 0] for piece in pieces]
    if around_from is not None:
        found[0] = jnp.where(detoured(lax.axis_index("pipe")), around, found[0])
    for k, piece in enumerate(found):
        start = pl.multiple_of((mine ^ k) * rows, rows)
        stash[:, pl.ds(start, rows), :] = piece
    outside = outside_of(segment_ref)
    factor = factor_ref[0]
    for start in range(0, upstream_ref.shape[2], HEAD_DIM):
        head = slice(start, start + HEAD_DIM)
        queries, keys, values = stash[0, :, head], stash[1, :, head], stash[2, :, head]
        upstream = upstream_ref[0, :, head]
        probs = probabilities(queries, keys, outside)
        grad_value = product(probs.astype(jnp.bfloat16), upstream, NN)
        grad_probs = product(values, upstream, NT)
        center = jnp.sum(probs * grad_probs, axis=0, keepdims=True)
        grad_logits = (probs * ((grad_probs - center) * SCALE)).astype(jnp.bfloat16)
        out_ref[0, 0, :, head] = (product(grad_logits, keys, TN) * factor).astype(jnp.bfloat16)
        out_ref[1, 0, :, head] = (product(grad_logits, queries, NN) * factor).astype(jnp.bfloat16)
        out_ref[2, 0, :, head] = (grad_value * factor).astype(jnp.bfloat16)


def backward(chunk, pieces, around, upstream, segment, factor, earlier, carried=None):
    _, length, width = upstream.shape
    first, heads = CHUNKS[chunk]
    step = heads * HEAD_DIM
    place = first // heads
    around_from = None
    if DETOUR[0] <= first and first + heads <= sum(DETOUR):
        around_from = (first - DETOUR[0]) * HEAD_DIM
        pieces = [*pieces, around]
    parts = len(pieces)
    operands = [*pieces, upstream, segment, factor]
    in_specs = [pl.BlockSpec(memory_space=pltpu.VMEM)] * parts + [
        pl.BlockSpec((1, length, step), lambda i: (0, 0, place)),
        pl.BlockSpec((1, length), lambda i: (0, 0)),
        pl.BlockSpec(memory_space=pltpu.SMEM),
    ]
    out_specs = [pl.BlockSpec((3, 1, length, step), lambda i: (0, 0, 0, place))]
    out_shape = [jax.ShapeDtypeStruct((3, 1, length, width), jnp.bfloat16)]
    if carried is not None:
        whole = pl.BlockSpec(carried.shape, lambda i: (0, 0, 0))
        operands.append(carried)
        in_specs.append(whole)
        out_specs.append(whole)
        out_shape.append(jax.ShapeDtypeStruct(carried.shape, carried.dtype))
    aliases = {}
    if earlier is not None:
        aliases = {len(operands): 0}
        operands.append(earlier)
        in_specs.append(pl.BlockSpec(memory_space=pl.ANY))
    return pl.pallas_call(
        functools.partial(backward_kernel, parts, around_from, carried is not None),
        grid=(1,),
        in_specs=in_specs,
        out_specs=out_specs,
        out_shape=out_shape,
        scratch_shapes=[pltpu.VMEM((3, length, step), jnp.bfloat16)],
        input_output_aliases=aliases,
        compiler_params=pltpu.CompilerParams(vmem_limit_bytes=32 * 1024 * 1024),
        cost_estimate=pl.CostEstimate(
            flops=10 * length * length * step,
            bytes_accessed=14 * length * step,
            transcendentals=length * length * step // HEAD_DIM,
        ),
    )(*operands)


def fetched(piece, k, leg="direct"):
    sections, tensors = lax.axis_size("pipe"), lax.axis_size("tensor")
    pairs = []
    for p in range(sections):
        for t in range(tensors):
            start, end = p, sections - 1 - p
            if leg == "aside":
                end = p ^ 1
            if leg == "onward":
                start = p ^ 1
            if leg == "all" or (leg == "direct") != detoured(p):
                pairs.append((start * tensors + t, end * tensors + (t ^ k)))
    return lax.ppermute(piece, AXES, pairs)


def detoured(section):
    half = lax.axis_size("pipe") // 2
    place = section % half
    return (place == 2) | (place == half - 3)


def shifted(array, by):
    sections = lax.axis_size("pipe")
    with jax.named_scope("direct_out" if by > 0 else "direct_grad"):
        return lax.ppermute(array, "pipe", [(p, (p + by) % sections) for p in range(sections)])


def on_device(fwd_qkv, fwd_segments, parked, bwd_segments, grad_out, loss_tokens):
    length, width = grad_out.shape[1:]
    tensors = lax.axis_size("tensor")
    mine = lax.axis_index("tensor")

    def cut(whole, k, first, heads):
        start = (mine ^ k) * width + first * HEAD_DIM
        return lax.dynamic_slice_in_dim(whole, start, heads * HEAD_DIM, axis=3)

    def fetched_chunk(whole, chunk, partners):
        first, heads = CHUNKS[chunk]
        pieces = []
        for k in partners:
            goes_around = k == 0 and DETOUR[0] <= first and first + heads <= sum(DETOUR)
            with jax.named_scope(f"stash_{k}_{chunk}"):
                piece = cut(whole, k, first, heads)
                pieces.append(fetched(piece, k, "direct" if goes_around else "all"))
        return pieces

    upstream = shifted(grad_out, -1)
    leading = cut(parked, 3, *CHUNKS[0])
    leading, parked = lax.optimization_barrier((leading, parked))
    with jax.named_scope("stash_3_0"):
        leading = fetched(leading, 3, "all")
    with jax.named_scope("aside_0"):
        around = fetched(cut(parked, 0, *DETOUR), 0, "aside")
    with jax.named_scope("onward_0"):
        around = fetched(around, 0, "onward")
    pieces = [[*fetched_chunk(parked, 0, range(3)), leading]]
    with jax.named_scope("forward_heads"):
        forward_out = forward(fwd_qkv, fwd_segments)
    received = shifted(forward_out, 1)
    tokens = loss_tokens.astype(jnp.float32)
    pieces[0][3], tokens = lax.optimization_barrier((pieces[0][3], tokens))
    token_total = lax.psum(tokens, "dp")
    factor = jnp.float32(lax.axis_size("dp") * length) / token_total
    parked, token_total = lax.optimization_barrier((parked, token_total))
    pieces.append(fetched_chunk(parked, 1, range(tensors)))
    (grads,) = backward(0, pieces[0], around, upstream, bwd_segments, factor, None)
    parked, grads = lax.optimization_barrier((parked, grads))
    others = fetched_chunk(parked, 2, range(3))
    parked, received = lax.optimization_barrier((parked, received))
    final = fetched_chunk(parked, 2, [3])
    pieces.append([*others, *final])
    grads, received = backward(
        1, pieces[1], around, upstream, bwd_segments, factor, grads, received
    )
    (grads,) = backward(2, pieces[2], around, upstream, bwd_segments, factor, grads)
    return (received, grads)


def solution(mesh):
    placed = (
        P(None, ("pipe", "dp"), None, "tensor"),
        P(("pipe", "dp"), None),
        P(None, ("pipe", "dp"), "tensor", None),
        P(("pipe", "dp"), None),
        P(("pipe", "dp"), None, "tensor"),
        P(("pipe", "dp")),
    )
    return jax.shard_map(
        on_device,
        mesh=mesh,
        in_specs=placed,
        out_specs=(P(("pipe", "dp"), None, "tensor"), P(None, ("pipe", "dp"), None, "tensor")),
        check_vma=False,
    )
```

```python
import functools
import math

import jax
import jax.numpy as jnp
from jax import lax
from jax.experimental import pallas as pl
from jax.experimental.pallas import tpu as pltpu
from jax.sharding import PartitionSpec as P

HEAD_DIM = 128
FORWARD_STEPS = 2
CHUNKS = ((0, 10), (12, 4), (10, 2))
DETOUR = (0, 12)
SCALE = HEAD_DIM ** (-0.5)
EXPONENT = SCALE * math.log2(math.e)
NT = (((1,), (1,)), ((), ()))
NN = (((1,), (0,)), ((), ()))
TN = (((0,), (0,)), ((), ()))
AXES = ("pipe", "tensor")


def product(left, right, dims):
    return lax.dot_general(left, right, dims, preferred_element_type=jnp.float32)


def probabilities(queries, keys, outside):
    logits = product(keys, queries, NT) + outside
    highest = jnp.max(logits, axis=0, keepdims=True)
    weights = jnp.exp2((logits - highest) * EXPONENT)
    return weights * (1.0 / jnp.sum(weights, axis=0, keepdims=True))


def outside_of(segment_ref):
    length = segment_ref.shape[1]
    across = jnp.broadcast_to(segment_ref[...].astype(jnp.float32), (length, length))
    return jnp.where(across == across.T, 0.0, -1e31).astype(jnp.float32)


def forward_kernel(qkv_ref, segment_ref, out_ref, outside):
    @pl.when(pl.program_id(0) == 0)
    def _():
        outside[...] = outside_of(segment_ref)

    for start in range(0, out_ref.shape[2], HEAD_DIM):
        head = slice(start, start + HEAD_DIM)
        probs = probabilities(qkv_ref[0, 0, :, head], qkv_ref[1, 0, :, head], outside[...])
        mixed = product(probs.astype(jnp.bfloat16), qkv_ref[2, 0, :, head], TN)
        out_ref[0, :, head] = mixed.astype(jnp.bfloat16)


def forward(qkv, segment):
    _, _, length, width = qkv.shape
    step = width // FORWARD_STEPS
    return pl.pallas_call(
        forward_kernel,
        grid=(FORWARD_STEPS,),
        in_specs=[
            pl.BlockSpec((3, 1, length, step), lambda c: (0, 0, 0, c)),
            pl.BlockSpec((1, length), lambda c: (0, 0)),
        ],
        out_specs=pl.BlockSpec((1, length, step), lambda c: (0, 0, c)),
        out_shape=jax.ShapeDtypeStruct((1, length, width), jnp.bfloat16),
        scratch_shapes=[pltpu.VMEM((length, length), jnp.float32)],
        compiler_params=pltpu.CompilerParams(vmem_limit_bytes=56 * 1024 * 1024),
        cost_estimate=pl.CostEstimate(
            flops=4 * length * length * width,
            bytes_accessed=8 * length * width,
            transcendentals=length * length * width // HEAD_DIM,
        ),
    )(qkv, segment)


def backward_kernel(parts, around_from, carries, *refs):
    pieces, refs = refs[:parts], refs[parts:]
    upstream_ref, segment_ref, factor_ref = refs[:3]
    out_ref, stash = refs[-2:]
    if carries:
        out_ref = refs[-3]
        refs[-2][...] = refs[3][...]
    mine = lax.axis_index("tensor")
    rows = pieces[0].shape[2]
    if around_from is not None:
        columns = slice(around_from, around_from + pieces[0].shape[3])
        around = pieces[-1][:, 0, :, columns]
        pieces = pieces[:-1]
    found = [piece[:, 0] for piece in pieces]
    if around_from is not None:
        found[0] = jnp.where(detoured(lax.axis_index("pipe")), around, found[0])
    for k, piece in enumerate(found):
        start = pl.multiple_of((mine ^ k) * rows, rows)
        stash[:, pl.ds(start, rows), :] = piece
    outside = outside_of(segment_ref)
    factor = factor_ref[0]
    for start in range(0, upstream_ref.shape[2], HEAD_DIM):
        head = slice(start, start + HEAD_DIM)
        queries, keys, values = stash[0, :, head], stash[1, :, head], stash[2, :, head]
        upstream = upstream_ref[0, :, head]
        probs = probabilities(queries, keys, outside)
        grad_value = product(probs.astype(jnp.bfloat16), upstream, NN)
        grad_probs = product(values, upstream, NT)
        center = jnp.sum(probs * grad_probs, axis=0, keepdims=True)
        grad_logits = (probs * ((grad_probs - center) * SCALE)).astype(jnp.bfloat16)
        out_ref[0, 0, :, head] = (product(grad_logits, keys, TN) * factor).astype(jnp.bfloat16)
        out_ref[1, 0, :, head] = (product(grad_logits, queries, NN) * factor).astype(jnp.bfloat16)
        out_ref[2, 0, :, head] = (grad_value * factor).astype(jnp.bfloat16)


def backward(chunk, pieces, around, upstream, segment, factor, earlier, carried=None):
    _, length, width = upstream.shape
    first, heads = CHUNKS[chunk]
    step = heads * HEAD_DIM
    place = first // heads
    around_from = None
    if DETOUR[0] <= first and first + heads <= sum(DETOUR):
        around_from = (first - DETOUR[0]) * HEAD_DIM
        pieces = [*pieces, around]
    parts = len(pieces)
    operands = [*pieces, upstream, segment, factor]
    in_specs = [pl.BlockSpec(memory_space=pltpu.VMEM)] * parts + [
        pl.BlockSpec((1, length, step), lambda i: (0, 0, place)),
        pl.BlockSpec((1, length), lambda i: (0, 0)),
        pl.BlockSpec(memory_space=pltpu.SMEM),
    ]
    out_specs = [pl.BlockSpec((3, 1, length, step), lambda i: (0, 0, 0, place))]
    out_shape = [jax.ShapeDtypeStruct((3, 1, length, width), jnp.bfloat16)]
    if carried is not None:
        whole = pl.BlockSpec(carried.shape, lambda i: (0, 0, 0))
        operands.append(carried)
        in_specs.append(whole)
        out_specs.append(whole)
        out_shape.append(jax.ShapeDtypeStruct(carried.shape, carried.dtype))
    aliases = {}
    if earlier is not None:
        aliases = {len(operands): 0}
        operands.append(earlier)
        in_specs.append(pl.BlockSpec(memory_space=pl.ANY))
    return pl.pallas_call(
        functools.partial(backward_kernel, parts, around_from, carried is not None),
        grid=(1,),
        in_specs=in_specs,
        out_specs=out_specs,
        out_shape=out_shape,
        scratch_shapes=[pltpu.VMEM((3, length, step), jnp.bfloat16)],
        input_output_aliases=aliases,
        compiler_params=pltpu.CompilerParams(vmem_limit_bytes=32 * 1024 * 1024),
        cost_estimate=pl.CostEstimate(
            flops=10 * length * length * step,
            bytes_accessed=14 * length * step,
            transcendentals=length * length * step // HEAD_DIM,
        ),
    )(*operands)


def fetched(piece, k, leg="direct"):
    sections, tensors = lax.axis_size("pipe"), lax.axis_size("tensor")
    pairs = []
    for p in range(sections):
        for t in range(tensors):
            start, end = p, sections - 1 - p
            if leg == "aside":
                end = p ^ 1
            if leg == "onward":
                start = p ^ 1
            if leg == "all" or (leg == "direct") != detoured(p):
                pairs.append((start * tensors + t, end * tensors + (t ^ k)))
    return lax.ppermute(piece, AXES, pairs)


def detoured(section):
    half = lax.axis_size("pipe") // 2
    place = section % half
    return (place == 2) | (place == half - 3)


def shifted(array, by):
    sections = lax.axis_size("pipe")
    with jax.named_scope("direct_out" if by > 0 else "direct_grad"):
        return lax.ppermute(array, "pipe", [(p, (p + by) % sections) for p in range(sections)])


def on_device(fwd_qkv, fwd_segments, parked, bwd_segments, grad_out, loss_tokens):
    length, width = grad_out.shape[1:]
    tensors = lax.axis_size("tensor")
    mine = lax.axis_index("tensor")

    def cut(whole, k, first, heads):
        start = (mine ^ k) * width + first * HEAD_DIM
        return lax.dynamic_slice_in_dim(whole, start, heads * HEAD_DIM, axis=3)

    def fetched_chunk(whole, chunk, partners):
        first, heads = CHUNKS[chunk]
        pieces = []
        for k in partners:
            goes_around = k == 0 and DETOUR[0] <= first and first + heads <= sum(DETOUR)
            with jax.named_scope(f"stash_{k}_{chunk}"):
                piece = cut(whole, k, first, heads)
                pieces.append(fetched(piece, k, "direct" if goes_around else "all"))
        return pieces

    upstream = shifted(grad_out, -1)
    leading = cut(parked, 3, *CHUNKS[0])
    leading, parked = lax.optimization_barrier((leading, parked))
    with jax.named_scope("stash_3_0"):
        leading = fetched(leading, 3, "all")
    with jax.named_scope("aside_0"):
        around = fetched(cut(parked, 0, *DETOUR), 0, "aside")
    with jax.named_scope("onward_0"):
        around = fetched(around, 0, "onward")
    pieces = [[*fetched_chunk(parked, 0, range(3)), leading]]
    with jax.named_scope("forward_heads"):
        forward_out = forward(fwd_qkv, fwd_segments)
    received = shifted(forward_out, 1)
    tokens = loss_tokens.astype(jnp.float32)
    pieces[0][3], tokens = lax.optimization_barrier((pieces[0][3], tokens))
    token_total = lax.psum(tokens, "dp")
    factor = jnp.float32(lax.axis_size("dp") * length) / token_total
    parked, token_total = lax.optimization_barrier((parked, token_total))
    pieces.append(fetched_chunk(parked, 1, range(tensors)))
    (grads,) = backward(0, pieces[0], around, upstream, bwd_segments, factor, None)
    parked, grads = lax.optimization_barrier((parked, grads))
    others = fetched_chunk(parked, 2, range(3))
    parked, received = lax.optimization_barrier((parked, received))
    final = fetched_chunk(parked, 2, [3])
    pieces.append([*others, *final])
    grads, received = backward(
        1, pieces[1], around, upstream, bwd_segments, factor, grads, received
    )
    (grads,) = backward(2, pieces[2], around, upstream, bwd_segments, factor, grads)
    return (received, grads)


def solution(mesh):
    placed = (
        P(None, ("pipe", "dp"), None, "tensor"),
        P(("pipe", "dp"), None),
        P(None, ("pipe", "dp"), "tensor", None),
        P(("pipe", "dp"), None),
        P(("pipe", "dp"), None, "tensor"),
        P(("pipe", "dp")),
    )
    return jax.shard_map(
        on_device,
        mesh=mesh,
        in_specs=placed,
        out_specs=(P(("pipe", "dp"), None, "tensor"), P(None, ("pipe", "dp"), None, "tensor")),
        check_vma=False,
    )
```

```python
import functools
import math

import jax
import jax.numpy as jnp
from jax import lax
from jax.experimental import pallas as pl
from jax.experimental.pallas import tpu as pltpu
from jax.sharding import PartitionSpec as P

HEAD_DIM = 128
FORWARD_STEPS = 2
CHUNKS = ((0, 10), (12, 4), (10, 2))
DETOUR = (0, 10)
SCALE = HEAD_DIM ** (-0.5)
EXPONENT = SCALE * math.log2(math.e)
NT = (((1,), (1,)), ((), ()))
NN = (((1,), (0,)), ((), ()))
TN = (((0,), (0,)), ((), ()))
AXES = ("pipe", "tensor")


def product(left, right, dims):
    return lax.dot_general(left, right, dims, preferred_element_type=jnp.float32)


def probabilities(queries, keys, outside):
    logits = product(keys, queries, NT) + outside
    highest = jnp.max(logits, axis=0, keepdims=True)
    weights = jnp.exp2((logits - highest) * EXPONENT)
    return weights * (1.0 / jnp.sum(weights, axis=0, keepdims=True))


def outside_of(segment_ref):
    length = segment_ref.shape[1]
    across = jnp.broadcast_to(segment_ref[...].astype(jnp.float32), (length, length))
    return jnp.where(across == across.T, 0.0, -1e31).astype(jnp.float32)


def forward_kernel(qkv_ref, segment_ref, out_ref, outside):
    @pl.when(pl.program_id(0) == 0)
    def _():
        outside[...] = outside_of(segment_ref)

    for start in range(0, out_ref.shape[2], HEAD_DIM):
        head = slice(start, start + HEAD_DIM)
        probs = probabilities(qkv_ref[0, 0, :, head], qkv_ref[1, 0, :, head], outside[...])
        mixed = product(probs.astype(jnp.bfloat16), qkv_ref[2, 0, :, head], TN)
        out_ref[0, :, head] = mixed.astype(jnp.bfloat16)


def forward(qkv, segment):
    _, _, length, width = qkv.shape
    step = width // FORWARD_STEPS
    return pl.pallas_call(
        forward_kernel,
        grid=(FORWARD_STEPS,),
        in_specs=[
            pl.BlockSpec((3, 1, length, step), lambda c: (0, 0, 0, c)),
            pl.BlockSpec((1, length), lambda c: (0, 0)),
        ],
        out_specs=pl.BlockSpec((1, length, step), lambda c: (0, 0, c)),
        out_shape=jax.ShapeDtypeStruct((1, length, width), jnp.bfloat16),
        scratch_shapes=[pltpu.VMEM((length, length), jnp.float32)],
        compiler_params=pltpu.CompilerParams(vmem_limit_bytes=56 * 1024 * 1024),
        cost_estimate=pl.CostEstimate(
            flops=4 * length * length * width,
            bytes_accessed=8 * length * width,
            transcendentals=length * length * width // HEAD_DIM,
        ),
    )(qkv, segment)


def backward_kernel(parts, around_from, goes, carries, *refs):
    pieces, refs = refs[:parts], refs[parts:]
    upstream_ref, segment_ref, factor_ref = refs[:3]
    out_ref, stash = refs[-2:]
    if carries:
        out_ref = refs[-3]
        refs[-2][...] = refs[3][...]
    mine = lax.axis_index("tensor")
    rows = pieces[0].shape[2]
    if around_from is not None:
        columns = slice(around_from, around_from + pieces[0].shape[3])
        around = pieces[-1][:, 0, :, columns]
        pieces = pieces[:-1]
    found = [piece[:, 0] for piece in pieces]
    if around_from is not None:
        source = lax.axis_size("pipe") - 1 - lax.axis_index("pipe")
        found[0] = jnp.where(goes(source), around, found[0])
    for k, piece in enumerate(found):
        start = pl.multiple_of((mine ^ k) * rows, rows)
        stash[:, pl.ds(start, rows), :] = piece
    outside = outside_of(segment_ref)
    factor = factor_ref[0]
    for start in range(0, upstream_ref.shape[2], HEAD_DIM):
        head = slice(start, start + HEAD_DIM)
        queries, keys, values = stash[0, :, head], stash[1, :, head], stash[2, :, head]
        upstream = upstream_ref[0, :, head]
        probs = probabilities(queries, keys, outside)
        grad_value = product(probs.astype(jnp.bfloat16), upstream, NN)
        grad_probs = product(values, upstream, NT)
        center = jnp.sum(probs * grad_probs, axis=0, keepdims=True)
        grad_logits = (probs * ((grad_probs - center) * SCALE)).astype(jnp.bfloat16)
        out_ref[0, 0, :, head] = (product(grad_logits, keys, TN) * factor).astype(jnp.bfloat16)
        out_ref[1, 0, :, head] = (product(grad_logits, queries, NN) * factor).astype(jnp.bfloat16)
        out_ref[2, 0, :, head] = (grad_value * factor).astype(jnp.bfloat16)


def backward(chunk, pieces, around, upstream, segment, factor, earlier, carried=None):
    _, length, width = upstream.shape
    first, heads = CHUNKS[chunk]
    step = heads * HEAD_DIM
    place = first // heads
    around_from = None
    goes = detoured if chunk == 0 else detoured_late
    if around is not None:
        around_from = 0
        pieces = [*pieces, around]
    parts = len(pieces)
    operands = [*pieces, upstream, segment, factor]
    in_specs = [pl.BlockSpec(memory_space=pltpu.VMEM)] * parts + [
        pl.BlockSpec((1, length, step), lambda i: (0, 0, place)),
        pl.BlockSpec((1, length), lambda i: (0, 0)),
        pl.BlockSpec(memory_space=pltpu.SMEM),
    ]
    out_specs = [pl.BlockSpec((3, 1, length, step), lambda i: (0, 0, 0, place))]
    out_shape = [jax.ShapeDtypeStruct((3, 1, length, width), jnp.bfloat16)]
    if carried is not None:
        whole = pl.BlockSpec(carried.shape, lambda i: (0, 0, 0))
        operands.append(carried)
        in_specs.append(whole)
        out_specs.append(whole)
        out_shape.append(jax.ShapeDtypeStruct(carried.shape, carried.dtype))
    aliases = {}
    if earlier is not None:
        aliases = {len(operands): 0}
        operands.append(earlier)
        in_specs.append(pl.BlockSpec(memory_space=pl.ANY))
    return pl.pallas_call(
        functools.partial(backward_kernel, parts, around_from, goes, carried is not None),
        grid=(1,),
        in_specs=in_specs,
        out_specs=out_specs,
        out_shape=out_shape,
        scratch_shapes=[pltpu.VMEM((3, length, step), jnp.bfloat16)],
        input_output_aliases=aliases,
        compiler_params=pltpu.CompilerParams(vmem_limit_bytes=32 * 1024 * 1024),
        cost_estimate=pl.CostEstimate(
            flops=10 * length * length * step,
            bytes_accessed=14 * length * step,
            transcendentals=length * length * step // HEAD_DIM,
        ),
    )(*operands)


def fetched(piece, k, leg="direct", goes=None):
    sections, tensors = lax.axis_size("pipe"), lax.axis_size("tensor")
    goes = goes or detoured
    pairs = []
    for p in range(sections):
        for t in range(tensors):
            start, end = p, sections - 1 - p
            if leg == "aside":
                end = p ^ 1
            if leg == "onward":
                start = p ^ 1
            if leg == "all" or (leg == "direct") != goes(p):
                pairs.append((start * tensors + t, end * tensors + (t ^ k)))
    return lax.ppermute(piece, AXES, pairs)


def detoured(section):
    half = lax.axis_size("pipe") // 2
    place = section % half
    return (place == 2) | (place == half - 3)


def detoured_late(section):
    return section == lax.axis_size("pipe") - 3


def shifted(array, by):
    sections = lax.axis_size("pipe")
    with jax.named_scope("direct_out" if by > 0 else "direct_grad"):
        return lax.ppermute(array, "pipe", [(p, (p + by) % sections) for p in range(sections)])


def on_device(fwd_qkv, fwd_segments, parked, bwd_segments, grad_out, loss_tokens):
    length, width = grad_out.shape[1:]
    tensors = lax.axis_size("tensor")
    mine = lax.axis_index("tensor")

    def cut(whole, k, first, heads):
        start = (mine ^ k) * width + first * HEAD_DIM
        return lax.dynamic_slice_in_dim(whole, start, heads * HEAD_DIM, axis=3)

    def fetched_chunk(whole, chunk, partners):
        first, heads = CHUNKS[chunk]
        pieces = []
        for k in partners:
            leg = "direct" if k == 0 and chunk != 1 else "all"
            goes = detoured if chunk == 0 else detoured_late
            with jax.named_scope(f"stash_{k}_{chunk}"):
                pieces.append(fetched(cut(whole, k, first, heads), k, leg, goes))
        return pieces

    upstream = shifted(grad_out, -1)
    leading = cut(parked, 3, *CHUNKS[0])
    leading, parked = lax.optimization_barrier((leading, parked))
    with jax.named_scope("stash_3_0"):
        leading = fetched(leading, 3, "all")
    with jax.named_scope("aside_0"):
        around = fetched(cut(parked, 0, *DETOUR), 0, "aside")
    with jax.named_scope("onward_0"):
        around = fetched(around, 0, "onward")
    pieces = [[*fetched_chunk(parked, 0, range(3)), leading]]
    with jax.named_scope("forward_heads"):
        forward_out = forward(fwd_qkv, fwd_segments)
    received = shifted(forward_out, 1)
    tokens = loss_tokens.astype(jnp.float32)
    pieces[0][3], tokens = lax.optimization_barrier((pieces[0][3], tokens))
    token_total = lax.psum(tokens, "dp")
    factor = jnp.float32(lax.axis_size("dp") * length) / token_total
    parked, token_total = lax.optimization_barrier((parked, token_total))
    pieces.append(fetched_chunk(parked, 1, range(tensors)))
    (grads,) = backward(0, pieces[0], around, upstream, bwd_segments, factor, None)
    parked, grads = lax.optimization_barrier((parked, grads))
    others = fetched_chunk(parked, 2, range(3))
    parked, received = lax.optimization_barrier((parked, received))
    with jax.named_scope("aside_2"):
        late = fetched(cut(parked, 0, *CHUNKS[2]), 0, "aside", detoured_late)
    with jax.named_scope("onward_2"):
        late = fetched(late, 0, "onward", detoured_late)
    final = fetched_chunk(parked, 2, [3])
    pieces.append([*others, *final])
    grads, received = backward(
        1, pieces[1], None, upstream, bwd_segments, factor, grads, received
    )
    (grads,) = backward(2, pieces[2], late, upstream, bwd_segments, factor, grads)
    return (received, grads)


def solution(mesh):
    placed = (
        P(None, ("pipe", "dp"), None, "tensor"),
        P(("pipe", "dp"), None),
        P(None, ("pipe", "dp"), "tensor", None),
        P(("pipe", "dp"), None),
        P(("pipe", "dp"), None, "tensor"),
        P(("pipe", "dp")),
    )
    return jax.shard_map(
        on_device,
        mesh=mesh,
        in_specs=placed,
        out_specs=(P(("pipe", "dp"), None, "tensor"), P(None, ("pipe", "dp"), None, "tensor")),
        check_vma=False,
    )
```

```python
import functools
import math

import jax
import jax.numpy as jnp
from jax import lax
from jax.experimental import pallas as pl
from jax.experimental.pallas import tpu as pltpu
from jax.sharding import PartitionSpec as P

HEAD_DIM = 128
FORWARD_STEPS = 2
CHUNKS = ((0, 10), (12, 4), (10, 2))
DETOUR = (0, 10)
SCALE = HEAD_DIM ** (-0.5)
EXPONENT = SCALE * math.log2(math.e)
NT = (((1,), (1,)), ((), ()))
NN = (((1,), (0,)), ((), ()))
TN = (((0,), (0,)), ((), ()))
AXES = ("pipe", "tensor")


def product(left, right, dims):
    return lax.dot_general(left, right, dims, preferred_element_type=jnp.float32)


def probabilities(queries, keys, outside):
    logits = product(keys, queries, NT) + outside
    highest = jnp.max(logits, axis=0, keepdims=True)
    weights = jnp.exp2((logits - highest) * EXPONENT)
    return weights * (1.0 / jnp.sum(weights, axis=0, keepdims=True))


def outside_of(segment_ref):
    length = segment_ref.shape[1]
    across = jnp.broadcast_to(segment_ref[...].astype(jnp.float32), (length, length))
    return jnp.where(across == across.T, 0.0, -1e31).astype(jnp.float32)


def forward_kernel(qkv_ref, segment_ref, out_ref, outside):
    @pl.when(pl.program_id(0) == 0)
    def _():
        outside[...] = outside_of(segment_ref)

    for start in range(0, out_ref.shape[2], HEAD_DIM):
        head = slice(start, start + HEAD_DIM)
        probs = probabilities(qkv_ref[0, 0, :, head], qkv_ref[1, 0, :, head], outside[...])
        mixed = product(probs.astype(jnp.bfloat16), qkv_ref[2, 0, :, head], TN)
        out_ref[0, :, head] = mixed.astype(jnp.bfloat16)


def forward(qkv, segment):
    _, _, length, width = qkv.shape
    step = width // FORWARD_STEPS
    return pl.pallas_call(
        forward_kernel,
        grid=(FORWARD_STEPS,),
        in_specs=[
            pl.BlockSpec((3, 1, length, step), lambda c: (0, 0, 0, c)),
            pl.BlockSpec((1, length), lambda c: (0, 0)),
        ],
        out_specs=pl.BlockSpec((1, length, step), lambda c: (0, 0, c)),
        out_shape=jax.ShapeDtypeStruct((1, length, width), jnp.bfloat16),
        scratch_shapes=[pltpu.VMEM((length, length), jnp.float32)],
        compiler_params=pltpu.CompilerParams(vmem_limit_bytes=56 * 1024 * 1024),
        cost_estimate=pl.CostEstimate(
            flops=4 * length * length * width,
            bytes_accessed=8 * length * width,
            transcendentals=length * length * width // HEAD_DIM,
        ),
    )(qkv, segment)


def backward_kernel(parts, around_from, goes, carries, *refs):
    pieces, refs = refs[:parts], refs[parts:]
    upstream_ref, segment_ref, factor_ref = refs[:3]
    out_ref, stash = refs[-2:]
    if carries:
        out_ref = refs[-3]
        refs[-2][...] = refs[3][...]
    mine = lax.axis_index("tensor")
    rows = pieces[0].shape[2]
    if around_from is not None:
        columns = slice(around_from, around_from + pieces[0].shape[3])
        around = pieces[-1][:, 0, :, columns]
        pieces = pieces[:-1]
    found = [piece[:, 0] for piece in pieces]
    if around_from is not None:
        source = lax.axis_size("pipe") - 1 - lax.axis_index("pipe")
        found[0] = jnp.where(goes(source), around, found[0])
    for k, piece in enumerate(found):
        start = pl.multiple_of((mine ^ k) * rows, rows)
        stash[:, pl.ds(start, rows), :] = piece
    outside = outside_of(segment_ref)
    factor = factor_ref[0]
    for start in range(0, upstream_ref.shape[2], HEAD_DIM):
        head = slice(start, start + HEAD_DIM)
        queries, keys, values = stash[0, :, head], stash[1, :, head], stash[2, :, head]
        upstream = upstream_ref[0, :, head]
        probs = probabilities(queries, keys, outside)
        grad_value = product(probs.astype(jnp.bfloat16), upstream, NN)
        grad_probs = product(values, upstream, NT)
        center = jnp.sum(probs * grad_probs, axis=0, keepdims=True)
        grad_logits = (probs * ((grad_probs - center) * SCALE)).astype(jnp.bfloat16)
        out_ref[0, 0, :, head] = (product(grad_logits, keys, TN) * factor).astype(jnp.bfloat16)
        out_ref[1, 0, :, head] = (product(grad_logits, queries, NN) * factor).astype(jnp.bfloat16)
        out_ref[2, 0, :, head] = (grad_value * factor).astype(jnp.bfloat16)


def backward(chunk, pieces, around, upstream, segment, factor, earlier, carried=None):
    _, length, width = upstream.shape
    first, heads = CHUNKS[chunk]
    step = heads * HEAD_DIM
    place = first // heads
    around_from = None
    goes = detoured if chunk == 0 else detoured_late
    if around is not None:
        around_from = 0
        pieces = [*pieces, around]
    parts = len(pieces)
    operands = [*pieces, upstream, segment, factor]
    in_specs = [pl.BlockSpec(memory_space=pltpu.VMEM)] * parts + [
        pl.BlockSpec((1, length, step), lambda i: (0, 0, place)),
        pl.BlockSpec((1, length), lambda i: (0, 0)),
        pl.BlockSpec(memory_space=pltpu.SMEM),
    ]
    out_specs = [pl.BlockSpec((3, 1, length, step), lambda i: (0, 0, 0, place))]
    out_shape = [jax.ShapeDtypeStruct((3, 1, length, width), jnp.bfloat16)]
    if carried is not None:
        whole = pl.BlockSpec(carried.shape, lambda i: (0, 0, 0))
        operands.append(carried)
        in_specs.append(whole)
        out_specs.append(whole)
        out_shape.append(jax.ShapeDtypeStruct(carried.shape, carried.dtype))
    aliases = {}
    if earlier is not None:
        aliases = {len(operands): 0}
        operands.append(earlier)
        in_specs.append(pl.BlockSpec(memory_space=pl.ANY))
    return pl.pallas_call(
        functools.partial(backward_kernel, parts, around_from, goes, carried is not None),
        grid=(1,),
        in_specs=in_specs,
        out_specs=out_specs,
        out_shape=out_shape,
        scratch_shapes=[pltpu.VMEM((3, length, step), jnp.bfloat16)],
        input_output_aliases=aliases,
        compiler_params=pltpu.CompilerParams(vmem_limit_bytes=32 * 1024 * 1024),
        cost_estimate=pl.CostEstimate(
            flops=10 * length * length * step,
            bytes_accessed=14 * length * step,
            transcendentals=length * length * step // HEAD_DIM,
        ),
    )(*operands)


def fetched(piece, k, leg="direct", goes=None):
    sections, tensors = lax.axis_size("pipe"), lax.axis_size("tensor")
    goes = goes or detoured
    pairs = []
    for p in range(sections):
        for t in range(tensors):
            start, end = p, sections - 1 - p
            if leg == "aside":
                end = p ^ 1
            if leg == "onward":
                start = p ^ 1
            if leg == "all" or (leg == "direct") != goes(p):
                pairs.append((start * tensors + t, end * tensors + (t ^ k)))
    return lax.ppermute(piece, AXES, pairs)


def detoured(section):
    half = lax.axis_size("pipe") // 2
    place = section % half
    return (place == 2) | (place == half - 3)


def detoured_late(section):
    return section == lax.axis_size("pipe") - 3


def shifted(array, by):
    sections = lax.axis_size("pipe")
    with jax.named_scope("direct_out" if by > 0 else "direct_grad"):
        return lax.ppermute(array, "pipe", [(p, (p + by) % sections) for p in range(sections)])


def on_device(fwd_qkv, fwd_segments, parked, bwd_segments, grad_out, loss_tokens):
    length, width = grad_out.shape[1:]
    tensors = lax.axis_size("tensor")
    mine = lax.axis_index("tensor")

    def cut(whole, k, first, heads):
        start = (mine ^ k) * width + first * HEAD_DIM
        return lax.dynamic_slice_in_dim(whole, start, heads * HEAD_DIM, axis=3)

    def fetched_chunk(whole, chunk, partners):
        first, heads = CHUNKS[chunk]
        pieces = []
        for k in partners:
            leg = "direct" if k == 0 and chunk != 1 else "all"
            goes = detoured if chunk == 0 else detoured_late
            with jax.named_scope(f"stash_{k}_{chunk}"):
                pieces.append(fetched(cut(whole, k, first, heads), k, leg, goes))
        return pieces

    upstream = shifted(grad_out, -1)
    leading = cut(parked, 3, *CHUNKS[0])
    leading, parked = lax.optimization_barrier((leading, parked))
    with jax.named_scope("stash_3_0"):
        leading = fetched(leading, 3, "all")
    with jax.named_scope("aside_0"):
        around = fetched(cut(parked, 0, *DETOUR), 0, "aside")
    with jax.named_scope("onward_0"):
        around = fetched(around, 0, "onward")
    pieces = [[*fetched_chunk(parked, 0, range(3)), leading]]
    with jax.named_scope("forward_heads"):
        forward_out = forward(fwd_qkv, fwd_segments)
    received = shifted(forward_out, 1)
    tokens = loss_tokens.astype(jnp.float32)
    pieces[0][3], tokens = lax.optimization_barrier((pieces[0][3], tokens))
    token_total = lax.psum(tokens, "dp")
    factor = jnp.float32(lax.axis_size("dp") * length) / token_total
    parked, token_total = lax.optimization_barrier((parked, token_total))
    pieces.append(fetched_chunk(parked, 1, range(tensors)))
    (grads,) = backward(0, pieces[0], around, upstream, bwd_segments, factor, None)
    parked, grads = lax.optimization_barrier((parked, grads))
    others = fetched_chunk(parked, 2, range(3))
    parked, received = lax.optimization_barrier((parked, received))
    with jax.named_scope("aside_2"):
        late = fetched(cut(parked, 0, *CHUNKS[2]), 0, "aside", detoured_late)
    final = fetched_chunk(parked, 2, [3])
    pieces.append([*others, *final])
    late, grads = lax.optimization_barrier((late, grads))
    grads, received = backward(
        1, pieces[1], None, upstream, bwd_segments, factor, grads, received
    )
    late, grads = lax.optimization_barrier((late, grads))
    with jax.named_scope("onward_2"):
        late = fetched(late, 0, "onward", detoured_late)
    (grads,) = backward(2, pieces[2], late, upstream, bwd_segments, factor, grads)
    return (received, grads)


def solution(mesh):
    placed = (
        P(None, ("pipe", "dp"), None, "tensor"),
        P(("pipe", "dp"), None),
        P(None, ("pipe", "dp"), "tensor", None),
        P(("pipe", "dp"), None),
        P(("pipe", "dp"), None, "tensor"),
        P(("pipe", "dp")),
    )
    return jax.shard_map(
        on_device,
        mesh=mesh,
        in_specs=placed,
        out_specs=(P(("pipe", "dp"), None, "tensor"), P(None, ("pipe", "dp"), None, "tensor")),
        check_vma=False,
    )
```

```python
import functools
import math

import jax
import jax.numpy as jnp
from jax import lax
from jax.experimental import pallas as pl
from jax.experimental.pallas import tpu as pltpu
from jax.sharding import PartitionSpec as P

HEAD_DIM = 128
FORWARD_STEPS = 2
CHUNKS = ((0, 10), (12, 4), (10, 2))
DETOUR = (0, 10)
SCALE = HEAD_DIM ** (-0.5)
EXPONENT = SCALE * math.log2(math.e)
NT = (((1,), (1,)), ((), ()))
NN = (((1,), (0,)), ((), ()))
TN = (((0,), (0,)), ((), ()))
AXES = ("pipe", "tensor")


def product(left, right, dims):
    return lax.dot_general(left, right, dims, preferred_element_type=jnp.float32)


def probabilities(queries, keys, outside):
    logits = product(keys, queries, NT) + outside
    highest = jnp.max(logits, axis=0, keepdims=True)
    weights = jnp.exp2((logits - highest) * EXPONENT)
    return weights * (1.0 / jnp.sum(weights, axis=0, keepdims=True))


def outside_of(segment_ref):
    length = segment_ref.shape[1]
    across = jnp.broadcast_to(segment_ref[...].astype(jnp.float32), (length, length))
    return jnp.where(across == across.T, 0.0, -1e31).astype(jnp.float32)


def forward_kernel(qkv_ref, segment_ref, out_ref, outside):
    @pl.when(pl.program_id(0) == 0)
    def _():
        outside[...] = outside_of(segment_ref)

    for start in range(0, out_ref.shape[2], HEAD_DIM):
        head = slice(start, start + HEAD_DIM)
        probs = probabilities(qkv_ref[0, 0, :, head], qkv_ref[1, 0, :, head], outside[...])
        mixed = product(probs.astype(jnp.bfloat16), qkv_ref[2, 0, :, head], TN)
        out_ref[0, :, head] = mixed.astype(jnp.bfloat16)


def forward(qkv, segment):
    _, _, length, width = qkv.shape
    step = width // FORWARD_STEPS
    return pl.pallas_call(
        forward_kernel,
        grid=(FORWARD_STEPS,),
        in_specs=[
            pl.BlockSpec((3, 1, length, step), lambda c: (0, 0, 0, c)),
            pl.BlockSpec((1, length), lambda c: (0, 0)),
        ],
        out_specs=pl.BlockSpec((1, length, step), lambda c: (0, 0, c)),
        out_shape=jax.ShapeDtypeStruct((1, length, width), jnp.bfloat16),
        scratch_shapes=[pltpu.VMEM((length, length), jnp.float32)],
        compiler_params=pltpu.CompilerParams(vmem_limit_bytes=56 * 1024 * 1024),
        cost_estimate=pl.CostEstimate(
            flops=4 * length * length * width,
            bytes_accessed=8 * length * width,
            transcendentals=length * length * width // HEAD_DIM,
        ),
    )(qkv, segment)


def backward_kernel(parts, around_from, goes, carries, *refs):
    pieces, refs = refs[:parts], refs[parts:]
    upstream_ref, segment_ref, factor_ref = refs[:3]
    out_ref, stash = refs[-2:]
    if carries:
        out_ref = refs[-3]
        refs[-2][...] = refs[3][...]
    mine = lax.axis_index("tensor")
    rows = pieces[0].shape[2]
    if around_from is not None:
        columns = slice(around_from, around_from + pieces[0].shape[3])
        around = pieces[-1][:, 0, :, columns]
        pieces = pieces[:-1]
    found = [piece[:, 0] for piece in pieces]
    if around_from is not None:
        source = lax.axis_size("pipe") - 1 - lax.axis_index("pipe")
        found[0] = jnp.where(goes(source), around, found[0])
    for k, piece in enumerate(found):
        start = pl.multiple_of((mine ^ k) * rows, rows)
        stash[:, pl.ds(start, rows), :] = piece
    if segment_ref.shape[0] == 1:
        outside = outside_of(segment_ref)
        out_ref = refs[-3]
        refs[-2][...] = outside
    else:
        outside = segment_ref[...]
    factor = factor_ref[0]
    for start in range(0, upstream_ref.shape[2], HEAD_DIM):
        head = slice(start, start + HEAD_DIM)
        queries, keys, values = stash[0, :, head], stash[1, :, head], stash[2, :, head]
        upstream = upstream_ref[0, :, head]
        probs = probabilities(queries, keys, outside)
        grad_value = product(probs.astype(jnp.bfloat16), upstream, NN)
        grad_probs = product(values, upstream, NT)
        center = jnp.sum(probs * grad_probs, axis=0, keepdims=True)
        grad_logits = (probs * ((grad_probs - center) * SCALE)).astype(jnp.bfloat16)
        out_ref[0, 0, :, head] = (product(grad_logits, keys, TN) * factor).astype(jnp.bfloat16)
        out_ref[1, 0, :, head] = (product(grad_logits, queries, NN) * factor).astype(jnp.bfloat16)
        out_ref[2, 0, :, head] = (grad_value * factor).astype(jnp.bfloat16)


def backward(chunk, pieces, around, upstream, segment, factor, earlier, carried=None):
    _, length, width = upstream.shape
    first, heads = CHUNKS[chunk]
    step = heads * HEAD_DIM
    place = first // heads
    around_from = None
    goes = detoured if chunk == 0 else detoured_late
    if around is not None:
        around_from = 0
        pieces = [*pieces, around]
    parts = len(pieces)
    operands = [*pieces, upstream, segment, factor]
    in_specs = [pl.BlockSpec(memory_space=pltpu.VMEM)] * parts + [
        pl.BlockSpec((1, length, step), lambda i: (0, 0, place)),
        pl.BlockSpec(segment.shape, lambda i: (0, 0)),
        pl.BlockSpec(memory_space=pltpu.SMEM),
    ]
    out_specs = [pl.BlockSpec((3, 1, length, step), lambda i: (0, 0, 0, place))]
    out_shape = [jax.ShapeDtypeStruct((3, 1, length, width), jnp.bfloat16)]
    if segment.shape[0] == 1:
        out_specs.append(pl.BlockSpec((length, length), lambda i: (0, 0)))
        out_shape.append(jax.ShapeDtypeStruct((length, length), jnp.float32))
    if carried is not None:
        whole = pl.BlockSpec(carried.shape, lambda i: (0, 0, 0))
        operands.append(carried)
        in_specs.append(whole)
        out_specs.append(whole)
        out_shape.append(jax.ShapeDtypeStruct(carried.shape, carried.dtype))
    aliases = {}
    if earlier is not None:
        aliases = {len(operands): 0}
        operands.append(earlier)
        in_specs.append(pl.BlockSpec(memory_space=pl.ANY))
    return pl.pallas_call(
        functools.partial(backward_kernel, parts, around_from, goes, carried is not None),
        grid=(1,),
        in_specs=in_specs,
        out_specs=out_specs,
        out_shape=out_shape,
        scratch_shapes=[pltpu.VMEM((3, length, step), jnp.bfloat16)],
        input_output_aliases=aliases,
        compiler_params=pltpu.CompilerParams(vmem_limit_bytes=32 * 1024 * 1024),
        cost_estimate=pl.CostEstimate(
            flops=10 * length * length * step,
            bytes_accessed=14 * length * step,
            transcendentals=length * length * step // HEAD_DIM,
        ),
    )(*operands)


def fetched(piece, k, leg="direct", goes=None):
    sections, tensors = lax.axis_size("pipe"), lax.axis_size("tensor")
    goes = goes or detoured
    pairs = []
    for p in range(sections):
        for t in range(tensors):
            start, end = p, sections - 1 - p
            if leg == "aside":
                end = p ^ 1
            if leg == "onward":
                start = p ^ 1
            if leg == "all" or (leg == "direct") != goes(p):
                pairs.append((start * tensors + t, end * tensors + (t ^ k)))
    return lax.ppermute(piece, AXES, pairs)


def detoured(section):
    half = lax.axis_size("pipe") // 2
    place = section % half
    return (place == 2) | (place == half - 3)


def detoured_late(section):
    return section == lax.axis_size("pipe") - 3


def shifted(array, by):
    sections = lax.axis_size("pipe")
    with jax.named_scope("direct_out" if by > 0 else "direct_grad"):
        return lax.ppermute(array, "pipe", [(p, (p + by) % sections) for p in range(sections)])


def on_device(fwd_qkv, fwd_segments, parked, bwd_segments, grad_out, loss_tokens):
    length, width = grad_out.shape[1:]
    tensors = lax.axis_size("tensor")
    mine = lax.axis_index("tensor")

    def cut(whole, k, first, heads):
        start = (mine ^ k) * width + first * HEAD_DIM
        return lax.dynamic_slice_in_dim(whole, start, heads * HEAD_DIM, axis=3)

    def fetched_chunk(whole, chunk, partners):
        first, heads = CHUNKS[chunk]
        pieces = []
        for k in partners:
            leg = "direct" if k == 0 and chunk != 1 else "all"
            goes = detoured if chunk == 0 else detoured_late
            with jax.named_scope(f"stash_{k}_{chunk}"):
                pieces.append(fetched(cut(whole, k, first, heads), k, leg, goes))
        return pieces

    upstream = shifted(grad_out, -1)
    leading = cut(parked, 3, *CHUNKS[0])
    leading, parked = lax.optimization_barrier((leading, parked))
    with jax.named_scope("stash_3_0"):
        leading = fetched(leading, 3, "all")
    with jax.named_scope("aside_0"):
        around = fetched(cut(parked, 0, *DETOUR), 0, "aside")
    with jax.named_scope("onward_0"):
        around = fetched(around, 0, "onward")
    pieces = [[*fetched_chunk(parked, 0, range(3)), leading]]
    with jax.named_scope("forward_heads"):
        forward_out = forward(fwd_qkv, fwd_segments)
    received = shifted(forward_out, 1)
    tokens = loss_tokens.astype(jnp.float32)
    pieces[0][3], tokens = lax.optimization_barrier((pieces[0][3], tokens))
    token_total = lax.psum(tokens, "dp")
    factor = jnp.float32(lax.axis_size("dp") * length) / token_total
    parked, token_total = lax.optimization_barrier((parked, token_total))
    pieces.append(fetched_chunk(parked, 1, range(tensors)))
    grads, outside = backward(0, pieces[0], around, upstream, bwd_segments, factor, None)
    parked, grads = lax.optimization_barrier((parked, grads))
    others = fetched_chunk(parked, 2, range(3))
    parked, received = lax.optimization_barrier((parked, received))
    with jax.named_scope("aside_2"):
        late = fetched(cut(parked, 0, *CHUNKS[2]), 0, "aside", detoured_late)
    final = fetched_chunk(parked, 2, [3])
    pieces.append([*others, *final])
    late, grads = lax.optimization_barrier((late, grads))
    grads, received = backward(
        1, pieces[1], None, upstream, outside, factor, grads, received
    )
    late, grads = lax.optimization_barrier((late, grads))
    with jax.named_scope("onward_2"):
        late = fetched(late, 0, "onward", detoured_late)
    (grads,) = backward(2, pieces[2], late, upstream, outside, factor, grads)
    return (received, grads)


def solution(mesh):
    placed = (
        P(None, ("pipe", "dp"), None, "tensor"),
        P(("pipe", "dp"), None),
        P(None, ("pipe", "dp"), "tensor", None),
        P(("pipe", "dp"), None),
        P(("pipe", "dp"), None, "tensor"),
        P(("pipe", "dp")),
    )
    return jax.shard_map(
        on_device,
        mesh=mesh,
        in_specs=placed,
        out_specs=(P(("pipe", "dp"), None, "tensor"), P(None, ("pipe", "dp"), None, "tensor")),
        check_vma=False,
    )
```

```python
import functools
import math

import jax
import jax.numpy as jnp
from jax import lax
from jax.experimental import pallas as pl
from jax.experimental.pallas import tpu as pltpu
from jax.sharding import PartitionSpec as P

HEAD_DIM = 128
FORWARD_STEPS = 2
CHUNKS = ((0, 10), (10, 5), (15, 1))
DETOUR = (0, 10)
SCALE = HEAD_DIM ** (-0.5)
EXPONENT = SCALE * math.log2(math.e)
NT = (((1,), (1,)), ((), ()))
NN = (((1,), (0,)), ((), ()))
TN = (((0,), (0,)), ((), ()))
AXES = ("pipe", "tensor")


def product(left, right, dims):
    return lax.dot_general(left, right, dims, preferred_element_type=jnp.float32)


def probabilities(queries, keys, outside):
    logits = product(keys, queries, NT) + outside
    highest = jnp.max(logits, axis=0, keepdims=True)
    weights = jnp.exp2((logits - highest) * EXPONENT)
    return weights * (1.0 / jnp.sum(weights, axis=0, keepdims=True))


def outside_of(segment_ref):
    length = segment_ref.shape[1]
    across = jnp.broadcast_to(segment_ref[...].astype(jnp.float32), (length, length))
    return jnp.where(across == across.T, 0.0, -1e31).astype(jnp.float32)


def forward_kernel(qkv_ref, segment_ref, out_ref, outside):
    @pl.when(pl.program_id(0) == 0)
    def _():
        outside[...] = outside_of(segment_ref)

    for start in range(0, out_ref.shape[2], HEAD_DIM):
        head = slice(start, start + HEAD_DIM)
        probs = probabilities(qkv_ref[0, 0, :, head], qkv_ref[1, 0, :, head], outside[...])
        mixed = product(probs.astype(jnp.bfloat16), qkv_ref[2, 0, :, head], TN)
        out_ref[0, :, head] = mixed.astype(jnp.bfloat16)


def forward(qkv, segment):
    _, _, length, width = qkv.shape
    step = width // FORWARD_STEPS
    return pl.pallas_call(
        forward_kernel,
        grid=(FORWARD_STEPS,),
        in_specs=[
            pl.BlockSpec((3, 1, length, step), lambda c: (0, 0, 0, c)),
            pl.BlockSpec((1, length), lambda c: (0, 0)),
        ],
        out_specs=pl.BlockSpec((1, length, step), lambda c: (0, 0, c)),
        out_shape=jax.ShapeDtypeStruct((1, length, width), jnp.bfloat16),
        scratch_shapes=[pltpu.VMEM((length, length), jnp.float32)],
        compiler_params=pltpu.CompilerParams(vmem_limit_bytes=56 * 1024 * 1024),
        cost_estimate=pl.CostEstimate(
            flops=4 * length * length * width,
            bytes_accessed=8 * length * width,
            transcendentals=length * length * width // HEAD_DIM,
        ),
    )(qkv, segment)


def backward_kernel(parts, around_from, goes, carries, *refs):
    pieces, refs = refs[:parts], refs[parts:]
    upstream_ref, segment_ref, factor_ref = refs[:3]
    out_ref, stash = refs[-2:]
    if carries:
        out_ref = refs[-3]
        refs[-2][...] = refs[3][...]
    mine = lax.axis_index("tensor")
    rows = pieces[0].shape[2]
    if around_from is not None:
        columns = slice(around_from, around_from + pieces[0].shape[3])
        around = pieces[-1][:, 0, :, columns]
        pieces = pieces[:-1]
    found = [piece[:, 0] for piece in pieces]
    if around_from is not None:
        source = lax.axis_size("pipe") - 1 - lax.axis_index("pipe")
        found[0] = jnp.where(goes(source), around, found[0])
    for k, piece in enumerate(found):
        start = pl.multiple_of((mine ^ k) * rows, rows)
        stash[:, pl.ds(start, rows), :] = piece
    if segment_ref.shape[0] == 1:
        outside = outside_of(segment_ref)
        out_ref = refs[-3]
        refs[-2][...] = outside
    else:
        outside = segment_ref[...]
    factor = factor_ref[0]
    for start in range(0, upstream_ref.shape[2], HEAD_DIM):
        head = slice(start, start + HEAD_DIM)
        queries, keys, values = stash[0, :, head], stash[1, :, head], stash[2, :, head]
        upstream = upstream_ref[0, :, head]
        probs = probabilities(queries, keys, outside)
        grad_value = product(probs.astype(jnp.bfloat16), upstream, NN)
        grad_probs = product(values, upstream, NT)
        center = jnp.sum(probs * grad_probs, axis=0, keepdims=True)
        grad_logits = (probs * ((grad_probs - center) * SCALE)).astype(jnp.bfloat16)
        out_ref[0, 0, :, head] = (product(grad_logits, keys, TN) * factor).astype(jnp.bfloat16)
        out_ref[1, 0, :, head] = (product(grad_logits, queries, NN) * factor).astype(jnp.bfloat16)
        out_ref[2, 0, :, head] = (grad_value * factor).astype(jnp.bfloat16)


def backward(chunk, pieces, around, upstream, segment, factor, earlier, carried=None):
    _, length, width = upstream.shape
    first, heads = CHUNKS[chunk]
    step = heads * HEAD_DIM
    place = first // heads
    around_from = None
    goes = detoured if chunk == 0 else detoured_late
    if around is not None:
        around_from = 0
        pieces = [*pieces, around]
    parts = len(pieces)
    operands = [*pieces, upstream, segment, factor]
    in_specs = [pl.BlockSpec(memory_space=pltpu.VMEM)] * parts + [
        pl.BlockSpec((1, length, step), lambda i: (0, 0, place)),
        pl.BlockSpec(segment.shape, lambda i: (0, 0)),
        pl.BlockSpec(memory_space=pltpu.SMEM),
    ]
    out_specs = [pl.BlockSpec((3, 1, length, step), lambda i: (0, 0, 0, place))]
    out_shape = [jax.ShapeDtypeStruct((3, 1, length, width), jnp.bfloat16)]
    if segment.shape[0] == 1:
        out_specs.append(pl.BlockSpec((length, length), lambda i: (0, 0)))
        out_shape.append(jax.ShapeDtypeStruct((length, length), jnp.float32))
    if carried is not None:
        whole = pl.BlockSpec(carried.shape, lambda i: (0, 0, 0))
        operands.append(carried)
        in_specs.append(whole)
        out_specs.append(whole)
        out_shape.append(jax.ShapeDtypeStruct(carried.shape, carried.dtype))
    aliases = {}
    if earlier is not None:
        aliases = {len(operands): 0}
        operands.append(earlier)
        in_specs.append(pl.BlockSpec(memory_space=pl.ANY))
    return pl.pallas_call(
        functools.partial(backward_kernel, parts, around_from, goes, carried is not None),
        grid=(1,),
        in_specs=in_specs,
        out_specs=out_specs,
        out_shape=out_shape,
        scratch_shapes=[pltpu.VMEM((3, length, step), jnp.bfloat16)],
        input_output_aliases=aliases,
        compiler_params=pltpu.CompilerParams(vmem_limit_bytes=32 * 1024 * 1024),
        cost_estimate=pl.CostEstimate(
            flops=10 * length * length * step,
            bytes_accessed=14 * length * step,
            transcendentals=length * length * step // HEAD_DIM,
        ),
    )(*operands)


def fetched(piece, k, leg="direct", goes=None):
    sections, tensors = lax.axis_size("pipe"), lax.axis_size("tensor")
    goes = goes or detoured
    pairs = []
    for p in range(sections):
        for t in range(tensors):
            start, end = p, sections - 1 - p
            if leg == "aside":
                end = p ^ 1
            if leg == "onward":
                start = p ^ 1
            if leg == "all" or (leg == "direct") != goes(p):
                pairs.append((start * tensors + t, end * tensors + (t ^ k)))
    return lax.ppermute(piece, AXES, pairs)


def detoured(section):
    half = lax.axis_size("pipe") // 2
    place = section % half
    return (place == 2) | (place == half - 3)


def detoured_late(section):
    return section == lax.axis_size("pipe") - 3


def shifted(array, by):
    sections = lax.axis_size("pipe")
    with jax.named_scope("direct_out" if by > 0 else "direct_grad"):
        return lax.ppermute(array, "pipe", [(p, (p + by) % sections) for p in range(sections)])


def on_device(fwd_qkv, fwd_segments, parked, bwd_segments, grad_out, loss_tokens):
    length, width = grad_out.shape[1:]
    tensors = lax.axis_size("tensor")
    mine = lax.axis_index("tensor")

    def cut(whole, k, first, heads):
        start = (mine ^ k) * width + first * HEAD_DIM
        return lax.dynamic_slice_in_dim(whole, start, heads * HEAD_DIM, axis=3)

    def fetched_chunk(whole, chunk, partners):
        first, heads = CHUNKS[chunk]
        pieces = []
        for k in partners:
            leg = "direct" if k == 0 and chunk != 1 else "all"
            goes = detoured if chunk == 0 else detoured_late
            with jax.named_scope(f"stash_{k}_{chunk}"):
                pieces.append(fetched(cut(whole, k, first, heads), k, leg, goes))
        return pieces

    upstream = shifted(grad_out, -1)
    leading = cut(parked, 3, *CHUNKS[0])
    leading, parked = lax.optimization_barrier((leading, parked))
    with jax.named_scope("stash_3_0"):
        leading = fetched(leading, 3, "all")
    with jax.named_scope("aside_0"):
        around = fetched(cut(parked, 0, *DETOUR), 0, "aside")
    with jax.named_scope("onward_0"):
        around = fetched(around, 0, "onward")
    pieces = [[*fetched_chunk(parked, 0, range(3)), leading]]
    with jax.named_scope("forward_heads"):
        forward_out = forward(fwd_qkv, fwd_segments)
    received = shifted(forward_out, 1)
    tokens = loss_tokens.astype(jnp.float32)
    pieces[0][3], tokens = lax.optimization_barrier((pieces[0][3], tokens))
    token_total = lax.psum(tokens, "dp")
    factor = jnp.float32(lax.axis_size("dp") * length) / token_total
    parked, token_total = lax.optimization_barrier((parked, token_total))
    pieces.append(fetched_chunk(parked, 1, range(tensors)))
    grads, outside = backward(0, pieces[0], around, upstream, bwd_segments, factor, None)
    parked, grads = lax.optimization_barrier((parked, grads))
    others = fetched_chunk(parked, 2, range(3))
    parked, received = lax.optimization_barrier((parked, received))
    with jax.named_scope("aside_2"):
        late = fetched(cut(parked, 0, *CHUNKS[2]), 0, "aside", detoured_late)
    final = fetched_chunk(parked, 2, [3])
    pieces.append([*others, *final])
    late, grads = lax.optimization_barrier((late, grads))
    grads, received = backward(
        1, pieces[1], None, upstream, outside, factor, grads, received
    )
    late, grads = lax.optimization_barrier((late, grads))
    with jax.named_scope("onward_2"):
        late = fetched(late, 0, "onward", detoured_late)
    (grads,) = backward(2, pieces[2], late, upstream, outside, factor, grads)
    return (received, grads)


def solution(mesh):
    placed = (
        P(None, ("pipe", "dp"), None, "tensor"),
        P(("pipe", "dp"), None),
        P(None, ("pipe", "dp"), "tensor", None),
        P(("pipe", "dp"), None),
        P(("pipe", "dp"), None, "tensor"),
        P(("pipe", "dp")),
    )
    return jax.shard_map(
        on_device,
        mesh=mesh,
        in_specs=placed,
        out_specs=(P(("pipe", "dp"), None, "tensor"), P(None, ("pipe", "dp"), None, "tensor")),
        check_vma=False,
    )
```
